32 devices in a mesh: grid: 8 (over z, core), pencil: 4 (over y, x).
Axes of the slice: x: 2, y: 2, z: 4, core: 2. Of those that a mesh axis runs over, the one named last changes fastest.
Arguments:
- field: bfloat16 [8, 512, 256, 128], P('grid', 'pencil'), may hold values from -6 to 6
- levels: int32 [8, 3], P('grid'), may hold values from 7 to 9, as said below
- coefficients: int32 [8], P('grid'), may hold values from -2 to 2
- failed: int32 [8], P('grid'), may hold values 0 or 1
- owner_map: int32 [64], replicated, may hold values from -1 to 47, as said below
- velocity: float32 [3], replicated, may hold values from -1 to 1
- diffusivity: float32 [3], replicated, may hold values from 0.5 to 4
Outputs:
- combined: float32 [48, 2, 128, 4096], P('grid', None, 'pencil')
The draws below stay inside these ranges and needn't reach their ends.
Inputs may be any that keep to these rules, and one draw needn't show every extreme that they name: `levels`: each row is (9, 8, 7) or (8, 9, 7); each occurs in 4 rows. `owner_map`: blocks held by no grid map to -1; every other block maps to a distinct row, and every row is named once. Owner o holds rows o * 6 to o * 6 + 5: 2 blocks held by grids of both level vectors and 2 held only by grids of each one, so every grid holds exactly 4 of each owner's blocks.
All inputs are finite; a program needn't handle non-finite values. No bound on the sum of `failed` on one device may be relied on, other than what follows from the above.
Results may differ from the reference program's by a relative error of at most 0.0056.
Values may be sent and summed in bfloat16 or wider, within the bound.
No kernel may reach another device: no remote copies, remote signals or barrier semaphores. Data moves between devices by JAX's collectives and lax.ppermute only.
A program may use at most 320 MiB of HBM per device.

```python
import math
import jax
import jax.numpy as jnp
from jax import lax

LEV_MID = 8
LEV_Z = 7
SIDE_MID = 256
SIDE_HI = 512
SIDE_Z = 128
BLOCK = 64
GRIDS = 8
SLOTS = 6


def draw_levels(key, part):
    ordering = jax.random.permutation(key, GRIDS) % 2
    first_kind = jnp.array([LEV_MID + 1, LEV_MID, LEV_Z], jnp.int32)
    second_kind = jnp.array([LEV_MID, LEV_MID + 1, LEV_Z], jnp.int32)
    return jnp.where((ordering == 0)[:, None], first_kind[None, :], second_kind[None, :]).astype(jnp.int32)


def draw_owner_map(key, part):
    per_side = SIDE_HI // BLOCK
    quarter = per_side // 4
    per_class = per_side // 2 * (per_side // 2)
    share = per_class // GRIDS
    slot_count = 3 * share
    block_ids = jnp.arange(per_side * per_side, dtype=jnp.int32)
    across = block_ids // per_side
    down_ids = block_ids % per_side
    outer_x = (across < quarter) | (across >= per_side - quarter)
    outer_y = (down_ids < quarter) | (down_ids >= per_side - quarter)
    members = [outer_x & outer_y, outer_y & ~outer_x, outer_x & ~outer_y]
    result = jnp.full(block_ids.shape, -1, jnp.int32)
    for number, member in enumerate(members):
        rank_in = jnp.cumsum(member.astype(jnp.int32)) - 1
        ordering = jax.random.permutation(jax.random.fold_in(key, number + 1), per_class).astype(jnp.int32)
        picked = ordering[jnp.clip(rank_in, 0, per_class - 1)]
        owner_id = picked % GRIDS
        slot_id = number * share + picked // GRIDS
        result = jnp.where(member, owner_id * slot_count + slot_id, result)
    return result.astype(jnp.int32)


def with_ends(drawn, key, low, top_value):
    longest = drawn.shape.index(max(drawn.shape))
    spots = []
    for shift in (0, 1):
        where = [jax.random.randint(jax.random.fold_in(key, axis), (), 0, length) for axis, length in enumerate(drawn.shape)]
        where[longest] = (where[longest] + shift) % drawn.shape[longest]
        spots.append(tuple(where))
    return drawn.at[spots[0]].set(low).at[spots[1]].set(top_value)


def steps_of(key, shape, shards, smallest, high):
    factor_of = 1.0
    for dim, blocks in shards:
        steps = jax.random.uniform(jax.random.fold_in(jax.random.fold_in(key, 6), dim), (blocks,), jnp.float32, smallest / len(shards), high / len(shards))
        factor_of = factor_of * jnp.repeat(jnp.exp(steps), shape[dim] // blocks).reshape((-1,) + (1,) * (len(shape) - 1 - dim))
    return factor_of


def scatter_about(key, dims, spread, most, shards=(), held_as=jnp.bfloat16):
    values = jax.random.normal(key, dims, jnp.float32) * spread
    if len(shards) > 0:
        values = steps_of(key, dims, shards, -0.22, 0.18) * values
    return jnp.clip(values, min=-most, max=most).astype(held_as)


def setup_inputs(seed: int = 0) -> dict:
    streams_of = jax.random.split(jax.random.key(seed), 8)
    field = scatter_about(streams_of[0], (GRIDS, SIDE_HI, SIDE_MID, SIDE_Z), 1.0, 6.0, ((0, 8), (1, 4)))
    levels = draw_levels(jax.random.fold_in(streams_of[7], 71), 0)
    coefficients = with_ends(jax.random.randint(streams_of[2], (GRIDS,), -2, 3), jax.random.fold_in(streams_of[2], 1), -2, 2).astype(jnp.int32)
    failed = with_ends((jax.random.randint(streams_of[3], (GRIDS,), 0, 4) < 1).astype(jnp.int32), jax.random.fold_in(streams_of[3], 1), 0, 1)
    owner_map = draw_owner_map(jax.random.fold_in(streams_of[7], 71), 0)
    velocity = jnp.clip(jax.random.uniform(streams_of[5], (3,), jnp.float32, -1.0, 1.0), -1.0, 1.0)
    diffusivity = jnp.clip(jnp.exp(jax.random.uniform(streams_of[6], (3,), jnp.float32, math.log(0.5), math.log(4.0))), 0.5, 4.0)
    return dict(field=field, levels=levels, coefficients=coefficients, failed=failed, owner_map=owner_map, velocity=velocity, diffusivity=diffusivity)


def signed_modes(positions, length):
    return jnp.where(positions < length // 2, positions, positions - length).astype(jnp.float32)

def dft_tables(length):
    positions = jnp.arange(length, dtype=jnp.int32)
    product = positions[:, None] * positions[None, :] % length
    angles = product.astype(jnp.float32) * (2.0 * math.pi / length)
    return jnp.stack([jnp.cos(angles), -jnp.sin(angles)]).astype(jnp.bfloat16)

def complex_table(length):
    tables = dft_tables(length)
    return jnp.stack([jnp.stack([tables[0], -tables[1]]), jnp.stack([tables[1], tables[0]])])

def apply_factor(spectrum, z_modes, long_modes, mid_modes, swapped, velocity, diffusivity, long_len, mid_len, z_len):
    nu_long = jnp.where(swapped, diffusivity[1], diffusivity[0])
    nu_mid = jnp.where(swapped, diffusivity[0], diffusivity[1])
    speed_long = jnp.where(swapped, velocity[1], velocity[0])
    speed_mid = jnp.where(swapped, velocity[0], velocity[1])
    z_grid = z_modes[:, None, None]
    long_grid = long_modes[None, :, None]
    mid_grid = mid_modes[None, None, :]
    exponent = (diffusivity[2] * z_grid * z_grid + nu_long * long_grid * long_grid + nu_mid * mid_grid * mid_grid) * (-4.0 / (long_len * long_len))
    phases = (velocity[2] * z_grid + speed_long * long_grid + speed_mid * mid_grid) * (-2.0 * math.pi / mid_len)
    magnitude = jnp.exp(exponent) * (1.0 / math.sqrt(long_len * mid_len * z_len))
    factor_re = magnitude * jnp.cos(phases)
    factor_im = magnitude * jnp.sin(phases)
    real_part = spectrum[0] * factor_re - spectrum[1] * factor_im
    imag_part = spectrum[0] * factor_im + spectrum[1] * factor_re
    return jnp.stack([real_part, imag_part])

def block_rows(swapped, owner_map, per_long, per_mid):
    along_long = jnp.arange(per_long, dtype=jnp.int32)[:, None] * jnp.ones((1, per_mid), jnp.int32)
    mid_raw = jnp.arange(per_mid, dtype=jnp.int32)
    mid_global = jnp.where(mid_raw < per_mid // 2, mid_raw, mid_raw + per_long - per_mid)
    along_mid = jnp.ones((per_long, 1), jnp.int32) * mid_global[None, :]
    block_x = jnp.where(swapped, along_mid, along_long)
    block_y = jnp.where(swapped, along_long, along_mid)
    return owner_map[(block_x * per_long + block_y).reshape(-1)]

def to_blocks(shifted, swapped, block_len):
    z_len = shifted.shape[1]
    per_long = shifted.shape[2] // block_len
    per_mid = shifted.shape[3] // block_len
    grouped = shifted.reshape(2, z_len, per_long, block_len, per_mid, block_len).transpose(2, 4, 0, 1, 3, 5)
    turned = jnp.where(swapped, grouped.transpose(0, 1, 2, 3, 5, 4), grouped)
    return turned.reshape(per_long * per_mid, 2, z_len, block_len * block_len)

def transform_grid(samples, swapped, velocity, diffusivity):
    long_len, mid_len, z_len = samples.shape
    highest = lax.Precision.HIGHEST
    along_z = jnp.einsum('abc,pck->pabk', samples.astype(jnp.float32), dft_tables(z_len).astype(jnp.float32), precision=highest).astype(jnp.bfloat16)
    along_mid = jnp.einsum('qabc,pqbd->padc', along_z.astype(jnp.float32), complex_table(mid_len).astype(jnp.float32), precision=highest).astype(jnp.bfloat16)
    spectrum = jnp.einsum('qabc,pqae->pceb', along_mid.astype(jnp.float32), complex_table(long_len).astype(jnp.float32), precision=highest)
    z_modes = signed_modes(jnp.arange(z_len, dtype=jnp.int32), z_len)
    long_modes = signed_modes(jnp.arange(long_len, dtype=jnp.int32), long_len)
    mid_modes = signed_modes(jnp.arange(mid_len, dtype=jnp.int32), mid_len)
    return apply_factor(spectrum, z_modes, long_modes, mid_modes, swapped, velocity, diffusivity, long_len, mid_len, z_len)

def reference(field, levels, coefficients, failed, owner_map, velocity, diffusivity):
    per_long = SIDE_HI // BLOCK
    per_mid = SIDE_MID // BLOCK

    def add_grid(combined, inputs):
        samples, level_row, coefficient, failure = inputs
        swapped = level_row[0] < level_row[1]
        shifted = transform_grid(samples, swapped, velocity, diffusivity)
        blocks = to_blocks(shifted, swapped, BLOCK)
        row_ids = block_rows(swapped, owner_map, per_long, per_mid)
        weight = (coefficient * (1 - failure)).astype(jnp.float32)
        return (combined.at[row_ids].add(weight * blocks), None)
    initial = jnp.zeros((GRIDS * SLOTS, 2, SIDE_Z, BLOCK * BLOCK), jnp.float32)
    combined, _ = lax.scan(add_grid, initial, (field, levels, coefficients, failed))
    return combined
```

```python
import functools
import math

import jax
import jax.numpy as jnp
import numpy as np
from jax import lax
from jax.experimental import pallas as pl
from jax.experimental.pallas import tpu as pltpu
from jax.sharding import PartitionSpec as P

CHUNKS = 2
VMEM_LIMIT = 56 * 1024 * 1024


def signed_modes(positions, length):
    return jnp.where(positions < length // 2, positions, positions - length).astype(jnp.float32)


def dft_tables(length):
    positions = jnp.arange(length, dtype=jnp.int32)
    product = positions[:, None] * positions[None, :] % length
    angles = product.astype(jnp.float32) * (2.0 * math.pi / length)
    return jnp.stack([jnp.cos(angles), -jnp.sin(angles)]).astype(jnp.bfloat16)


def complex_table(length):
    tables = dft_tables(length)
    return jnp.stack([jnp.stack([tables[0], -tables[1]]), jnp.stack([tables[1], tables[0]])])


def apply_factor(
    spectrum,
    z_modes,
    long_modes,
    mid_modes,
    swapped,
    velocity,
    diffusivity,
    long_len,
    mid_len,
    z_len,
):
    nu_long = jnp.where(swapped, diffusivity[1], diffusivity[0])
    nu_mid = jnp.where(swapped, diffusivity[0], diffusivity[1])
    speed_long = jnp.where(swapped, velocity[1], velocity[0])
    speed_mid = jnp.where(swapped, velocity[0], velocity[1])
    z_grid = z_modes[:, None, None]
    long_grid = long_modes[None, :, None]
    mid_grid = mid_modes[None, None, :]
    exponent = (
        diffusivity[2] * z_grid * z_grid
        + nu_long * long_grid * long_grid
        + nu_mid * mid_grid * mid_grid
    ) * (-4.0 / (long_len * long_len))
    phases = (velocity[2] * z_grid + speed_long * long_grid + speed_mid * mid_grid) * (
        -2.0 * math.pi / mid_len
    )
    magnitude = jnp.exp(exponent) * (1.0 / math.sqrt(long_len * mid_len * z_len))
    factor_re = magnitude * jnp.cos(phases)
    factor_im = magnitude * jnp.sin(phases)
    real_part = spectrum[0] * factor_re - spectrum[1] * factor_im
    imag_part = spectrum[0] * factor_im + spectrum[1] * factor_re
    return jnp.stack([real_part, imag_part])


def block_rows(swapped, owner_map, per_long, per_mid):
    along_long = jnp.arange(per_long, dtype=jnp.int32)[:, None] * jnp.ones((1, per_mid), jnp.int32)
    mid_raw = jnp.arange(per_mid, dtype=jnp.int32)
    mid_global = jnp.where(mid_raw < per_mid // 2, mid_raw, mid_raw + per_long - per_mid)
    along_mid = jnp.ones((per_long, 1), jnp.int32) * mid_global[None, :]
    block_x = jnp.where(swapped, along_mid, along_long)
    block_y = jnp.where(swapped, along_long, along_mid)
    return owner_map[(block_x * per_long + block_y).reshape(-1)]


def turn_inner(grouped):
    return grouped.transpose(0, 1, 2, 3, 5, 4)


def keep_inner(grouped):
    return grouped


def wide_body(field, levels, coefficients, failed, owner_map, velocity, diffusivity):
    samples = field[0]
    local_long, mid_len, z_len = samples.shape
    pencils = lax.axis_size("pencil")
    grid_count = lax.axis_size("grid")
    long_len = local_long * pencils
    z_local = z_len // pencils
    block_len = mid_len // 4
    per_long = long_len // block_len
    per_mid = mid_len // block_len
    swapped = levels[0, 0] < levels[0, 1]
    along_z = jnp.einsum(
        "abc,pck->pabk", samples, dft_tables(z_len), preferred_element_type=jnp.float32
    ).astype(jnp.bfloat16)
    along_mid = jnp.einsum(
        "qabc,pqbd->padc", along_z, complex_table(mid_len), preferred_element_type=jnp.float32
    ).astype(jnp.bfloat16)
    table_long = complex_table(long_len)
    spectrum = jnp.einsum(
        "qabc,pqae->pceb",
        lax.all_to_all(along_mid, "pencil", split_axis=3, concat_axis=1, tiled=True),
        table_long,
        preferred_element_type=jnp.float32,
    )
    z_start = lax.axis_index("pencil") * z_local
    z_modes = signed_modes(z_start + jnp.arange(z_local, dtype=jnp.int32), z_len)
    long_modes = signed_modes(jnp.arange(long_len, dtype=jnp.int32), long_len)
    mid_modes = signed_modes(jnp.arange(mid_len, dtype=jnp.int32), mid_len)
    shifted = apply_factor(
        spectrum,
        z_modes,
        long_modes,
        mid_modes,
        swapped,
        velocity,
        diffusivity,
        long_len,
        mid_len,
        z_len,
    )
    grouped = shifted.reshape(2, z_local, per_long, block_len, per_mid, block_len).transpose(
        2, 4, 0, 1, 3, 5
    )
    turned = lax.cond(swapped, turn_inner, keep_inner, grouped)
    held_count = per_long * per_mid
    blocks = turned.reshape(held_count, 2, z_local, block_len * block_len)
    row_ids = block_rows(swapped, owner_map, per_long, per_mid)
    weight = (coefficients[0] * (1 - failed[0])).astype(jnp.float32)
    weighted = blocks * weight
    slot_count = (2 * held_count - per_mid * per_mid) // grid_count
    capacity = held_count // grid_count
    owners = row_ids // slot_count
    slot_ids = row_ids % slot_count
    positions_all = jnp.arange(held_count, dtype=jnp.int32)
    earlier = (owners[:, None] == owners[None, :]) & (
        positions_all[None, :] < positions_all[:, None]
    )
    rank_in = jnp.sum(earlier.astype(jnp.int32), axis=1)
    target = owners * capacity + rank_in
    outgoing = (
        jnp.zeros_like(weighted)
        .at[target]
        .set(weighted)
        .reshape(grid_count, capacity, 2, z_local, block_len * block_len)
    )
    labels = (
        jnp.zeros((held_count,), jnp.float32)
        .at[target]
        .set(slot_ids.astype(jnp.float32))
        .reshape(grid_count, capacity)
    )
    incoming, got_labels = (
        lax.all_to_all(outgoing, "grid", split_axis=0, concat_axis=0, tiled=True),
        lax.all_to_all(labels, "grid", split_axis=0, concat_axis=0, tiled=True),
    )
    selector = (
        got_labels.reshape(1, -1)
        == jnp.arange(slot_count, dtype=jnp.int32).astype(jnp.float32)[:, None]
    ).astype(jnp.float32)
    combined = jnp.dot(
        selector, incoming.reshape(grid_count * capacity, -1), precision=lax.Precision.HIGHEST
    ).reshape(slot_count, 2, z_local, block_len * block_len)
    return combined


def host_tables(length):
    positions = np.arange(length)
    angles = (positions[:, None] * positions[None, :] % length) * (2.0 * math.pi / length)
    return np.cos(angles), -np.sin(angles)


def z_table(chunk, chunks, grid_count, pencils, z_len):
    groups = pencils // 2
    per_device = z_len // (grid_count * pencils)
    slots = per_device // chunks
    cos, sin = host_tables(z_len)
    table = np.zeros((grid_count, 2, chunks, groups, slots, chunks, z_len))
    for device in range(grid_count):
        for group in range(groups):
            for slot in range(slots):
                index = chunk * slots + slot
                mode = group * (z_len // pencils) + device * per_device + index
                parts = [cos[:, mode], sin[:, mode]]
                if mode == 0:
                    parts[1] = cos[:, z_len // 2]
                for half in range(chunks):
                    table[device, 0, half, group, slot, half] = parts[0]
                    table[device, 1, half, group, slot, half] = parts[1]
    return jnp.asarray(table.reshape(-1, chunks * z_len), jnp.bfloat16)


def mid_table(mid_len, block_len):
    cos, sin = host_tables(mid_len)
    order = np.arange(mid_len).reshape(mid_len // block_len, block_len // 2, 2).transpose(2, 0, 1).reshape(-1)
    plain = np.concatenate([cos, sin], axis=1)
    turned = np.concatenate([cos[:, order], sin[:, order]], axis=1)
    return jnp.asarray(np.stack([plain, turned]), jnp.bfloat16)


def long_tables(long_len, block_len, pencils):
    cos, sin = host_tables(long_len)
    order = np.arange(long_len).reshape(long_len // block_len, block_len // 2, 2).transpose(2, 0, 1).reshape(-1)
    real = np.stack([cos, -sin]).reshape(2, long_len, pencils, -1).transpose(1, 2, 0, 3).reshape(long_len, -1)
    imag = np.stack([sin, cos]).reshape(2, long_len, pencils, -1).transpose(1, 2, 0, 3).reshape(long_len, -1)
    first = np.concatenate([real[order], imag[order]], axis=0)
    second = np.concatenate([real, imag], axis=0).T
    return jnp.asarray(first, jnp.bfloat16), jnp.asarray(second, jnp.bfloat16)


def z_kernel(table_ref, field_ref, out_ref):
    halves, rows, mid_len, z_len = field_ref.shape
    lines = [field_ref[half].reshape(rows * mid_len, z_len) for half in range(halves)]
    joined = jnp.concatenate(lines, axis=1)
    out_ref[...] = lax.dot_general(
        table_ref[...], joined, (((1,), (1,)), ((), ())), preferred_element_type=jnp.float32
    ).astype(jnp.bfloat16)


def transform_z(samples, table, chunks):
    local_long, mid_len, z_len = samples.shape
    columns = table.shape[0]
    rows = 8
    split = samples.reshape(chunks, local_long // chunks, mid_len, z_len)
    return pl.pallas_call(
        z_kernel,
        grid=(local_long // chunks // rows,),
        in_specs=[
            pl.BlockSpec(table.shape, lambda i: (0, 0)),
            pl.BlockSpec((chunks, rows, mid_len, z_len), lambda i: (0, i, 0, 0)),
        ],
        out_specs=pl.BlockSpec((columns, rows * mid_len), lambda i: (0, i)),
        out_shape=jax.ShapeDtypeStruct((columns, local_long // chunks * mid_len), jnp.bfloat16),
        compiler_params=pltpu.CompilerParams(vmem_limit_bytes=VMEM_LIMIT),
        cost_estimate=pl.CostEstimate(
            flops=2 * columns * samples.size, bytes_accessed=4 * samples.size, transcendentals=0
        ),
        name="transform_z",
    )(table, split)


def mid_kernel(first_chunk, rows, weights_ref, place_ref, table_ref, *refs):
    sources, out_ref = refs[:-1], refs[-1]
    columns = sources[0].shape[0]
    mid_len = table_ref.shape[1]
    half = columns // 2
    pencils, classes, slots, _, halves = out_ref.shape[:5]
    groups = pencils // 2
    lead = place_ref[0] == 0
    row_ids = lax.broadcasted_iota(jnp.int32, (rows, half, mid_len), 1)
    special = lead & (row_ids % (groups * slots) == 0)
    for kind in range(classes):
        total = None
        for number, source in enumerate(sources):
            term = source[...].astype(jnp.float32) * weights_ref[kind, number]
            total = term if total is None else total + term
        total = total.astype(jnp.bfloat16)
        lines = jnp.concatenate([total[:, a * mid_len : (a + 1) * mid_len] for a in range(rows)], axis=0)
        product = jnp.dot(lines, table_ref[kind], preferred_element_type=jnp.float32)
        product = product.reshape(rows, columns, 2 * mid_len)
        re_cos, re_sin = product[:, :half, :mid_len], product[:, :half, mid_len:]
        im_cos, im_sin = product[:, half:, :mid_len], product[:, half:, mid_len:]
        plus = [re_cos - im_sin, re_sin + im_cos]
        minus = [re_cos + im_sin, re_sin - im_cos]
        if first_chunk:
            plus = [jnp.where(special, re_cos, plus[0]), jnp.where(special, re_sin, plus[1])]
            minus = [jnp.where(special, im_cos, minus[0]), jnp.where(special, im_sin, minus[1])]
        for part in range(2):
            up = jnp.transpose(plus[part], (1, 0, 2))
            down = jnp.transpose(minus[part], (1, 0, 2))
            for piece in range(halves):
                for group in range(groups):
                    for slot in range(slots):
                        at = (piece * groups + group) * slots + slot
                        out_ref[group, kind, slot, part, piece] = up[at].astype(jnp.bfloat16)
                        value = down[at]
                        if first_chunk and slot == 0:
                            other = (piece * groups + (group + 1) % groups) * slots
                            value = jnp.where(lead, down[other], value)
                        out_ref[pencils - 1 - group, kind, slot, part, piece] = value.astype(jnp.bfloat16)


def transform_mid(sources, weights, place, table, first_chunk, chunks, pencils, slots):
    columns, length = sources[0].shape
    classes, mid_len, _ = table.shape
    lines = length // mid_len
    rows = 16
    shape = (pencils, classes, slots, 2, chunks, lines, mid_len)
    return pl.pallas_call(
        functools.partial(mid_kernel, first_chunk, rows),
        grid=(lines // rows,),
        in_specs=[
            pl.BlockSpec(memory_space=pltpu.SMEM),
            pl.BlockSpec(memory_space=pltpu.SMEM),
            pl.BlockSpec(table.shape, lambda i: (0, 0, 0)),
        ]
        + [pl.BlockSpec((columns, rows * mid_len), lambda i: (0, i))] * len(sources),
        out_specs=pl.BlockSpec(shape[:5] + (rows, mid_len), lambda i: (0, 0, 0, 0, 0, i, 0)),
        out_shape=jax.ShapeDtypeStruct(shape, jnp.bfloat16),
        compiler_params=pltpu.CompilerParams(vmem_limit_bytes=VMEM_LIMIT),
        cost_estimate=pl.CostEstimate(
            flops=8 * columns * length * mid_len,
            bytes_accessed=2 * len(sources) * columns * length + 2 * math.prod(shape),
            transcendentals=0,
        ),
        name="transform_mid",
    )(weights, place, table, *sources)


def long_kernel(rows_ref, place_ref, z_ref, first_ref, second_ref, plane_ref, *refs):
    sources, out_ref, gathered = refs[:-2], refs[-2], refs[-1]
    pencils = len(sources)
    classes, _, _, local_long, mid_len = sources[0].shape
    depth = 2 * pencils * local_long
    long_len = pencils * local_long
    pairs = out_ref.shape[3]
    per_long = long_len // (2 * pairs)
    per_mid = mid_len // (2 * pairs)
    edge = per_mid // 2
    slot = pl.program_id(0)
    for number, source in enumerate(sources):
        for kind in range(classes):
            gathered[kind, place_ref[1] ^ number] = source[kind, 0]
    first = jnp.dot(first_ref[...], gathered[0].reshape(depth, mid_len), preferred_element_type=jnp.float32)
    second = lax.dot_general(
        gathered[1].reshape(depth, mid_len),
        second_ref[...],
        (((0,), (0,)), ((), ())),
        preferred_element_type=jnp.float32,
    )
    z_re, z_im = z_ref[0, slot], z_ref[1, slot]
    low = lax.broadcasted_iota(jnp.int32, (pairs, 4 * pairs), 1) < 2 * pairs
    span = 4 * pairs
    for across in range(per_long):
        held = across < edge or across >= per_long - edge
        narrow = across if across < edge else across - (per_long - per_mid)
        for couple in range(per_long // 2):
            near = couple < edge // 2 or couple >= (per_long - edge) // 2
            thin = couple if couple < edge // 2 else couple - (per_long - per_mid) // 2
            if not held and not near:
                continue
            tiles = []
            for parity in range(2):
                parts = []
                for part in range(2):
                    value = None
                    if near:
                        top = ((part * 2 + parity) * per_long + across) * pairs
                        value = first[top : top + pairs, thin * span : (thin + 1) * span]
                    if held:
                        top = (parity * per_mid + narrow) * pairs
                        left = part * long_len + couple * span
                        term = second[top : top + pairs, left : left + span]
                        value = term if value is None else value + term
                    parts.append(value)
                top = across * pairs
                plane_re = plane_ref[0, parity, top : top + pairs, couple * span : (couple + 1) * span]
                plane_im = plane_ref[1, parity, top : top + pairs, couple * span : (couple + 1) * span]
                factor_re = plane_re * z_re - plane_im * z_im
                factor_im = plane_re * z_im + plane_im * z_re
                tiles.append(
                    [
                        parts[0] * factor_re - parts[1] * factor_im,
                        parts[0] * factor_im + parts[1] * factor_re,
                    ]
                )
            for part in range(2):
                even, odd = tiles[0][part], tiles[1][part]
                block = across * per_long + 2 * couple
                left = jnp.where(low, even, pltpu.roll(odd, 2 * pairs, 1))
                right = jnp.where(low, pltpu.roll(even, 2 * pairs, 1), odd)
                out_ref[rows_ref[block], 0, part] = left.astype(jnp.bfloat16)
                out_ref[rows_ref[block + 1], 0, part] = right.astype(jnp.bfloat16)


def transform_long(sources, row_ids, place, z_factor, first, second, plane, row_count, pairs):
    classes, slots, _, local_long, mid_len = sources[0].shape
    pencils = len(sources)
    depth = 2 * pencils * local_long
    shape = (row_count, slots, 2, pairs, 4 * pairs)
    return pl.pallas_call(
        long_kernel,
        grid=(slots,),
        in_specs=[
            pl.BlockSpec(memory_space=pltpu.SMEM),
            pl.BlockSpec(memory_space=pltpu.SMEM),
            pl.BlockSpec(memory_space=pltpu.SMEM),
            pl.BlockSpec(first.shape, lambda i: (0, 0)),
            pl.BlockSpec(second.shape, lambda i: (0, 0)),
            pl.BlockSpec(plane.shape, lambda i: (0, 0, 0, 0)),
        ]
        + [pl.BlockSpec((classes, 1, 2, local_long, mid_len), lambda i: (0, i, 0, 0, 0))] * pencils,
        out_specs=pl.BlockSpec((row_count, 1, 2, pairs, 4 * pairs), lambda i: (0, i, 0, 0, 0)),
        out_shape=jax.ShapeDtypeStruct(shape, jnp.bfloat16),
        scratch_shapes=[pltpu.VMEM((classes, pencils, 2, local_long, mid_len), jnp.bfloat16)],
        compiler_params=pltpu.CompilerParams(vmem_limit_bytes=VMEM_LIMIT),
        cost_estimate=pl.CostEstimate(
            flops=2 * classes * slots * depth * depth * mid_len,
            bytes_accessed=2 * pencils * sources[0].size + 2 * math.prod(shape) + 4 * depth * depth,
            transcendentals=0,
        ),
        name="transform_long",
    )(row_ids, place, z_factor, first, second, plane, *sources)


def rows_kernel(grid_count, place_ref, *refs):
    sources, out_ref, gathered = refs[:-2], refs[-2], refs[-1]
    chunks = len(sources) // grid_count
    slots, _, pairs, span = sources[0].shape[1:]
    z_local = out_ref.shape[2]
    for chunk in range(chunks):
        for number in range(grid_count):
            for slot in range(slots):
                spot = (place_ref[0] ^ number) * (chunks * slots) + chunk * slots + slot
                gathered[spot] = sources[chunk * grid_count + number][0, slot, 0]

    def write(order):
        for top in range(0, z_local, 8):
            taken = jnp.stack([gathered[order(top + k)].astype(jnp.float32) for k in range(8)])
            turned = jnp.transpose(taken, (1, 0, 2))
            for pair in range(pairs):
                out_ref[0, 0, top : top + 8, pair * span : (pair + 1) * span] = turned[pair]

    @pl.when(place_ref[1] == 0)
    def _():
        write(lambda z: z)

    @pl.when(place_ref[1] != 0)
    def _():
        write(lambda z: (z_local - z) % z_local)


def lay_rows(sources, place, grid_count, z_local):
    rows, slots, _, pairs, span = sources[0].shape
    return pl.pallas_call(
        functools.partial(rows_kernel, grid_count),
        grid=(rows, 2),
        in_specs=[pl.BlockSpec(memory_space=pltpu.SMEM)]
        + [pl.BlockSpec((1, slots, 1, pairs, span), lambda i, j: (i, 0, j, 0, 0))] * len(sources),
        out_specs=pl.BlockSpec((1, 1, z_local, pairs * span), lambda i, j: (i, j, 0, 0)),
        out_shape=jax.ShapeDtypeStruct((rows, 2, z_local, pairs * span), jnp.float32),
        scratch_shapes=[pltpu.VMEM((z_local, pairs, span), jnp.bfloat16)],
        compiler_params=pltpu.CompilerParams(vmem_limit_bytes=VMEM_LIMIT),
        cost_estimate=pl.CostEstimate(
            flops=0, bytes_accessed=6 * len(sources) * sources[0].size, transcendentals=0
        ),
        name="lay_rows",
    )(place, *sources)


def exchange(parts, axis):
    count = parts.shape[0]
    me = lax.axis_index(axis)
    got = []
    for step in range(count):
        sent = lax.dynamic_index_in_dim(parts, me ^ step, keepdims=False)
        if step:
            sent = lax.ppermute(sent, axis, [(d, d ^ step) for d in range(count)])
        got.append(sent)
    return got


def mode_factor(modes, diffusion, speed, long_len, mid_len):
    magnitude = jnp.exp(diffusion * modes * modes * (-4.0 / (long_len * long_len)))
    phase = speed * modes * (-2.0 * math.pi / mid_len)
    return magnitude * jnp.cos(phase), magnitude * jnp.sin(phase)


def body(field, levels, coefficients, failed, owner_map, velocity, diffusivity):
    samples = field[0]
    local_long, mid_len, z_len = samples.shape
    pencils = lax.axis_size("pencil")
    grid_count = lax.axis_size("grid")
    long_len = local_long * pencils
    z_local = z_len // pencils
    block_len = mid_len // 4
    per_long = long_len // block_len
    per_mid = mid_len // block_len
    row_count = 2 * per_long * per_mid - per_mid * per_mid
    per_device = z_len // (grid_count * pencils)
    slots = per_device // CHUNKS
    me = lax.axis_index("grid")
    pencil = lax.axis_index("pencil")

    weight = (coefficients[0] * (1 - failed[0])).astype(jnp.float32)
    swapped = levels[0, 0] < levels[0, 1]
    mine = jnp.stack([jnp.where(swapped, 0.0, weight), jnp.where(swapped, weight, 0.0)])
    weights = lax.all_gather(mine, "grid", axis=1)
    near = jnp.take(weights, me ^ jnp.arange(grid_count, dtype=jnp.int32), axis=1)

    positions = jnp.arange(long_len, dtype=jnp.int32)
    modes = signed_modes(positions, long_len)
    x_re, x_im = mode_factor(modes, diffusivity[0], velocity[0], long_len, mid_len)
    y_re, y_im = mode_factor(modes, diffusivity[1], velocity[1], long_len, mid_len)
    by_parity = [v.reshape(long_len // 2, 2).T[:, :, None] for v in (x_re, x_im)]
    plane = jnp.stack(
        [by_parity[0] * y_re - by_parity[1] * y_im, by_parity[0] * y_im + by_parity[1] * y_re]
    )
    place_in = me * per_device + jnp.arange(per_device, dtype=jnp.int32)
    back = pencil >= pencils // 2
    z_index = pencil * z_local + jnp.where(back, (z_local - place_in) % z_local, place_in)
    z_re, z_im = mode_factor(
        signed_modes(z_index, z_len), diffusivity[2], velocity[2], long_len, mid_len
    )
    z_factor = jnp.stack([z_re, z_im]) * (1.0 / math.sqrt(long_len * mid_len * z_len))

    place = jnp.stack([me, pencil]).astype(jnp.int32)
    side = jnp.stack([me, back.astype(jnp.int32)]).astype(jnp.int32)
    mid = mid_table(mid_len, block_len)
    first, second = long_tables(long_len, block_len, pencils)

    arrived = []
    for chunk in range(CHUNKS):
        along_z = transform_z(samples, z_table(chunk, CHUNKS, grid_count, pencils, z_len), CHUNKS)
        parts = along_z.reshape(grid_count, -1, along_z.shape[1])
        sources = exchange(parts, "grid")
        along_mid = transform_mid(sources, near, place, mid, chunk == 0, CHUNKS, pencils, slots)
        along_mid = along_mid.reshape(along_mid.shape[:4] + (local_long, mid_len))
        lines = exchange(along_mid, "pencil")
        rows = transform_long(
            lines,
            owner_map,
            place,
            z_factor[:, chunk * slots : (chunk + 1) * slots],
            first,
            second,
            plane,
            row_count,
            block_len // 2,
        )
        arrived += exchange(rows.reshape((grid_count, -1) + rows.shape[1:]), "grid")
    return lay_rows(arrived, side, grid_count, z_local)


def solution(mesh):
    placed = (P("grid", "pencil", None, None), P("grid", None), P("grid"), P("grid"), P(), P(), P())
    devices = mesh.shape["grid"] * mesh.shape["pencil"]

    def run(field, *rest):
        few = field.shape[3] % (devices * CHUNKS) == 0 and mesh.shape["pencil"] % 2 == 0
        return jax.shard_map(
            body if few else wide_body,
            mesh=mesh,
            in_specs=placed,
            out_specs=P("grid", None, "pencil", None),
            check_vma=False,
        )(field, *rest)

    return run
```

```python
import functools
import math

import jax
import jax.numpy as jnp
import numpy as np
from jax import lax
from jax.experimental import pallas as pl
from jax.experimental.pallas import tpu as pltpu
from jax.sharding import PartitionSpec as P

CHUNKS = 2
VMEM_LIMIT = 56 * 1024 * 1024


def signed_modes(positions, length):
    return jnp.where(positions < length // 2, positions, positions - length).astype(jnp.float32)


def dft_tables(length):
    positions = jnp.arange(length, dtype=jnp.int32)
    product = positions[:, None] * positions[None, :] % length
    angles = product.astype(jnp.float32) * (2.0 * math.pi / length)
    return jnp.stack([jnp.cos(angles), -jnp.sin(angles)]).astype(jnp.bfloat16)


def complex_table(length):
    tables = dft_tables(length)
    return jnp.stack([jnp.stack([tables[0], -tables[1]]), jnp.stack([tables[1], tables[0]])])


def apply_factor(
    spectrum,
    z_modes,
    long_modes,
    mid_modes,
    swapped,
    velocity,
    diffusivity,
    long_len,
    mid_len,
    z_len,
):
    nu_long = jnp.where(swapped, diffusivity[1], diffusivity[0])
    nu_mid = jnp.where(swapped, diffusivity[0], diffusivity[1])
    speed_long = jnp.where(swapped, velocity[1], velocity[0])
    speed_mid = jnp.where(swapped, velocity[0], velocity[1])
    z_grid = z_modes[:, None, None]
    long_grid = long_modes[None, :, None]
    mid_grid = mid_modes[None, None, :]
    exponent = (
        diffusivity[2] * z_grid * z_grid
        + nu_long * long_grid * long_grid
        + nu_mid * mid_grid * mid_grid
    ) * (-4.0 / (long_len * long_len))
    phases = (velocity[2] * z_grid + speed_long * long_grid + speed_mid * mid_grid) * (
        -2.0 * math.pi / mid_len
    )
    magnitude = jnp.exp(exponent) * (1.0 / math.sqrt(long_len * mid_len * z_len))
    factor_re = magnitude * jnp.cos(phases)
    factor_im = magnitude * jnp.sin(phases)
    real_part = spectrum[0] * factor_re - spectrum[1] * factor_im
    imag_part = spectrum[0] * factor_im + spectrum[1] * factor_re
    return jnp.stack([real_part, imag_part])


def block_rows(swapped, owner_map, per_long, per_mid):
    along_long = jnp.arange(per_long, dtype=jnp.int32)[:, None] * jnp.ones((1, per_mid), jnp.int32)
    mid_raw = jnp.arange(per_mid, dtype=jnp.int32)
    mid_global = jnp.where(mid_raw < per_mid // 2, mid_raw, mid_raw + per_long - per_mid)
    along_mid = jnp.ones((per_long, 1), jnp.int32) * mid_global[None, :]
    block_x = jnp.where(swapped, along_mid, along_long)
    block_y = jnp.where(swapped, along_long, along_mid)
    return owner_map[(block_x * per_long + block_y).reshape(-1)]


def turn_inner(grouped):
    return grouped.transpose(0, 1, 2, 3, 5, 4)


def keep_inner(grouped):
    return grouped


def wide_body(field, levels, coefficients, failed, owner_map, velocity, diffusivity):
    samples = field[0]
    local_long, mid_len, z_len = samples.shape
    pencils = lax.axis_size("pencil")
    grid_count = lax.axis_size("grid")
    long_len = local_long * pencils
    z_local = z_len // pencils
    block_len = mid_len // 4
    per_long = long_len // block_len
    per_mid = mid_len // block_len
    swapped = levels[0, 0] < levels[0, 1]
    along_z = jnp.einsum(
        "abc,pck->pabk", samples, dft_tables(z_len), preferred_element_type=jnp.float32
    ).astype(jnp.bfloat16)
    along_mid = jnp.einsum(
        "qabc,pqbd->padc", along_z, complex_table(mid_len), preferred_element_type=jnp.float32
    ).astype(jnp.bfloat16)
    table_long = complex_table(long_len)
    spectrum = jnp.einsum(
        "qabc,pqae->pceb",
        lax.all_to_all(along_mid, "pencil", split_axis=3, concat_axis=1, tiled=True),
        table_long,
        preferred_element_type=jnp.float32,
    )
    z_start = lax.axis_index("pencil") * z_local
    z_modes = signed_modes(z_start + jnp.arange(z_local, dtype=jnp.int32), z_len)
    long_modes = signed_modes(jnp.arange(long_len, dtype=jnp.int32), long_len)
    mid_modes = signed_modes(jnp.arange(mid_len, dtype=jnp.int32), mid_len)
    shifted = apply_factor(
        spectrum,
        z_modes,
        long_modes,
        mid_modes,
        swapped,
        velocity,
        diffusivity,
        long_len,
        mid_len,
        z_len,
    )
    grouped = shifted.reshape(2, z_local, per_long, block_len, per_mid, block_len).transpose(
        2, 4, 0, 1, 3, 5
    )
    turned = lax.cond(swapped, turn_inner, keep_inner, grouped)
    held_count = per_long * per_mid
    blocks = turned.reshape(held_count, 2, z_local, block_len * block_len)
    row_ids = block_rows(swapped, owner_map, per_long, per_mid)
    weight = (coefficients[0] * (1 - failed[0])).astype(jnp.float32)
    weighted = blocks * weight
    slot_count = (2 * held_count - per_mid * per_mid) // grid_count
    capacity = held_count // grid_count
    owners = row_ids // slot_count
    slot_ids = row_ids % slot_count
    positions_all = jnp.arange(held_count, dtype=jnp.int32)
    earlier = (owners[:, None] == owners[None, :]) & (
        positions_all[None, :] < positions_all[:, None]
    )
    rank_in = jnp.sum(earlier.astype(jnp.int32), axis=1)
    target = owners * capacity + rank_in
    outgoing = (
        jnp.zeros_like(weighted)
        .at[target]
        .set(weighted)
        .reshape(grid_count, capacity, 2, z_local, block_len * block_len)
    )
    labels = (
        jnp.zeros((held_count,), jnp.float32)
        .at[target]
        .set(slot_ids.astype(jnp.float32))
        .reshape(grid_count, capacity)
    )
    incoming, got_labels = (
        lax.all_to_all(outgoing, "grid", split_axis=0, concat_axis=0, tiled=True),
        lax.all_to_all(labels, "grid", split_axis=0, concat_axis=0, tiled=True),
    )
    selector = (
        got_labels.reshape(1, -1)
        == jnp.arange(slot_count, dtype=jnp.int32).astype(jnp.float32)[:, None]
    ).astype(jnp.float32)
    combined = jnp.dot(
        selector, incoming.reshape(grid_count * capacity, -1), precision=lax.Precision.HIGHEST
    ).reshape(slot_count, 2, z_local, block_len * block_len)
    return combined


def host_tables(length):
    positions = np.arange(length)
    angles = (positions[:, None] * positions[None, :] % length) * (2.0 * math.pi / length)
    return np.cos(angles), -np.sin(angles)


def z_table(chunk, chunks, grid_count, pencils, z_len):
    groups = pencils // 2
    per_device = z_len // (grid_count * pencils)
    slots = per_device // chunks
    cos, sin = host_tables(z_len)
    table = np.zeros((grid_count, 2, chunks, groups, slots, chunks, z_len))
    for device in range(grid_count):
        for group in range(groups):
            for slot in range(slots):
                index = chunk * slots + slot
                mode = group * (z_len // pencils) + device * per_device + index
                parts = [cos[:, mode], sin[:, mode]]
                if mode == 0:
                    parts[1] = cos[:, z_len // 2]
                for half in range(chunks):
                    table[device, 0, half, group, slot, half] = parts[0]
                    table[device, 1, half, group, slot, half] = parts[1]
    return jnp.asarray(table.reshape(-1, chunks * z_len), jnp.bfloat16)


def mid_table(mid_len, block_len):
    cos, sin = host_tables(mid_len)
    order = np.arange(mid_len).reshape(mid_len // block_len, block_len // 2, 2).transpose(2, 0, 1).reshape(-1)
    plain = np.concatenate([cos, sin], axis=1)
    turned = np.concatenate([cos[:, order], sin[:, order]], axis=1)
    return jnp.asarray(np.stack([plain, turned]), jnp.bfloat16)


def long_tables(long_len, block_len, pencils):
    cos, sin = host_tables(long_len)
    order = np.arange(long_len).reshape(long_len // block_len, block_len // 2, 2).transpose(2, 0, 1).reshape(-1)
    real = np.stack([cos, -sin]).reshape(2, long_len, pencils, -1).transpose(1, 2, 0, 3).reshape(long_len, -1)
    imag = np.stack([sin, cos]).reshape(2, long_len, pencils, -1).transpose(1, 2, 0, 3).reshape(long_len, -1)
    first = np.concatenate([real[order], imag[order]], axis=0)
    second = np.concatenate([real, imag], axis=0).T
    return jnp.asarray(first, jnp.bfloat16), jnp.asarray(second, jnp.bfloat16)


def z_kernel(weight_ref, table_ref, field_ref, *out_refs):
    halves, rows, mid_len, z_len = field_ref.shape
    tiles, _, columns, lanes = out_refs[0].shape
    last = pl.num_programs(0) - 1

    @pl.when(pl.program_id(0) < last)
    def _():
        lines = [field_ref[half].reshape(rows * mid_len, z_len) for half in range(halves)]
        joined = jnp.concatenate(lines, axis=1)
        found = lax.dot_general(
            table_ref[...], joined, (((1,), (1,)), ((), ())), preferred_element_type=jnp.float32
        ).astype(jnp.bfloat16)
        for unit, out_ref in enumerate(out_refs):
            for tile in range(tiles):
                for row in range(rows):
                    left = row * mid_len + tile * lanes
                    out_ref[tile, row] = found[unit * columns : (unit + 1) * columns, left : left + lanes]

    @pl.when(pl.program_id(0) == last)
    def _():
        for out_ref in out_refs:
            for tile in range(tiles):
                out_ref[tile, 0] = jnp.full((columns, lanes), weight_ref[tile], jnp.float32).astype(jnp.bfloat16)


def transform_z(samples, table, weight, chunks, units):
    local_long, mid_len, z_len = samples.shape
    columns = table.shape[0] // units
    rows = 8
    lines = local_long // chunks
    steps = lines // rows
    tiles = weight.shape[0]
    lanes = mid_len // tiles
    split = samples.reshape(chunks, lines, mid_len, z_len)
    return pl.pallas_call(
        z_kernel,
        grid=(steps + 1,),
        in_specs=[
            pl.BlockSpec(memory_space=pltpu.SMEM),
            pl.BlockSpec(table.shape, lambda i: (0, 0)),
            pl.BlockSpec((chunks, rows, mid_len, z_len), lambda i: (0, jnp.minimum(i, steps - 1), 0, 0)),
        ],
        out_specs=[pl.BlockSpec((tiles, rows, columns, lanes), lambda i: (0, i, 0, 0))] * units,
        out_shape=[jax.ShapeDtypeStruct((tiles, lines + 1, columns, lanes), jnp.bfloat16)] * units,
        compiler_params=pltpu.CompilerParams(vmem_limit_bytes=VMEM_LIMIT),
        cost_estimate=pl.CostEstimate(
            flops=2 * units * columns * samples.size, bytes_accessed=4 * samples.size, transcendentals=0
        ),
        name="transform_z",
    )(weight, table, split)


def unit_specs(shape, rows):
    tiles, lines, columns, lanes = shape
    return [
        pl.BlockSpec((tiles, rows, columns, lanes), lambda i: (0, i, 0, 0)),
        pl.BlockSpec((tiles, 1, columns, lanes), lambda i: (0, lines - 1, 0, 0)),
    ]


def weighted_sum(sources, weights, kind):
    total = None
    for source, weight in zip(sources, weights):
        term = source * weight[kind]
        total = term if total is None else total + term
    return total


def relay_kernel(place_ref, *refs):
    out_refs = refs[-2:]
    passing = [refs[-4], refs[-3]]
    sources, weights = refs[:-4:2], refs[1:-4:2]
    rows = out_refs[0].shape[1]
    last = pl.num_programs(0) - 1
    outer = place_ref[2] != 0

    @pl.when(outer)
    def _():
        for out_ref, source in zip(out_refs, passing):
            out_ref[...] = source[...]

    @pl.when(jnp.logical_not(outer))
    def _():
        values = [source[...].astype(jnp.float32) for source in sources]
        scales = [weight[...].astype(jnp.float32) for weight in weights]
        for kind, out_ref in enumerate(out_refs):
            out_ref[...] = weighted_sum(values, scales, kind).astype(jnp.bfloat16)

    @pl.when(jnp.logical_not(outer) & (pl.program_id(0) == last))
    def _():
        for kind, out_ref in enumerate(out_refs):
            for tile in range(out_ref.shape[0]):
                out_ref[tile, rows - 1] = jnp.full(out_ref.shape[2:], float(tile == kind), jnp.bfloat16)


def relay(sources, passing, place):
    shape = sources[0].shape
    rows = 13 if shape[1] % 13 == 0 else 1
    specs = unit_specs(shape, rows)
    return pl.pallas_call(
        relay_kernel,
        grid=(shape[1] // rows,),
        in_specs=[pl.BlockSpec(memory_space=pltpu.SMEM)] + specs * len(sources) + specs[:1] * 2,
        out_specs=specs[:1] * 2,
        out_shape=[jax.ShapeDtypeStruct(shape, jnp.bfloat16)] * 2,
        compiler_params=pltpu.CompilerParams(vmem_limit_bytes=VMEM_LIMIT),
        cost_estimate=pl.CostEstimate(
            flops=0, bytes_accessed=2 * (len(sources) + 4) * math.prod(shape), transcendentals=0
        ),
        name="relay",
    )(place, *[ref for source in sources for ref in (source, source)], *passing)


def mid_kernel(first_chunk, place_ref, table_ref, *refs):
    pencils = 4
    refs, out_refs, gathered = refs[: -pencils - 1], refs[-pencils - 1 : -1], refs[-1]
    tiles, rows, columns, lanes = refs[0].shape
    mid_len = tiles * lanes
    half = columns // 2
    classes, slots, _, halves = out_refs[0].shape[:4]
    groups = pencils // 2
    lead = place_ref[0] == 0
    outer = place_ref[2] != 0
    row_ids = lax.broadcasted_iota(jnp.int32, (rows, half, mid_len), 1)
    special = lead & (row_ids % (groups * slots) == 0)
    sources = [ref[...] for ref in refs[0::2]]
    weights = [ref[...] for ref in refs[1::2]]
    for kept in (sources, weights):
        for spare in (-1, -2):
            kept[spare - 2] = jnp.where(outer, kept[spare], kept[spare - 2])
        del kept[-2:]
    sources = [source.astype(jnp.float32) for source in sources]
    weights = [weight.astype(jnp.float32) for weight in weights]
    for kind in range(classes):
        total = weighted_sum(sources, weights, kind).astype(jnp.bfloat16)
        lines = jnp.concatenate([total[tile].reshape(rows * columns, lanes) for tile in range(tiles)], axis=1)
        product = jnp.dot(lines, table_ref[kind], preferred_element_type=jnp.float32)
        product = product.reshape(rows, columns, 2 * mid_len)
        re_cos, re_sin = product[:, :half, :mid_len], product[:, :half, mid_len:]
        im_cos, im_sin = product[:, half:, :mid_len], product[:, half:, mid_len:]
        plus = [re_cos - im_sin, re_sin + im_cos]
        minus = [re_cos + im_sin, re_sin - im_cos]
        if first_chunk:
            plus = [jnp.where(special, re_cos, plus[0]), jnp.where(special, re_sin, plus[1])]
            minus = [jnp.where(special, im_cos, minus[0]), jnp.where(special, im_sin, minus[1])]
        for part in range(2):
            up = jnp.transpose(plus[part], (1, 0, 2))
            down = jnp.transpose(minus[part], (1, 0, 2))
            for piece in range(halves):
                for group in range(groups):
                    for slot in range(slots):
                        at = (piece * groups + group) * slots + slot
                        gathered[group, kind, slot, part, piece] = up[at].astype(jnp.bfloat16)
                        value = down[at]
                        if first_chunk and slot == 0:
                            other = (piece * groups + (group + 1) % groups) * slots
                            value = jnp.where(lead, down[other], value)
                        gathered[pencils - 1 - group, kind, slot, part, piece] = value.astype(jnp.bfloat16)
    for step, out_ref in enumerate(out_refs):
        out_ref[...] = gathered[place_ref[1] ^ step]


def transform_mid(sources, place, table, first_chunk, chunks, pencils, slots):
    tiles, lines, columns, lanes = sources[0].shape
    lines -= 1
    classes, mid_len, _ = table.shape
    rows = 16
    shape = (classes, slots, 2, chunks, lines, mid_len)
    block = shape[:4] + (rows, mid_len)
    size = sources[0].size
    return pl.pallas_call(
        functools.partial(mid_kernel, first_chunk),
        grid=(lines // rows,),
        in_specs=[pl.BlockSpec(memory_space=pltpu.SMEM), pl.BlockSpec(table.shape, lambda i: (0, 0, 0))]
        + unit_specs(sources[0].shape, rows) * len(sources),
        out_specs=[pl.BlockSpec(block, lambda i: (0, 0, 0, 0, i, 0))] * pencils,
        out_shape=[jax.ShapeDtypeStruct(shape, jnp.bfloat16)] * pencils,
        scratch_shapes=[pltpu.VMEM((pencils,) + block, jnp.bfloat16)],
        compiler_params=pltpu.CompilerParams(vmem_limit_bytes=VMEM_LIMIT),
        cost_estimate=pl.CostEstimate(
            flops=8 * size * mid_len,
            bytes_accessed=2 * len(sources) * size + 2 * pencils * math.prod(shape),
            transcendentals=0,
        ),
        name="transform_mid",
    )(place, table, *[ref for source in sources for ref in (source, source)])


def long_kernel(pencils, rows_ref, place_ref, z_ref, first_ref, second_ref, plane_ref, *refs):
    sources, out_refs, gathered, laid = refs[:pencils], refs[pencils:-2], refs[-2], refs[-1]
    classes, _, _, local_long, mid_len = sources[0].shape
    depth = 2 * pencils * local_long
    long_len = pencils * local_long
    owned, _, _, pairs, _ = out_refs[0].shape
    per_long = long_len // (2 * pairs)
    per_mid = mid_len // (2 * pairs)
    edge = per_mid // 2
    slot = pl.program_id(0)
    for number, source in enumerate(sources):
        for kind in range(classes):
            gathered[kind, place_ref[1] ^ number] = source[kind, 0]
    first = jnp.dot(first_ref[...], gathered[0].reshape(depth, mid_len), preferred_element_type=jnp.float32)
    second = lax.dot_general(
        gathered[1].reshape(depth, mid_len),
        second_ref[...],
        (((0,), (0,)), ((), ())),
        preferred_element_type=jnp.float32,
    )
    z_re, z_im = z_ref[0, slot], z_ref[1, slot]
    low = lax.broadcasted_iota(jnp.int32, (pairs, 4 * pairs), 1) < 2 * pairs
    span = 4 * pairs
    for across in range(per_long):
        held = across < edge or across >= per_long - edge
        narrow = across if across < edge else across - (per_long - per_mid)
        for couple in range(per_long // 2):
            near = couple < edge // 2 or couple >= (per_long - edge) // 2
            thin = couple if couple < edge // 2 else couple - (per_long - per_mid) // 2
            if not held and not near:
                continue
            tiles = []
            for parity in range(2):
                parts = []
                for part in range(2):
                    value = None
                    if near:
                        top = ((part * 2 + parity) * per_long + across) * pairs
                        value = first[top : top + pairs, thin * span : (thin + 1) * span]
                    if held:
                        top = (parity * per_mid + narrow) * pairs
                        left = part * long_len + couple * span
                        term = second[top : top + pairs, left : left + span]
                        value = term if value is None else value + term
                    parts.append(value)
                top = across * pairs
                plane_re = plane_ref[0, parity, top : top + pairs, couple * span : (couple + 1) * span]
                plane_im = plane_ref[1, parity, top : top + pairs, couple * span : (couple + 1) * span]
                factor_re = plane_re * z_re - plane_im * z_im
                factor_im = plane_re * z_im + plane_im * z_re
                tiles.append(
                    [
                        parts[0] * factor_re - parts[1] * factor_im,
                        parts[0] * factor_im + parts[1] * factor_re,
                    ]
                )
            for part in range(2):
                even, odd = tiles[0][part], tiles[1][part]
                block = across * per_long + 2 * couple
                left = jnp.where(low, even, pltpu.roll(odd, 2 * pairs, 1))
                right = jnp.where(low, pltpu.roll(even, 2 * pairs, 1), odd)
                laid[rows_ref[block], part] = left.astype(jnp.bfloat16)
                laid[rows_ref[block + 1], part] = right.astype(jnp.bfloat16)
    for step, out_ref in enumerate(out_refs):
        top = (place_ref[0] ^ step) * owned
        for row in range(owned):
            out_ref[row, 0] = laid[top + row]


def transform_long(sources, row_ids, place, z_factor, first, second, plane, row_count, grid_count, pairs):
    classes, slots, _, local_long, mid_len = sources[0].shape
    pencils = len(sources)
    depth = 2 * pencils * local_long
    owned = row_count // grid_count
    shape = (owned, slots, 2, pairs, 4 * pairs)
    return pl.pallas_call(
        functools.partial(long_kernel, pencils),
        grid=(slots,),
        in_specs=[
            pl.BlockSpec(memory_space=pltpu.SMEM),
            pl.BlockSpec(memory_space=pltpu.SMEM),
            pl.BlockSpec(memory_space=pltpu.SMEM),
            pl.BlockSpec(first.shape, lambda i: (0, 0)),
            pl.BlockSpec(second.shape, lambda i: (0, 0)),
            pl.BlockSpec(plane.shape, lambda i: (0, 0, 0, 0)),
        ]
        + [pl.BlockSpec((classes, 1, 2, local_long, mid_len), lambda i: (0, i, 0, 0, 0))] * pencils,
        out_specs=[pl.BlockSpec((owned, 1, 2, pairs, 4 * pairs), lambda i: (0, i, 0, 0, 0))] * grid_count,
        out_shape=[jax.ShapeDtypeStruct(shape, jnp.bfloat16)] * grid_count,
        scratch_shapes=[
            pltpu.VMEM((classes, pencils, 2, local_long, mid_len), jnp.bfloat16),
            pltpu.VMEM((row_count, 2, pairs, 4 * pairs), jnp.bfloat16),
        ],
        compiler_params=pltpu.CompilerParams(vmem_limit_bytes=VMEM_LIMIT),
        cost_estimate=pl.CostEstimate(
            flops=2 * classes * slots * depth * depth * mid_len,
            bytes_accessed=2 * pencils * sources[0].size + 2 * grid_count * math.prod(shape) + 4 * depth * depth,
            transcendentals=0,
        ),
        name="transform_long",
    )(row_ids, place, z_factor, first, second, plane, *sources)


def rows_kernel(grid_count, place_ref, *refs):
    sources, out_ref, gathered = refs[:-2], refs[-2], refs[-1]
    chunks = len(sources) // grid_count
    slots, _, pairs, span = sources[0].shape[1:]
    z_local = out_ref.shape[2]
    for chunk in range(chunks):
        for number in range(grid_count):
            for slot in range(slots):
                spot = (place_ref[0] ^ number) * (chunks * slots) + chunk * slots + slot
                gathered[spot] = sources[chunk * grid_count + number][0, slot, 0]

    def write(order):
        for top in range(0, z_local, 8):
            taken = jnp.stack([gathered[order(top + k)].astype(jnp.float32) for k in range(8)])
            turned = jnp.transpose(taken, (1, 0, 2))
            for pair in range(pairs):
                out_ref[0, 0, top : top + 8, pair * span : (pair + 1) * span] = turned[pair]

    @pl.when(place_ref[1] == 0)
    def _():
        write(lambda z: z)

    @pl.when(place_ref[1] != 0)
    def _():
        write(lambda z: (z_local - z) % z_local)


def lay_rows(sources, place, grid_count, z_local):
    rows, slots, _, pairs, span = sources[0].shape
    return pl.pallas_call(
        functools.partial(rows_kernel, grid_count),
        grid=(rows, 2),
        in_specs=[pl.BlockSpec(memory_space=pltpu.SMEM)]
        + [pl.BlockSpec((1, slots, 1, pairs, span), lambda i, j: (i, 0, j, 0, 0))] * len(sources),
        out_specs=pl.BlockSpec((1, 1, z_local, pairs * span), lambda i, j: (i, j, 0, 0)),
        out_shape=jax.ShapeDtypeStruct((rows, 2, z_local, pairs * span), jnp.float32),
        scratch_shapes=[pltpu.VMEM((z_local, pairs, span), jnp.bfloat16)],
        compiler_params=pltpu.CompilerParams(vmem_limit_bytes=VMEM_LIMIT),
        cost_estimate=pl.CostEstimate(
            flops=0, bytes_accessed=6 * len(sources) * sources[0].size, transcendentals=0
        ),
        name="lay_rows",
    )(place, *sources)


def exchange(parts, axis):
    count = len(parts)
    got = {0: parts[0]}
    for step in reversed(range(1, count)):
        got[step] = lax.ppermute(parts[step], axis, [(d, d ^ step) for d in range(count)])
    return [got[step] for step in range(count)]


FAR = (3, 0, 3, 0)
NEXT = (1, 2, 1, 2)
THIRD = (2, 3, 0, 1)
PAIR_SAME = [(d, d ^ 2) for d in range(8)]
PAIR_CROSS = [(d, d ^ 3) for d in range(8)]
INNER_SAME = [(2, 4), (4, 2), (3, 5), (5, 3)]
INNER_CROSS = [(2, 5), (5, 2), (3, 4), (4, 3)]
INNER_CORES = [(d, d ^ 1) for d in range(2, 6)]
CORES = [(d, d ^ 1) for d in range(8)]
ENTER_SAME = [(0, 2), (1, 3), (6, 4), (7, 5)]
ENTER_CROSS = [(0, 3), (1, 2), (6, 5), (7, 4)]
JUMP_SAME = [(d, d ^ 4) for d in range(8)]
JUMP_MIXED = [(0, 5), (1, 4), (6, 3), (7, 2), (2, 6), (3, 7), (4, 0), (5, 1)]


def unit_order(me):
    chips = jnp.stack(
        [jnp.array(chip, jnp.int32)[me // 2] for chip in (FAR, NEXT, THIRD, (0, 1, 2, 3))]
    )
    core = me % 2
    return jnp.stack([2 * chips + core, 2 * chips + 1 - core], axis=1).reshape(-1)


def gather_grids(units, place):
    far_same, far_cross, next_same, next_cross, third_same, third_cross, own, other = units
    pair_same = lax.ppermute(far_same, "grid", PAIR_SAME)
    pair_cross = lax.ppermute(far_cross, "grid", PAIR_CROSS)
    inner_core = lax.ppermute(third_cross, "grid", INNER_CORES)
    inner_same = lax.ppermute(next_same, "grid", INNER_SAME)
    inner_cross = lax.ppermute(next_cross, "grid", INNER_CROSS)
    core = lax.ppermute(other, "grid", CORES)
    sums = relay([third_same, inner_core, pair_same, pair_cross], [third_same, third_cross], place)
    enter_same = lax.ppermute(next_same, "grid", ENTER_SAME)
    enter_cross = lax.ppermute(next_cross, "grid", ENTER_CROSS)
    jump_same = lax.ppermute(sums[0], "grid", JUMP_SAME)
    jump_mixed = lax.ppermute(sums[1], "grid", JUMP_MIXED)
    return [
        own,
        core,
        enter_same,
        enter_cross,
        jump_same,
        jump_mixed,
        inner_same,
        inner_cross,
        pair_same,
        pair_cross,
    ]


def mode_factor(modes, diffusion, speed, long_len, mid_len):
    magnitude = jnp.exp(diffusion * modes * modes * (-4.0 / (long_len * long_len)))
    phase = speed * modes * (-2.0 * math.pi / mid_len)
    return magnitude * jnp.cos(phase), magnitude * jnp.sin(phase)


def body(field, levels, coefficients, failed, owner_map, velocity, diffusivity):
    samples = field[0]
    local_long, mid_len, z_len = samples.shape
    pencils = lax.axis_size("pencil")
    grid_count = lax.axis_size("grid")
    long_len = local_long * pencils
    z_local = z_len // pencils
    block_len = mid_len // 4
    per_long = long_len // block_len
    per_mid = mid_len // block_len
    row_count = 2 * per_long * per_mid - per_mid * per_mid
    per_device = z_len // (grid_count * pencils)
    slots = per_device // CHUNKS
    me = lax.axis_index("grid")
    pencil = lax.axis_index("pencil")

    weight = (coefficients[0] * (1 - failed[0])).astype(jnp.float32)
    swapped = levels[0, 0] < levels[0, 1]
    mine = jnp.stack([jnp.where(swapped, 0.0, weight), jnp.where(swapped, weight, 0.0)])
    positions = jnp.arange(long_len, dtype=jnp.int32)
    modes = signed_modes(positions, long_len)
    x_re, x_im = mode_factor(modes, diffusivity[0], velocity[0], long_len, mid_len)
    y_re, y_im = mode_factor(modes, diffusivity[1], velocity[1], long_len, mid_len)
    by_parity = [v.reshape(long_len // 2, 2).T[:, :, None] for v in (x_re, x_im)]
    plane = jnp.stack(
        [by_parity[0] * y_re - by_parity[1] * y_im, by_parity[0] * y_im + by_parity[1] * y_re]
    )
    place_in = me * per_device + jnp.arange(per_device, dtype=jnp.int32)
    back = pencil >= pencils // 2
    z_index = pencil * z_local + jnp.where(back, (z_local - place_in) % z_local, place_in)
    z_re, z_im = mode_factor(
        signed_modes(z_index, z_len), diffusivity[2], velocity[2], long_len, mid_len
    )
    z_factor = jnp.stack([z_re, z_im]) * (1.0 / math.sqrt(long_len * mid_len * z_len))

    outer = (me < 2) | (me >= grid_count - 2)
    place = jnp.stack([me, pencil, outer.astype(jnp.int32)]).astype(jnp.int32)
    side = jnp.stack([me, back.astype(jnp.int32)]).astype(jnp.int32)
    mid = mid_table(mid_len, block_len)
    first, second = long_tables(long_len, block_len, pencils)
    order = unit_order(me)

    arrived = []
    for chunk in range(CHUNKS):
        table = z_table(chunk, CHUNKS, grid_count, pencils, z_len)
        table = table.reshape(grid_count, -1, table.shape[1])[order].reshape(table.shape)
        units = transform_z(samples, table, mine, CHUNKS, grid_count)
        sources = gather_grids(units, place)
        along_mid = transform_mid(sources, place, mid, chunk == 0, CHUNKS, pencils, slots)
        along_mid = [v.reshape(v.shape[:3] + (local_long, mid_len)) for v in along_mid]
        lines = exchange(along_mid, "pencil")
        rows = transform_long(
            lines,
            owner_map,
            place,
            z_factor[:, chunk * slots : (chunk + 1) * slots],
            first,
            second,
            plane,
            row_count,
            grid_count,
            block_len // 2,
        )
        arrived += exchange(rows, "grid")
    return lay_rows(arrived, side, grid_count, z_local)


def solution(mesh):
    placed = (P("grid", "pencil", None, None), P("grid", None), P("grid"), P("grid"), P(), P(), P())
    devices = mesh.shape["grid"] * mesh.shape["pencil"]

    def run(field, *rest):
        few = mesh.shape["grid"] == 8 and mesh.shape["pencil"] == 4 and field.shape[3] % (devices * CHUNKS) == 0
        return jax.shard_map(
            body if few else wide_body,
            mesh=mesh,
            in_specs=placed,
            out_specs=P("grid", None, "pencil", None),
            check_vma=False,
        )(field, *rest)

    return run
```

```python
import functools
import math

import jax
import jax.numpy as jnp
import numpy as np
from jax import lax
from jax.experimental import pallas as pl
from jax.experimental.pallas import tpu as pltpu
from jax.sharding import PartitionSpec as P

CHUNKS = 2
MID_COST = 40
VMEM_LIMIT = 56 * 1024 * 1024


def signed_modes(positions, length):
    return jnp.where(positions < length // 2, positions, positions - length).astype(jnp.float32)


def dft_tables(length):
    positions = jnp.arange(length, dtype=jnp.int32)
    product = positions[:, None] * positions[None, :] % length
    angles = product.astype(jnp.float32) * (2.0 * math.pi / length)
    return jnp.stack([jnp.cos(angles), -jnp.sin(angles)]).astype(jnp.bfloat16)


def complex_table(length):
    tables = dft_tables(length)
    return jnp.stack([jnp.stack([tables[0], -tables[1]]), jnp.stack([tables[1], tables[0]])])


def apply_factor(
    spectrum,
    z_modes,
    long_modes,
    mid_modes,
    swapped,
    velocity,
    diffusivity,
    long_len,
    mid_len,
    z_len,
):
    nu_long = jnp.where(swapped, diffusivity[1], diffusivity[0])
    nu_mid = jnp.where(swapped, diffusivity[0], diffusivity[1])
    speed_long = jnp.where(swapped, velocity[1], velocity[0])
    speed_mid = jnp.where(swapped, velocity[0], velocity[1])
    z_grid = z_modes[:, None, None]
    long_grid = long_modes[None, :, None]
    mid_grid = mid_modes[None, None, :]
    exponent = (
        diffusivity[2] * z_grid * z_grid
        + nu_long * long_grid * long_grid
        + nu_mid * mid_grid * mid_grid
    ) * (-4.0 / (long_len * long_len))
    phases = (velocity[2] * z_grid + speed_long * long_grid + speed_mid * mid_grid) * (
        -2.0 * math.pi / mid_len
    )
    magnitude = jnp.exp(exponent) * (1.0 / math.sqrt(long_len * mid_len * z_len))
    factor_re = magnitude * jnp.cos(phases)
    factor_im = magnitude * jnp.sin(phases)
    real_part = spectrum[0] * factor_re - spectrum[1] * factor_im
    imag_part = spectrum[0] * factor_im + spectrum[1] * factor_re
    return jnp.stack([real_part, imag_part])


def block_rows(swapped, owner_map, per_long, per_mid):
    along_long = jnp.arange(per_long, dtype=jnp.int32)[:, None] * jnp.ones((1, per_mid), jnp.int32)
    mid_raw = jnp.arange(per_mid, dtype=jnp.int32)
    mid_global = jnp.where(mid_raw < per_mid // 2, mid_raw, mid_raw + per_long - per_mid)
    along_mid = jnp.ones((per_long, 1), jnp.int32) * mid_global[None, :]
    block_x = jnp.where(swapped, along_mid, along_long)
    block_y = jnp.where(swapped, along_long, along_mid)
    return owner_map[(block_x * per_long + block_y).reshape(-1)]


def turn_inner(grouped):
    return grouped.transpose(0, 1, 2, 3, 5, 4)


def keep_inner(grouped):
    return grouped


def wide_body(field, levels, coefficients, failed, owner_map, velocity, diffusivity):
    samples = field[0]
    local_long, mid_len, z_len = samples.shape
    pencils = lax.axis_size("pencil")
    grid_count = lax.axis_size("grid")
    long_len = local_long * pencils
    z_local = z_len // pencils
    block_len = mid_len // 4
    per_long = long_len // block_len
    per_mid = mid_len // block_len
    swapped = levels[0, 0] < levels[0, 1]
    along_z = jnp.einsum(
        "abc,pck->pabk", samples, dft_tables(z_len), preferred_element_type=jnp.float32
    ).astype(jnp.bfloat16)
    along_mid = jnp.einsum(
        "qabc,pqbd->padc", along_z, complex_table(mid_len), preferred_element_type=jnp.float32
    ).astype(jnp.bfloat16)
    table_long = complex_table(long_len)
    spectrum = jnp.einsum(
        "qabc,pqae->pceb",
        lax.all_to_all(along_mid, "pencil", split_axis=3, concat_axis=1, tiled=True),
        table_long,
        preferred_element_type=jnp.float32,
    )
    z_start = lax.axis_index("pencil") * z_local
    z_modes = signed_modes(z_start + jnp.arange(z_local, dtype=jnp.int32), z_len)
    long_modes = signed_modes(jnp.arange(long_len, dtype=jnp.int32), long_len)
    mid_modes = signed_modes(jnp.arange(mid_len, dtype=jnp.int32), mid_len)
    shifted = apply_factor(
        spectrum,
        z_modes,
        long_modes,
        mid_modes,
        swapped,
        velocity,
        diffusivity,
        long_len,
        mid_len,
        z_len,
    )
    grouped = shifted.reshape(2, z_local, per_long, block_len, per_mid, block_len).transpose(
        2, 4, 0, 1, 3, 5
    )
    turned = lax.cond(swapped, turn_inner, keep_inner, grouped)
    held_count = per_long * per_mid
    blocks = turned.reshape(held_count, 2, z_local, block_len * block_len)
    row_ids = block_rows(swapped, owner_map, per_long, per_mid)
    weight = (coefficients[0] * (1 - failed[0])).astype(jnp.float32)
    weighted = blocks * weight
    slot_count = (2 * held_count - per_mid * per_mid) // grid_count
    capacity = held_count // grid_count
    owners = row_ids // slot_count
    slot_ids = row_ids % slot_count
    positions_all = jnp.arange(held_count, dtype=jnp.int32)
    earlier = (owners[:, None] == owners[None, :]) & (
        positions_all[None, :] < positions_all[:, None]
    )
    rank_in = jnp.sum(earlier.astype(jnp.int32), axis=1)
    target = owners * capacity + rank_in
    outgoing = (
        jnp.zeros_like(weighted)
        .at[target]
        .set(weighted)
        .reshape(grid_count, capacity, 2, z_local, block_len * block_len)
    )
    labels = (
        jnp.zeros((held_count,), jnp.float32)
        .at[target]
        .set(slot_ids.astype(jnp.float32))
        .reshape(grid_count, capacity)
    )
    incoming, got_labels = (
        lax.all_to_all(outgoing, "grid", split_axis=0, concat_axis=0, tiled=True),
        lax.all_to_all(labels, "grid", split_axis=0, concat_axis=0, tiled=True),
    )
    selector = (
        got_labels.reshape(1, -1)
        == jnp.arange(slot_count, dtype=jnp.int32).astype(jnp.float32)[:, None]
    ).astype(jnp.float32)
    combined = jnp.dot(
        selector, incoming.reshape(grid_count * capacity, -1), precision=lax.Precision.HIGHEST
    ).reshape(slot_count, 2, z_local, block_len * block_len)
    return combined


def host_tables(length):
    positions = np.arange(length)
    angles = (positions[:, None] * positions[None, :] % length) * (2.0 * math.pi / length)
    return np.cos(angles), -np.sin(angles)


def z_table(chunk, chunks, grid_count, pencils, z_len):
    groups = pencils // 2
    per_device = z_len // (grid_count * pencils)
    slots = per_device // chunks
    cos, sin = host_tables(z_len)
    table = np.zeros((grid_count, 2, chunks, groups, slots, chunks, z_len))
    for device in range(grid_count):
        for group in range(groups):
            for slot in range(slots):
                index = chunk * slots + slot
                mode = group * (z_len // pencils) + device * per_device + index
                parts = [cos[:, mode], sin[:, mode]]
                if mode == 0:
                    parts[1] = cos[:, z_len // 2]
                for half in range(chunks):
                    table[device, 0, half, group, slot, half] = parts[0]
                    table[device, 1, half, group, slot, half] = parts[1]
    return jnp.asarray(table.reshape(-1, chunks * z_len), jnp.bfloat16)


def mid_table(mid_len, block_len):
    cos, sin = host_tables(mid_len)
    order = np.arange(mid_len).reshape(mid_len // block_len, block_len // 2, 2).transpose(2, 0, 1).reshape(-1)
    plain = np.concatenate([cos, sin], axis=1)
    turned = np.concatenate([cos[:, order], sin[:, order]], axis=1)
    return jnp.asarray(np.stack([plain, turned]), jnp.bfloat16)


def long_tables(long_len, block_len, pencils):
    cos, sin = host_tables(long_len)
    order = np.arange(long_len).reshape(long_len // block_len, block_len // 2, 2).transpose(2, 0, 1).reshape(-1)
    real = np.stack([cos, -sin]).reshape(2, long_len, pencils, -1).transpose(1, 2, 0, 3).reshape(long_len, -1)
    imag = np.stack([sin, cos]).reshape(2, long_len, pencils, -1).transpose(1, 2, 0, 3).reshape(long_len, -1)
    first = np.concatenate([real[order], imag[order]], axis=0)
    second = np.concatenate([real, imag], axis=0).T
    return jnp.asarray(first, jnp.bfloat16), jnp.asarray(second, jnp.bfloat16)


def z_kernel(levels_ref, coefficient_ref, failed_ref, table_ref, field_ref, *out_refs):
    halves, rows, mid_len, z_len = field_ref.shape
    tiles, _, columns, lanes = out_refs[0].shape
    last = pl.num_programs(0) - 1
    me = lax.axis_index("grid")
    chip, core = me // 2, me % 2
    odd = chip % 2
    units = []
    for aim in (3 - 3 * odd, 1 + odd, (chip + 2) % 4, chip):
        units += [2 * aim + core, 2 * aim + 1 - core]

    @pl.when(pl.program_id(0) < last)
    def _():
        lines = [field_ref[half].reshape(rows * mid_len, z_len) for half in range(halves)]
        joined = jnp.concatenate(lines, axis=1)
        table = [table_ref[chunk, unit] for chunk in range(halves) for unit in units]
        found = lax.dot_general(
            jnp.concatenate(table, axis=0), joined, (((1,), (1,)), ((), ())), preferred_element_type=jnp.float32
        ).astype(jnp.bfloat16)
        for unit, out_ref in enumerate(out_refs):
            for tile in range(tiles):
                for row in range(rows):
                    left = row * mid_len + tile * lanes
                    out_ref[tile, row] = found[unit * columns : (unit + 1) * columns, left : left + lanes]

    @pl.when(pl.program_id(0) == last)
    def _():
        weight = (coefficient_ref[0] * (1 - failed_ref[0])).astype(jnp.float32)
        swapped = levels_ref[0, 0] < levels_ref[0, 1]
        for tile in range(tiles):
            value = jnp.where(swapped == (tile == 1), weight, 0.0)
            value = jnp.full((columns, lanes), value, jnp.float32).astype(jnp.bfloat16)
            for out_ref in out_refs:
                out_ref[tile, 0] = value


def transform_z(samples, levels, coefficients, failed, table):
    local_long, mid_len, z_len = samples.shape
    chunks, units, columns, _ = table.shape
    rows = 8
    lines = local_long // chunks
    steps = lines // rows
    tiles = 2
    lanes = mid_len // tiles
    units *= chunks
    split = samples.reshape(chunks, lines, mid_len, z_len)
    return pl.pallas_call(
        z_kernel,
        grid=(steps + 1,),
        in_specs=[
            pl.BlockSpec(memory_space=pltpu.SMEM),
            pl.BlockSpec(memory_space=pltpu.SMEM),
            pl.BlockSpec(memory_space=pltpu.SMEM),
            pl.BlockSpec(table.shape, lambda i: (0, 0, 0, 0)),
            pl.BlockSpec((chunks, rows, mid_len, z_len), lambda i: (0, jnp.minimum(i, steps - 1), 0, 0)),
        ],
        out_specs=[pl.BlockSpec((tiles, rows, columns, lanes), lambda i: (0, i, 0, 0))] * units,
        out_shape=[jax.ShapeDtypeStruct((tiles, lines + 1, columns, lanes), jnp.bfloat16)] * units,
        compiler_params=pltpu.CompilerParams(vmem_limit_bytes=VMEM_LIMIT),
        cost_estimate=pl.CostEstimate(
            flops=2 * units * columns * samples.size, bytes_accessed=4 * samples.size, transcendentals=0
        ),
        name="transform_z",
    )(levels, coefficients, failed, table, split)


def is_outer():
    me = lax.axis_index("grid")
    return (me < 2) | (me >= 6)


def unit_specs(shape, rows):
    tiles, lines, columns, lanes = shape
    return [
        pl.BlockSpec((tiles, rows, columns, lanes), lambda i: (0, i, 0, 0)),
        pl.BlockSpec((tiles, 1, columns, lanes), lambda i: (0, lines - 1, 0, 0)),
    ]


def weighted_sum(sources, weights, kind):
    total = None
    for source, weight in zip(sources, weights):
        term = source * weight[kind]
        total = term if total is None else total + term
    return total


def relay_kernel(*refs):
    out_refs = refs[-2:]
    passing = [refs[-4], refs[-3]]
    sources, weights = refs[:-4:2], refs[1:-4:2]
    rows = out_refs[0].shape[1]
    last = pl.num_programs(0) - 1
    outer = is_outer()

    @pl.when(outer)
    def _():
        for out_ref, source in zip(out_refs, passing):
            out_ref[...] = source[...]

    @pl.when(jnp.logical_not(outer))
    def _():
        values = [source[...].astype(jnp.float32) for source in sources]
        scales = [weight[...].astype(jnp.float32) for weight in weights]
        for kind, out_ref in enumerate(out_refs):
            out_ref[...] = weighted_sum(values, scales, kind).astype(jnp.bfloat16)

    @pl.when(jnp.logical_not(outer) & (pl.program_id(0) == last))
    def _():
        for kind, out_ref in enumerate(out_refs):
            for tile in range(out_ref.shape[0]):
                out_ref[tile, rows - 1] = jnp.full(out_ref.shape[2:], float(tile == kind), jnp.bfloat16)


def relay(sources, passing):
    shape = sources[0].shape
    rows = 13 if shape[1] % 13 == 0 else 1
    specs = unit_specs(shape, rows)
    return pl.pallas_call(
        relay_kernel,
        grid=(shape[1] // rows,),
        in_specs=specs * len(sources) + specs[:1] * 2,
        out_specs=specs[:1] * 2,
        out_shape=[jax.ShapeDtypeStruct(shape, jnp.bfloat16)] * 2,
        compiler_params=pltpu.CompilerParams(vmem_limit_bytes=VMEM_LIMIT),
        cost_estimate=pl.CostEstimate(
            flops=0, bytes_accessed=2 * (len(sources) + 4) * math.prod(shape), transcendentals=0
        ),
        name="relay",
    )(*[ref for source in sources for ref in (source, source)], *passing)


def mid_kernel(first_chunk, apart, table_ref, *refs):
    out_refs = []
    if apart:
        refs, out_refs = refs[: -apart - 1] + refs[-1:], refs[-apart - 1 : -1]
    refs, out_ref = refs[:-1], refs[-1]
    tiles, rows, columns, lanes = refs[0].shape
    mid_len = tiles * lanes
    half = columns // 2
    pencils, classes, slots, _, halves = out_ref.shape[:5]
    groups = pencils // 2
    lead = lax.axis_index("grid") == 0
    outer = is_outer()
    row_ids = lax.broadcasted_iota(jnp.int32, (rows, half, mid_len), 1)
    special = lead & (row_ids % (groups * slots) == 0)
    sources = [ref[...] for ref in refs[0::2]]
    weights = [ref[...] for ref in refs[1::2]]
    for kept in (sources, weights):
        for spare in (-1, -2):
            kept[spare - 2] = jnp.where(outer, kept[spare], kept[spare - 2])
        del kept[-2:]
    sources = [source.astype(jnp.float32) for source in sources]
    weights = [weight.astype(jnp.float32) for weight in weights]
    for kind in range(classes):
        total = weighted_sum(sources, weights, kind).astype(jnp.bfloat16)
        lines = jnp.concatenate([total[tile].reshape(rows * columns, lanes) for tile in range(tiles)], axis=1)
        product = jnp.dot(lines, table_ref[kind], preferred_element_type=jnp.float32)
        product = product.reshape(rows, columns, 2 * mid_len)
        re_cos, re_sin = product[:, :half, :mid_len], product[:, :half, mid_len:]
        im_cos, im_sin = product[:, half:, :mid_len], product[:, half:, mid_len:]
        plus = [re_cos - im_sin, re_sin + im_cos]
        minus = [re_cos + im_sin, re_sin - im_cos]
        if first_chunk:
            plus = [jnp.where(special, re_cos, plus[0]), jnp.where(special, re_sin, plus[1])]
            minus = [jnp.where(special, im_cos, minus[0]), jnp.where(special, im_sin, minus[1])]
        for part in range(2):
            up = jnp.transpose(plus[part], (1, 0, 2))
            down = jnp.transpose(minus[part], (1, 0, 2))
            for piece in range(halves):
                for group in range(groups):
                    for slot in range(slots):
                        at = (piece * groups + group) * slots + slot
                        out_ref[group, kind, slot, part, piece] = up[at].astype(jnp.bfloat16)
                        value = down[at]
                        if first_chunk and slot == 0:
                            other = (piece * groups + (group + 1) % groups) * slots
                            value = jnp.where(lead, down[other], value)
                        out_ref[pencils - 1 - group, kind, slot, part, piece] = value.astype(jnp.bfloat16)
    for step, apart_ref in enumerate(out_refs):
        apart_ref[...] = out_ref[lax.axis_index("pencil") ^ step]


def transform_mid(sources, table, first_chunk, apart, chunks, pencils, slots):
    tiles, lines, columns, lanes = sources[0].shape
    lines -= 1
    classes, mid_len, _ = table.shape
    rows = 16
    shape = (pencils, classes, slots, 2, chunks, lines, mid_len)
    block = shape[:5] + (rows, mid_len)
    if apart:
        layout = dict(
            out_specs=[pl.BlockSpec(block[1:], lambda i: (0, 0, 0, 0, i, 0))] * pencils,
            out_shape=[jax.ShapeDtypeStruct(shape[1:], jnp.bfloat16)] * pencils,
            scratch_shapes=[pltpu.VMEM(block, jnp.bfloat16)],
        )
    else:
        layout = dict(
            out_specs=pl.BlockSpec(block, lambda i: (0, 0, 0, 0, 0, i, 0)),
            out_shape=jax.ShapeDtypeStruct(shape, jnp.bfloat16),
        )
    size = sources[0].size
    return pl.pallas_call(
        functools.partial(mid_kernel, first_chunk, pencils if apart else 0),
        grid=(lines // rows,),
        in_specs=[pl.BlockSpec(table.shape, lambda i: (0, 0, 0))]
        + unit_specs(sources[0].shape, rows) * len(sources),
        compiler_params=pltpu.CompilerParams(vmem_limit_bytes=VMEM_LIMIT),
        cost_estimate=pl.CostEstimate(
            flops=MID_COST * 8 * size * mid_len,
            bytes_accessed=2 * len(sources) * size + 2 * math.prod(shape),
            transcendentals=0,
        ),
        name="transform_mid",
        **layout,
    )(table, *[ref for source in sources for ref in (source, source)])


def long_kernel(rows_ref, z_ref, first_ref, second_ref, plane_ref, *refs):
    if len(refs) == 2:
        source_ref, out_ref = refs
    else:
        sources, out_ref, source_ref = refs[:-2], refs[-2], refs[-1]
        for step, source in enumerate(sources):
            source_ref[lax.axis_index("pencil") ^ step] = source[...]
    pencils, classes, _, _, local_long, mid_len = source_ref.shape
    depth = 2 * pencils * local_long
    long_len = pencils * local_long
    pairs = out_ref.shape[3]
    per_long = long_len // (2 * pairs)
    per_mid = mid_len // (2 * pairs)
    edge = per_mid // 2
    slot = pl.program_id(0)
    lines = [source_ref[:, kind, 0].reshape(depth, mid_len) for kind in range(classes)]
    first = jnp.dot(first_ref[...], lines[0], preferred_element_type=jnp.float32)
    second = lax.dot_general(
        lines[1],
        second_ref[...],
        (((0,), (0,)), ((), ())),
        preferred_element_type=jnp.float32,
    )
    z_re, z_im = z_ref[0, slot], z_ref[1, slot]
    low = lax.broadcasted_iota(jnp.int32, (pairs, 4 * pairs), 1) < 2 * pairs
    span = 4 * pairs
    for across in range(per_long):
        held = across < edge or across >= per_long - edge
        narrow = across if across < edge else across - (per_long - per_mid)
        for couple in range(per_long // 2):
            near = couple < edge // 2 or couple >= (per_long - edge) // 2
            thin = couple if couple < edge // 2 else couple - (per_long - per_mid) // 2
            if not held and not near:
                continue
            tiles = []
            for parity in range(2):
                parts = []
                for part in range(2):
                    value = None
                    if near:
                        top = ((part * 2 + parity) * per_long + across) * pairs
                        value = first[top : top + pairs, thin * span : (thin + 1) * span]
                    if held:
                        top = (parity * per_mid + narrow) * pairs
                        left = part * long_len + couple * span
                        term = second[top : top + pairs, left : left + span]
                        value = term if value is None else value + term
                    parts.append(value)
                top = across * pairs
                plane_re = plane_ref[0, parity, top : top + pairs, couple * span : (couple + 1) * span]
                plane_im = plane_ref[1, parity, top : top + pairs, couple * span : (couple + 1) * span]
                factor_re = plane_re * z_re - plane_im * z_im
                factor_im = plane_re * z_im + plane_im * z_re
                tiles.append(
                    [
                        parts[0] * factor_re - parts[1] * factor_im,
                        parts[0] * factor_im + parts[1] * factor_re,
                    ]
                )
            for part in range(2):
                even, odd = tiles[0][part], tiles[1][part]
                block = across * per_long + 2 * couple
                left = jnp.where(low, even, pltpu.roll(odd, 2 * pairs, 1))
                right = jnp.where(low, pltpu.roll(even, 2 * pairs, 1), odd)
                out_ref[rows_ref[block], 0, part] = left.astype(jnp.bfloat16)
                out_ref[rows_ref[block + 1], 0, part] = right.astype(jnp.bfloat16)


def transform_long(sources, row_ids, z_factor, first, second, plane, row_count, pairs):
    if len(sources) == 1:
        pencils, classes, slots, _, local_long, mid_len = sources[0].shape
    else:
        pencils = len(sources)
        classes, slots, _, local_long, mid_len = sources[0].shape
    block = (pencils, classes, 1, 2, local_long, mid_len)
    if len(sources) == 1:
        specs = [pl.BlockSpec(block, lambda i: (0, 0, i, 0, 0, 0))]
        scratch = []
    else:
        specs = [pl.BlockSpec(block[1:], lambda i: (0, i, 0, 0, 0))] * pencils
        scratch = [pltpu.VMEM(block, jnp.bfloat16)]
    depth = 2 * pencils * local_long
    shape = (row_count, slots, 2, pairs, 4 * pairs)
    return pl.pallas_call(
        long_kernel,
        grid=(slots,),
        in_specs=[
            pl.BlockSpec(memory_space=pltpu.SMEM),
            pl.BlockSpec(memory_space=pltpu.SMEM),
            pl.BlockSpec(first.shape, lambda i: (0, 0)),
            pl.BlockSpec(second.shape, lambda i: (0, 0)),
            pl.BlockSpec(plane.shape, lambda i: (0, 0, 0, 0)),
        ]
        + specs,
        scratch_shapes=scratch,
        out_specs=pl.BlockSpec((row_count, 1, 2, pairs, 4 * pairs), lambda i: (0, i, 0, 0, 0)),
        out_shape=jax.ShapeDtypeStruct(shape, jnp.bfloat16),
        compiler_params=pltpu.CompilerParams(vmem_limit_bytes=VMEM_LIMIT),
        cost_estimate=pl.CostEstimate(
            flops=2 * classes * slots * depth * depth * mid_len,
            bytes_accessed=4 * slots * math.prod(block) + 2 * math.prod(shape) + 4 * depth * depth,
            transcendentals=0,
        ),
        name="transform_long",
    )(row_ids, z_factor, first, second, plane, *sources)


def rows_kernel(*refs):
    sources, out_ref = refs[:-1], refs[-1]
    back = lax.axis_index("pencil") >= 2
    _, _, slots, _, pairs, span = sources[0].shape
    z_local = out_ref.shape[2]

    def write(order):
        for top in range(0, z_local, 8):
            taken = []
            for z in range(top, top + 8):
                chunk, slot = divmod(order(z) % (len(sources) * slots), slots)
                device = order(z) // (len(sources) * slots)
                taken.append(sources[chunk][device, 0, slot, 0].astype(jnp.float32))
            turned = jnp.transpose(jnp.stack(taken), (1, 0, 2))
            for pair in range(pairs):
                out_ref[0, 0, top : top + 8, pair * span : (pair + 1) * span] = turned[pair]

    @pl.when(jnp.logical_not(back))
    def _():
        write(lambda z: z)

    @pl.when(back)
    def _():
        write(lambda z: (z_local - z) % z_local)


def lay_rows(sources, z_local):
    grid_count, rows, slots, _, pairs, span = sources[0].shape
    return pl.pallas_call(
        rows_kernel,
        grid=(rows, 2),
        in_specs=[pl.BlockSpec((grid_count, 1, slots, 1, pairs, span), lambda i, j: (0, i, 0, j, 0, 0))] * len(sources),
        out_specs=pl.BlockSpec((1, 1, z_local, pairs * span), lambda i, j: (i, j, 0, 0)),
        out_shape=jax.ShapeDtypeStruct((rows, 2, z_local, pairs * span), jnp.float32),
        compiler_params=pltpu.CompilerParams(vmem_limit_bytes=VMEM_LIMIT),
        cost_estimate=pl.CostEstimate(
            flops=0, bytes_accessed=6 * len(sources) * sources[0].size, transcendentals=0
        ),
        name="lay_rows",
    )(*sources)


PAIR_SAME = [(d, d ^ 2) for d in range(8)]
PAIR_CROSS = [(d, d ^ 3) for d in range(8)]
INNER_SAME = [(2, 4), (4, 2), (3, 5), (5, 3)]
INNER_CROSS = [(2, 5), (5, 2), (3, 4), (4, 3)]
INNER_CORES = [(d, d ^ 1) for d in range(2, 6)]
CORES = [(d, d ^ 1) for d in range(8)]
ENTER_SAME = [(0, 2), (1, 3), (6, 4), (7, 5)]
ENTER_CROSS = [(0, 3), (1, 2), (6, 5), (7, 4)]
JUMP_SAME = [(d, d ^ 4) for d in range(8)]
JUMP_MIXED = [(0, 5), (1, 4), (6, 3), (7, 2), (2, 6), (3, 7), (4, 0), (5, 1)]


def after(values, earlier):
    return lax.optimization_barrier((list(values), list(earlier)))[0]


def send(value, pairs):
    return lax.ppermute(value, "grid", pairs)


def exchange(parts, axis):
    count = len(parts)
    got = {0: parts[0]}
    for step in reversed(range(1, count)):
        got[step] = lax.ppermute(parts[step], axis, [(d, d ^ step) for d in range(count)])
    return [got[step] for step in range(count)]


def gather_grids(chunks):
    early = []
    for units in chunks:
        first = [units[0], units[1], units[5], units[2], units[3]]
        if early:
            first = [after([value], [twin])[0] for value, twin in zip(first, early[-1])]
        plans = (PAIR_SAME, PAIR_CROSS, INNER_CORES, INNER_SAME, INNER_CROSS)
        early.append([send(value, pairs) for value, pairs in zip(first, plans)])
    sums = []
    for units, got in zip(chunks, early):
        third = after(units[4:6], got[3:] if sums else [])
        sums.append(relay([third[0], got[2], got[0], got[1]], third))
    late = []
    for units, passed in zip(chunks, sums):
        second = [passed[0], passed[1], units[2], units[3]]
        twins = late[-1] if late else [None, None] + early[-1][:2]
        second = [value if twin is None else after([value], [twin])[0] for value, twin in zip(second, twins)]
        plans = (JUMP_SAME, JUMP_MIXED, ENTER_SAME, ENTER_CROSS)
        late.append([send(value, pairs) for value, pairs in zip(second, plans)])
    cores = [send(units[7], CORES) for units in chunks]
    found = [
        [units[6], core] + second + first[3:5] + first[0:2]
        for units, core, second, first in zip(chunks, cores, late, early)
    ]
    return found, sums, late


def mode_factor(modes, diffusion, speed, long_len, mid_len):
    magnitude = jnp.exp(diffusion * modes * modes * (-4.0 / (long_len * long_len)))
    phase = speed * modes * (-2.0 * math.pi / mid_len)
    return magnitude * jnp.cos(phase), magnitude * jnp.sin(phase)


def body(field, levels, coefficients, failed, owner_map, velocity, diffusivity):
    samples = field[0]
    local_long, mid_len, z_len = samples.shape
    pencils = lax.axis_size("pencil")
    grid_count = lax.axis_size("grid")
    long_len = local_long * pencils
    z_local = z_len // pencils
    block_len = mid_len // 4
    per_long = long_len // block_len
    per_mid = mid_len // block_len
    row_count = 2 * per_long * per_mid - per_mid * per_mid
    per_device = z_len // (grid_count * pencils)
    slots = per_device // CHUNKS
    me = lax.axis_index("grid")
    pencil = lax.axis_index("pencil")

    positions = jnp.arange(long_len, dtype=jnp.int32)
    modes = signed_modes(positions, long_len)
    x_re, x_im = mode_factor(modes, diffusivity[0], velocity[0], long_len, mid_len)
    y_re, y_im = mode_factor(modes, diffusivity[1], velocity[1], long_len, mid_len)
    by_parity = [v.reshape(long_len // 2, 2).T[:, :, None] for v in (x_re, x_im)]
    plane = jnp.stack(
        [by_parity[0] * y_re - by_parity[1] * y_im, by_parity[0] * y_im + by_parity[1] * y_re]
    )
    place_in = me * per_device + jnp.arange(per_device, dtype=jnp.int32)
    back = pencil >= pencils // 2
    z_index = pencil * z_local + jnp.where(back, (z_local - place_in) % z_local, place_in)
    z_re, z_im = mode_factor(
        signed_modes(z_index, z_len), diffusivity[2], velocity[2], long_len, mid_len
    )
    z_factor = jnp.stack([z_re, z_im]) * (1.0 / math.sqrt(long_len * mid_len * z_len))

    mid = mid_table(mid_len, block_len)
    first, second = long_tables(long_len, block_len, pencils)
    tables = [z_table(chunk, CHUNKS, grid_count, pencils, z_len) for chunk in range(CHUNKS)]
    tables = jnp.stack([v.reshape(grid_count, -1, v.shape[1]) for v in tables])
    units = transform_z(samples, levels, coefficients, failed, tables)
    units = [list(units[chunk * grid_count : (chunk + 1) * grid_count]) for chunk in range(CHUNKS)]

    units[0][4], plane, z_factor = lax.optimization_barrier((units[0][4], plane, z_factor))
    found, sums, late = gather_grids(units)
    arrived = []
    rows = None
    for chunk, sources in enumerate(found):
        if chunk + 1 < CHUNKS:
            sources = after(sources, sums[chunk + 1])
        if rows is not None:
            sources = after(sources, [rows])
        apart = chunk == CHUNKS - 1
        along_mid = transform_mid(sources, mid, chunk == 0, apart, CHUNKS, pencils, slots)
        if apart:
            along_mid = [v.reshape(v.shape[:3] + (local_long, mid_len)) for v in along_mid]
            lines = exchange(along_mid, "pencil")
        else:
            along_mid = along_mid.reshape(along_mid.shape[:4] + (local_long, mid_len))
            lines = [lax.all_to_all(along_mid, "pencil", split_axis=0, concat_axis=0, tiled=True)]
        rows = transform_long(
            lines,
            owner_map,
            z_factor[:, chunk * slots : (chunk + 1) * slots],
            first,
            second,
            plane,
            row_count,
            block_len // 2,
        )
        rows = rows.reshape((grid_count, -1) + rows.shape[1:])
        sent = after([rows], late[-1])[0]
        arrived.append(lax.all_to_all(sent, "grid", split_axis=0, concat_axis=0, tiled=True))
    return lay_rows(arrived, z_local)


def solution(mesh):
    placed = (P("grid", "pencil", None, None), P("grid", None), P("grid"), P("grid"), P(), P(), P())
    devices = mesh.shape["grid"] * mesh.shape["pencil"]

    def run(field, *rest):
        few = mesh.shape["grid"] == 8 and mesh.shape["pencil"] == 4 and field.shape[3] % (devices * CHUNKS) == 0
        return jax.shard_map(
            body if few else wide_body,
            mesh=mesh,
            in_specs=placed,
            out_specs=P("grid", None, "pencil", None),
            check_vma=False,
        )(field, *rest)

    return run
```

```python
import functools
import itertools
import math

import jax
import jax.numpy as jnp
import numpy as np
from jax import lax
from jax.experimental import pallas as pl
from jax.experimental.pallas import tpu as pltpu
from jax.sharding import PartitionSpec as P

CHUNKS = 2
MID_COST = 40
HOLD_COST = 100_000_000_000
ROWS_PER_STEP = 3
VMEM_LIMIT = 56 * 1024 * 1024


def signed_modes(positions, length):
    return jnp.where(positions < length // 2, positions, positions - length).astype(jnp.float32)


def dft_tables(length):
    positions = jnp.arange(length, dtype=jnp.int32)
    product = positions[:, None] * positions[None, :] % length
    angles = product.astype(jnp.float32) * (2.0 * math.pi / length)
    return jnp.stack([jnp.cos(angles), -jnp.sin(angles)]).astype(jnp.bfloat16)


def complex_table(length):
    tables = dft_tables(length)
    return jnp.stack([jnp.stack([tables[0], -tables[1]]), jnp.stack([tables[1], tables[0]])])


def apply_factor(
    spectrum,
    z_modes,
    long_modes,
    mid_modes,
    swapped,
    velocity,
    diffusivity,
    long_len,
    mid_len,
    z_len,
):
    nu_long = jnp.where(swapped, diffusivity[1], diffusivity[0])
    nu_mid = jnp.where(swapped, diffusivity[0], diffusivity[1])
    speed_long = jnp.where(swapped, velocity[1], velocity[0])
    speed_mid = jnp.where(swapped, velocity[0], velocity[1])
    z_grid = z_modes[:, None, None]
    long_grid = long_modes[None, :, None]
    mid_grid = mid_modes[None, None, :]
    exponent = (
        diffusivity[2] * z_grid * z_grid
        + nu_long * long_grid * long_grid
        + nu_mid * mid_grid * mid_grid
    ) * (-4.0 / (long_len * long_len))
    phases = (velocity[2] * z_grid + speed_long * long_grid + speed_mid * mid_grid) * (
        -2.0 * math.pi / mid_len
    )
    magnitude = jnp.exp(exponent) * (1.0 / math.sqrt(long_len * mid_len * z_len))
    factor_re = magnitude * jnp.cos(phases)
    factor_im = magnitude * jnp.sin(phases)
    real_part = spectrum[0] * factor_re - spectrum[1] * factor_im
    imag_part = spectrum[0] * factor_im + spectrum[1] * factor_re
    return jnp.stack([real_part, imag_part])


def block_rows(swapped, owner_map, per_long, per_mid):
    along_long = jnp.arange(per_long, dtype=jnp.int32)[:, None] * jnp.ones((1, per_mid), jnp.int32)
    mid_raw = jnp.arange(per_mid, dtype=jnp.int32)
    mid_global = jnp.where(mid_raw < per_mid // 2, mid_raw, mid_raw + per_long - per_mid)
    along_mid = jnp.ones((per_long, 1), jnp.int32) * mid_global[None, :]
    block_x = jnp.where(swapped, along_mid, along_long)
    block_y = jnp.where(swapped, along_long, along_mid)
    return owner_map[(block_x * per_long + block_y).reshape(-1)]


def turn_inner(grouped):
    return grouped.transpose(0, 1, 2, 3, 5, 4)


def keep_inner(grouped):
    return grouped


def wide_body(field, levels, coefficients, failed, owner_map, velocity, diffusivity):
    samples = field[0]
    local_long, mid_len, z_len = samples.shape
    pencils = lax.axis_size("pencil")
    grid_count = lax.axis_size("grid")
    long_len = local_long * pencils
    z_local = z_len // pencils
    block_len = mid_len // 4
    per_long = long_len // block_len
    per_mid = mid_len // block_len
    swapped = levels[0, 0] < levels[0, 1]
    along_z = jnp.einsum(
        "abc,pck->pabk", samples, dft_tables(z_len), preferred_element_type=jnp.float32
    ).astype(jnp.bfloat16)
    along_mid = jnp.einsum(
        "qabc,pqbd->padc", along_z, complex_table(mid_len), preferred_element_type=jnp.float32
    ).astype(jnp.bfloat16)
    table_long = complex_table(long_len)
    spectrum = jnp.einsum(
        "qabc,pqae->pceb",
        lax.all_to_all(along_mid, "pencil", split_axis=3, concat_axis=1, tiled=True),
        table_long,
        preferred_element_type=jnp.float32,
    )
    z_start = lax.axis_index("pencil") * z_local
    z_modes = signed_modes(z_start + jnp.arange(z_local, dtype=jnp.int32), z_len)
    long_modes = signed_modes(jnp.arange(long_len, dtype=jnp.int32), long_len)
    mid_modes = signed_modes(jnp.arange(mid_len, dtype=jnp.int32), mid_len)
    shifted = apply_factor(
        spectrum,
        z_modes,
        long_modes,
        mid_modes,
        swapped,
        velocity,
        diffusivity,
        long_len,
        mid_len,
        z_len,
    )
    grouped = shifted.reshape(2, z_local, per_long, block_len, per_mid, block_len).transpose(
        2, 4, 0, 1, 3, 5
    )
    turned = lax.cond(swapped, turn_inner, keep_inner, grouped)
    held_count = per_long * per_mid
    blocks = turned.reshape(held_count, 2, z_local, block_len * block_len)
    row_ids = block_rows(swapped, owner_map, per_long, per_mid)
    weight = (coefficients[0] * (1 - failed[0])).astype(jnp.float32)
    weighted = blocks * weight
    slot_count = (2 * held_count - per_mid * per_mid) // grid_count
    capacity = held_count // grid_count
    owners = row_ids // slot_count
    slot_ids = row_ids % slot_count
    positions_all = jnp.arange(held_count, dtype=jnp.int32)
    earlier = (owners[:, None] == owners[None, :]) & (
        positions_all[None, :] < positions_all[:, None]
    )
    rank_in = jnp.sum(earlier.astype(jnp.int32), axis=1)
    target = owners * capacity + rank_in
    outgoing = (
        jnp.zeros_like(weighted)
        .at[target]
        .set(weighted)
        .reshape(grid_count, capacity, 2, z_local, block_len * block_len)
    )
    labels = (
        jnp.zeros((held_count,), jnp.float32)
        .at[target]
        .set(slot_ids.astype(jnp.float32))
        .reshape(grid_count, capacity)
    )
    incoming, got_labels = (
        lax.all_to_all(outgoing, "grid", split_axis=0, concat_axis=0, tiled=True),
        lax.all_to_all(labels, "grid", split_axis=0, concat_axis=0, tiled=True),
    )
    selector = (
        got_labels.reshape(1, -1)
        == jnp.arange(slot_count, dtype=jnp.int32).astype(jnp.float32)[:, None]
    ).astype(jnp.float32)
    combined = jnp.dot(
        selector, incoming.reshape(grid_count * capacity, -1), precision=lax.Precision.HIGHEST
    ).reshape(slot_count, 2, z_local, block_len * block_len)
    return combined


def host_tables(length):
    positions = np.arange(length)
    angles = (positions[:, None] * positions[None, :] % length) * (2.0 * math.pi / length)
    return np.cos(angles), -np.sin(angles)


def z_table(chunk, chunks, grid_count, pencils, z_len):
    groups = pencils // 2
    per_device = z_len // (grid_count * pencils)
    slots = per_device // chunks
    cos, sin = host_tables(z_len)
    table = np.zeros((grid_count, 2, chunks, groups, slots, chunks, z_len))
    for device in range(grid_count):
        for group in range(groups):
            for slot in range(slots):
                index = chunk * slots + slot
                mode = group * (z_len // pencils) + device * per_device + index
                parts = [cos[:, mode], sin[:, mode]]
                if mode == 0:
                    parts[1] = cos[:, z_len // 2]
                for half in range(chunks):
                    table[device, 0, half, group, slot, half] = parts[0]
                    table[device, 1, half, group, slot, half] = parts[1]
    return jnp.asarray(table.reshape(-1, chunks * z_len), jnp.bfloat16)


def mid_table(mid_len, block_len):
    cos, sin = host_tables(mid_len)
    order = np.arange(mid_len).reshape(mid_len // block_len, block_len // 2, 2).transpose(2, 0, 1).reshape(-1)
    plain = np.concatenate([cos, sin], axis=1)
    turned = np.concatenate([cos[:, order], sin[:, order]], axis=1)
    return jnp.asarray(np.stack([plain, turned]), jnp.bfloat16)


def long_tables(long_len, block_len):
    tables = host_tables(long_len)
    order = np.arange(long_len).reshape(long_len // block_len, block_len // 2, 2).transpose(2, 0, 1).reshape(-1)
    first = np.concatenate([table[order] for table in tables], axis=0)
    second = np.concatenate(tables, axis=1)
    return jnp.asarray(first, jnp.bfloat16), jnp.asarray(second, jnp.bfloat16)


def z_kernel(levels_ref, coefficient_ref, failed_ref, table_ref, field_ref, *out_refs):
    halves, rows, mid_len, z_len = field_ref.shape
    tiles, _, columns, lanes = out_refs[0].shape
    last = pl.num_programs(0) - 1
    me = lax.axis_index("grid")
    chip, core = me // 2, me % 2
    odd = chip % 2
    units = []
    for aim in (3 - 3 * odd, 1 + odd, (chip + 2) % 4, chip):
        units += [2 * aim + core, 2 * aim + 1 - core]

    @pl.when(pl.program_id(0) < last)
    def _():
        lines = [field_ref[half].reshape(rows * mid_len, z_len) for half in range(halves)]
        joined = jnp.concatenate(lines, axis=1)
        table = [table_ref[chunk, unit] for chunk in range(halves) for unit in units]
        found = lax.dot_general(
            jnp.concatenate(table, axis=0), joined, (((1,), (1,)), ((), ())), preferred_element_type=jnp.float32
        ).astype(jnp.bfloat16)
        for unit, out_ref in enumerate(out_refs):
            for tile in range(tiles):
                for row in range(rows):
                    left = row * mid_len + tile * lanes
                    out_ref[tile, row] = found[unit * columns : (unit + 1) * columns, left : left + lanes]

    @pl.when(pl.program_id(0) == last)
    def _():
        weight = (coefficient_ref[0] * (1 - failed_ref[0])).astype(jnp.float32)
        swapped = levels_ref[0, 0] < levels_ref[0, 1]
        for tile in range(tiles):
            value = jnp.where(swapped == (tile == 1), weight, 0.0)
            value = jnp.full((columns, lanes), value, jnp.float32).astype(jnp.bfloat16)
            for out_ref in out_refs:
                out_ref[tile, 0] = value


def transform_z(samples, levels, coefficients, failed, table):
    local_long, mid_len, z_len = samples.shape
    chunks, units, columns, _ = table.shape
    rows = 32
    lines = local_long // chunks
    steps = lines // rows
    tiles = 2
    lanes = mid_len // tiles
    units *= chunks
    split = samples.reshape(chunks, lines, mid_len, z_len)
    return pl.pallas_call(
        z_kernel,
        grid=(steps + 1,),
        in_specs=[
            pl.BlockSpec(memory_space=pltpu.SMEM),
            pl.BlockSpec(memory_space=pltpu.SMEM),
            pl.BlockSpec(memory_space=pltpu.SMEM),
            pl.BlockSpec(table.shape, lambda i: (0, 0, 0, 0)),
            pl.BlockSpec((chunks, rows, mid_len, z_len), lambda i: (0, jnp.minimum(i, steps - 1), 0, 0)),
        ],
        out_specs=[pl.BlockSpec((tiles, rows, columns, lanes), lambda i: (0, i, 0, 0))] * units,
        out_shape=[jax.ShapeDtypeStruct((tiles, lines + 1, columns, lanes), jnp.bfloat16)] * units,
        compiler_params=pltpu.CompilerParams(vmem_limit_bytes=VMEM_LIMIT),
        cost_estimate=pl.CostEstimate(
            flops=2 * units * columns * samples.size, bytes_accessed=4 * samples.size, transcendentals=0
        ),
        name="transform_z",
    )(levels, coefficients, failed, table, split)


def is_outer():
    me = lax.axis_index("grid")
    return (me < 2) | (me >= 6)


def unit_specs(shape, rows):
    tiles, lines, columns, lanes = shape
    return [
        pl.BlockSpec((tiles, rows, columns, lanes), lambda i: (0, i, 0, 0)),
        pl.BlockSpec((tiles, 1, columns, lanes), lambda i: (0, lines - 1, 0, 0)),
    ]


def weighted_sum(sources, weights, kind):
    total = None
    for source, weight in zip(sources, weights):
        term = source * weight[kind]
        total = term if total is None else total + term
    return total


def relay_kernel(*refs):
    out_refs = refs[-2:]
    passing = [refs[-4], refs[-3]]
    sources, weights = refs[:-4:2], refs[1:-4:2]
    rows = out_refs[0].shape[1]
    last = pl.num_programs(0) - 1
    outer = is_outer()

    @pl.when(outer)
    def _():
        for out_ref, source in zip(out_refs, passing):
            out_ref[...] = source[...]

    @pl.when(jnp.logical_not(outer))
    def _():
        values = [source[...].astype(jnp.float32) for source in sources]
        scales = [weight[...].astype(jnp.float32) for weight in weights]
        for kind, out_ref in enumerate(out_refs):
            out_ref[...] = weighted_sum(values, scales, kind).astype(jnp.bfloat16)

    @pl.when(jnp.logical_not(outer) & (pl.program_id(0) == last))
    def _():
        for kind, out_ref in enumerate(out_refs):
            for tile in range(out_ref.shape[0]):
                out_ref[tile, rows - 1] = jnp.full(out_ref.shape[2:], float(tile == kind), jnp.bfloat16)


def relay(sources, passing):
    shape = sources[0].shape
    rows = 13 if shape[1] % 13 == 0 else 1
    specs = unit_specs(shape, rows)
    return pl.pallas_call(
        relay_kernel,
        grid=(shape[1] // rows,),
        in_specs=specs * len(sources) + specs[:1] * 2,
        out_specs=specs[:1] * 2,
        out_shape=[jax.ShapeDtypeStruct(shape, jnp.bfloat16)] * 2,
        compiler_params=pltpu.CompilerParams(vmem_limit_bytes=VMEM_LIMIT),
        cost_estimate=pl.CostEstimate(
            flops=0, bytes_accessed=2 * (len(sources) + 4) * math.prod(shape), transcendentals=0
        ),
        name="relay",
    )(*[ref for source in sources for ref in (source, source)], *passing)


def turning(outer, inner):
    rows = np.arange(outer * inner)
    return jnp.asarray(rows[:, None] % outer * inner + rows[:, None] // outer == rows[None, :], jnp.bfloat16)


def mid_kernel(first_chunk, apart, turn_ref, table_ref, *refs):
    out_refs = []
    if apart:
        refs, out_refs = refs[: -apart - 1] + refs[-1:], refs[-apart - 1 : -1]
    refs, out_ref = refs[:-1], refs[-1]
    tiles, rows, columns, lanes = refs[0].shape
    mid_len = tiles * lanes
    half = columns // 2
    pencils, classes, slots, _, halves = out_ref.shape[:5]
    groups = pencils // 2
    lead = lax.axis_index("grid") == 0
    outer = is_outer()
    sources = [ref[...] for ref in refs[0::2]]
    weights = [ref[...] for ref in refs[1::2]]
    for kept in (sources, weights):
        for spare in (-1, -2):
            kept[spare - 2] = jnp.where(outer, kept[spare], kept[spare - 2])
        del kept[-2:]
    sources = [source.astype(jnp.float32) for source in sources]
    weights = [weight.astype(jnp.float32) for weight in weights]
    for kind in range(classes):
        total = weighted_sum(sources, weights, kind).astype(jnp.bfloat16)
        lines = jnp.concatenate([total[tile].reshape(rows * columns, lanes) for tile in range(tiles)], axis=1)
        lines = jnp.dot(turn_ref[...], lines, preferred_element_type=jnp.float32).astype(jnp.bfloat16)
        product = jnp.dot(lines, table_ref[kind], preferred_element_type=jnp.float32)
        product = product.reshape(columns, rows, 2 * mid_len)
        re_cos, re_sin = product[:half, :, :mid_len], product[:half, :, mid_len:]
        im_cos, im_sin = product[half:, :, :mid_len], product[half:, :, mid_len:]
        for part in range(2):
            alone, other = (re_cos, im_cos) if part == 0 else (re_sin, im_sin)
            up = re_cos - im_sin if part == 0 else re_sin + im_cos
            down = re_cos + im_sin if part == 0 else re_sin - im_cos
            for piece in range(halves):
                for group in range(groups):
                    for slot in range(slots):
                        at = (piece * groups + group) * slots + slot
                        value, mirrored = up[at], down[at]
                        if first_chunk and slot == 0:
                            follower = (piece * groups + (group + 1) % groups) * slots
                            if group == 0:
                                value = jnp.where(lead, alone[at], value)
                            turn = down[follower] if group + 1 < groups else other[follower]
                            mirrored = jnp.where(lead, turn, mirrored)
                        out_ref[group, kind, slot, part, piece] = value.astype(jnp.bfloat16)
                        out_ref[pencils - 1 - group, kind, slot, part, piece] = mirrored.astype(jnp.bfloat16)
    for step, apart_ref in enumerate(out_refs):
        apart_ref[...] = out_ref[lax.axis_index("pencil") ^ step]


def transform_mid(sources, table, first_chunk, apart, chunks, pencils, slots):
    tiles, lines, columns, lanes = sources[0].shape
    lines -= 1
    classes, mid_len, _ = table.shape
    rows = 32
    shape = (pencils, classes, slots, 2, chunks, lines, mid_len)
    block = shape[:5] + (rows, mid_len)
    if apart:
        layout = dict(
            out_specs=[pl.BlockSpec(block[1:], lambda i: (0, 0, 0, 0, i, 0))] * pencils,
            out_shape=[jax.ShapeDtypeStruct(shape[1:], jnp.bfloat16)] * pencils,
            scratch_shapes=[pltpu.VMEM(block, jnp.bfloat16)],
        )
    else:
        layout = dict(
            out_specs=pl.BlockSpec(block, lambda i: (0, 0, 0, 0, 0, i, 0)),
            out_shape=jax.ShapeDtypeStruct(shape, jnp.bfloat16),
        )
    size = sources[0].size
    return pl.pallas_call(
        functools.partial(mid_kernel, first_chunk, pencils if apart else 0),
        grid=(lines // rows,),
        in_specs=[
            pl.BlockSpec((rows * columns, rows * columns), lambda i: (0, 0)),
            pl.BlockSpec(table.shape, lambda i: (0, 0, 0)),
        ]
        + unit_specs(sources[0].shape, rows) * len(sources),
        compiler_params=pltpu.CompilerParams(vmem_limit_bytes=VMEM_LIMIT),
        cost_estimate=pl.CostEstimate(
            flops=MID_COST * 8 * size * mid_len,
            bytes_accessed=2 * len(sources) * size + 2 * math.prod(shape),
            transcendentals=0,
        ),
        name="transform_mid",
        **layout,
    )(turning(rows, columns), table, *[ref for source in sources for ref in (source, source)])


def long_kernel(rows_ref, z_ref, x_ref, y_ref, first_ref, second_ref, *refs):
    if len(refs) == 2:
        source_ref, out_ref = refs
    else:
        sources, out_ref, source_ref = refs[:-2], refs[-2], refs[-1]
        for step, source in enumerate(sources):
            source_ref[lax.axis_index("pencil") ^ step] = source[...]
    pencils, classes, _, _, local_long, mid_len = source_ref.shape
    long_len = pencils * local_long
    pairs = out_ref.shape[3]
    per_long = long_len // (2 * pairs)
    per_mid = mid_len // (2 * pairs)
    edge = per_mid // 2
    slot = pl.program_id(0)
    lines = [
        jnp.concatenate(
            [source_ref[:, kind, 0, part].reshape(long_len, mid_len) for part in range(2)], axis=1
        )
        for kind in range(classes)
    ]
    first = jnp.dot(first_ref[...], lines[0], preferred_element_type=jnp.float32)
    second = lax.dot_general(
        lines[1], second_ref[...], (((0,), (0,)), ((), ())), preferred_element_type=jnp.float32
    )
    z_re, z_im = z_ref[0, slot], z_ref[1, slot]
    low = lax.broadcasted_iota(jnp.int32, (pairs, 4 * pairs), 1) < 2 * pairs
    span = 4 * pairs
    for across in range(per_long):
        held = across < edge or across >= per_long - edge
        narrow = across if across < edge else across - (per_long - per_mid)
        columns = []
        for parity in range(2):
            x_re, x_im = (x_ref[part, parity, across * pairs : (across + 1) * pairs] for part in range(2))
            column = (x_re * z_re - x_im * z_im, x_re * z_im + x_im * z_re)
            columns.append([jnp.broadcast_to(value, (pairs, span)) for value in column])
        for couple in range(per_long // 2):
            near = couple < edge // 2 or couple >= (per_long - edge) // 2
            thin = couple if couple < edge // 2 else couple - (per_long - per_mid) // 2
            if not held and not near:
                continue
            y_re, y_im = (y_ref[part : part + 1, couple * span : (couple + 1) * span] for part in range(2))
            tiles = []
            for parity in range(2):
                parts = [None, None]
                if near:
                    top = (parity * per_long + across) * pairs

                    def taken(table, part):
                        left = part * mid_len + thin * span
                        return first[table * long_len + top : table * long_len + top + pairs, left : left + span]

                    parts = [taken(0, 0) - taken(1, 1), taken(1, 0) + taken(0, 1)]
                if held:
                    top = (parity * per_mid + narrow) * pairs

                    def turned(table, part):
                        left = table * long_len + couple * span
                        return second[part * mid_len + top : part * mid_len + top + pairs, left : left + span]

                    terms = [turned(0, 0) - turned(1, 1), turned(1, 0) + turned(0, 1)]
                    parts = [a + b for a, b in zip(parts, terms)] if near else terms
                x_re, x_im = columns[parity]
                factor_re = x_re * y_re - x_im * y_im
                factor_im = x_re * y_im + x_im * y_re
                tiles.append(
                    [
                        parts[0] * factor_re - parts[1] * factor_im,
                        parts[0] * factor_im + parts[1] * factor_re,
                    ]
                )
            for part in range(2):
                even, odd = tiles[0][part], tiles[1][part]
                block = across * per_long + 2 * couple
                left = jnp.where(low, even, pltpu.roll(odd, 2 * pairs, 1))
                right = jnp.where(low, pltpu.roll(even, 2 * pairs, 1), odd)
                out_ref[rows_ref[block], 0, part] = left.astype(jnp.bfloat16)
                out_ref[rows_ref[block + 1], 0, part] = right.astype(jnp.bfloat16)


def transform_long(sources, row_ids, z_factor, x_factor, y_factor, first, second, row_count, pairs):
    if len(sources) == 1:
        pencils, classes, slots, _, local_long, mid_len = sources[0].shape
    else:
        pencils = len(sources)
        classes, slots, _, local_long, mid_len = sources[0].shape
    block = (pencils, classes, 1, 2, local_long, mid_len)
    if len(sources) == 1:
        specs = [pl.BlockSpec(block, lambda i: (0, 0, i, 0, 0, 0))]
        scratch = []
    else:
        specs = [pl.BlockSpec(block[1:], lambda i: (0, i, 0, 0, 0))] * pencils
        scratch = [pltpu.VMEM(block, jnp.bfloat16)]
    depth = 2 * pencils * local_long
    shape = (row_count, slots, 2, pairs, 4 * pairs)
    return pl.pallas_call(
        long_kernel,
        grid=(slots,),
        in_specs=[
            pl.BlockSpec(memory_space=pltpu.SMEM),
            pl.BlockSpec(memory_space=pltpu.SMEM),
            pl.BlockSpec(x_factor.shape, lambda i: (0, 0, 0, 0)),
            pl.BlockSpec(y_factor.shape, lambda i: (0, 0)),
            pl.BlockSpec(first.shape, lambda i: (0, 0)),
            pl.BlockSpec(second.shape, lambda i: (0, 0)),
        ]
        + specs,
        scratch_shapes=scratch,
        out_specs=pl.BlockSpec((row_count, 1, 2, pairs, 4 * pairs), lambda i: (0, i, 0, 0, 0)),
        out_shape=jax.ShapeDtypeStruct(shape, jnp.bfloat16),
        compiler_params=pltpu.CompilerParams(vmem_limit_bytes=VMEM_LIMIT),
        cost_estimate=pl.CostEstimate(
            flops=2 * classes * slots * depth * depth * mid_len,
            bytes_accessed=4 * slots * math.prod(block) + 2 * math.prod(shape) + 4 * depth * depth,
            transcendentals=0,
        ),
        name="transform_long",
    )(row_ids, z_factor, x_factor, y_factor, first, second, *sources)


def rows_kernel(turn_ref, *refs):
    sources, out_ref = refs[:-1], refs[-1]
    back = lax.axis_index("pencil") >= 2
    _, _, slots, parts, pairs, span = sources[0].shape
    z_local = out_ref.shape[2]

    def write(order):
        for row, top in itertools.product(range(out_ref.shape[0]), range(0, z_local, 8)):
            sides = []
            for part in range(parts):
                taken = []
                for z in range(top, top + 8):
                    device, place = divmod(order(z), len(sources) * slots)
                    chunk, slot = divmod(place, slots)
                    taken.append(sources[chunk][device, row, slot, part])
                sides.append(jnp.concatenate(taken, axis=0))
            turned = jnp.dot(
                turn_ref[...], jnp.concatenate(sides, axis=1), preferred_element_type=jnp.float32
            )
            for part in range(parts):
                for pair in range(pairs):
                    out_ref[row, part, top : top + 8, pair * span : (pair + 1) * span] = turned[
                        pair * 8 : (pair + 1) * 8, part * span : (part + 1) * span
                    ]

    @pl.when(jnp.logical_not(back))
    def _():
        write(lambda z: z)

    @pl.when(back)
    def _():
        write(lambda z: (z_local - z) % z_local)


def lay_rows(sources, z_local):
    grid_count, rows, slots, parts, pairs, span = sources[0].shape
    return pl.pallas_call(
        rows_kernel,
        grid=(rows // ROWS_PER_STEP,),
        in_specs=[pl.BlockSpec((8 * pairs, 8 * pairs), lambda i: (0, 0))]
        + [pl.BlockSpec((grid_count, ROWS_PER_STEP, slots, parts, pairs, span), lambda i: (0, i, 0, 0, 0, 0))]
        * len(sources),
        out_specs=pl.BlockSpec((ROWS_PER_STEP, parts, z_local, pairs * span), lambda i: (i, 0, 0, 0)),
        out_shape=jax.ShapeDtypeStruct((rows, parts, z_local, pairs * span), jnp.float32),
        compiler_params=pltpu.CompilerParams(vmem_limit_bytes=VMEM_LIMIT),
        cost_estimate=pl.CostEstimate(
            flops=0, bytes_accessed=6 * len(sources) * sources[0].size, transcendentals=0
        ),
        name="lay_rows",
    )(turning(8, pairs), *sources)


PAIR_SAME = [(d, d ^ 2) for d in range(8)]
PAIR_CROSS = [(d, d ^ 3) for d in range(8)]
INNER_SAME = [(2, 4), (4, 2), (3, 5), (5, 3)]
INNER_CROSS = [(2, 5), (5, 2), (3, 4), (4, 3)]
INNER_CORES = [(d, d ^ 1) for d in range(2, 6)]
CORES = [(d, d ^ 1) for d in range(8)]
ENTER_SAME = [(0, 2), (1, 3), (6, 4), (7, 5)]
ENTER_CROSS = [(0, 3), (1, 2), (6, 5), (7, 4)]
JUMP_SAME = [(d, d ^ 4) for d in range(8)]
JUMP_MIXED = [(0, 5), (1, 4), (6, 3), (7, 2), (2, 6), (3, 7), (4, 0), (5, 1)]


def after(values, earlier):
    return lax.optimization_barrier((list(values), list(earlier)))[0]


def send(value, pairs):
    return lax.ppermute(value, "grid", pairs)


def hold_kernel(value_ref, *refs):
    out_ref = refs[-1]
    for row in range(value_ref.shape[0]):
        for column in range(value_ref.shape[1]):
            out_ref[row, column] = value_ref[row, column]


def hold(value, earlier):
    return pl.pallas_call(
        hold_kernel,
        in_specs=[pl.BlockSpec(memory_space=pltpu.SMEM)]
        + [pl.BlockSpec(memory_space=pl.ANY)] * len(earlier),
        out_specs=pl.BlockSpec(memory_space=pltpu.SMEM),
        out_shape=jax.ShapeDtypeStruct(value.shape, value.dtype),
        cost_estimate=pl.CostEstimate(flops=HOLD_COST, bytes_accessed=0, transcendentals=0),
        name="hold",
    )(value, *earlier)


def exchange(parts, axis):
    count = len(parts)
    got = {0: parts[0]}
    for step in reversed(range(1, count)):
        got[step] = lax.ppermute(parts[step], axis, [(d, d ^ step) for d in range(count)])
    return [got[step] for step in range(count)]


def tied(values, twins):
    return [after([value], [twin])[0] for value, twin in zip(values, twins)]


def send_early(units, twins):
    values = [units[0], units[1], units[5], units[2], units[3]]
    plans = (PAIR_SAME, PAIR_CROSS, INNER_CORES, INNER_SAME, INNER_CROSS)
    if twins:
        values = tied(values, twins)
    return [send(value, pairs) for value, pairs in zip(values, plans)]


def send_jump(sums, twins):
    if twins:
        sums = tied(sums, twins)
    return [send(value, pairs) for value, pairs in zip(sums, (JUMP_SAME, JUMP_MIXED))]


def send_enter(units, twins):
    return [send(value, pairs) for value, pairs in zip(tied(units[2:4], twins), (ENTER_SAME, ENTER_CROSS))]


def mode_factor(modes, diffusion, speed, long_len, mid_len):
    magnitude = jnp.exp(diffusion * modes * modes * (-4.0 / (long_len * long_len)))
    phase = speed * modes * (-2.0 * math.pi / mid_len)
    return magnitude * jnp.cos(phase), magnitude * jnp.sin(phase)


def body(field, levels, coefficients, failed, owner_map, velocity, diffusivity):
    samples = field[0]
    local_long, mid_len, z_len = samples.shape
    pencils = lax.axis_size("pencil")
    grid_count = lax.axis_size("grid")
    long_len = local_long * pencils
    z_local = z_len // pencils
    block_len = mid_len // 4
    per_long = long_len // block_len
    per_mid = mid_len // block_len
    row_count = 2 * per_long * per_mid - per_mid * per_mid
    per_device = z_len // (grid_count * pencils)
    slots = per_device // CHUNKS
    me = lax.axis_index("grid")
    pencil = lax.axis_index("pencil")

    positions = jnp.arange(long_len, dtype=jnp.int32)
    modes = signed_modes(positions, long_len)
    x_re, x_im = mode_factor(modes, diffusivity[0], velocity[0], long_len, mid_len)
    y_re, y_im = mode_factor(modes, diffusivity[1], velocity[1], long_len, mid_len)
    x_factor = jnp.stack([x_re, x_im]).reshape(2, long_len // 2, 2).transpose(0, 2, 1)[..., None]
    y_factor = jnp.stack([y_re, y_im])
    place_in = me * per_device + jnp.arange(per_device, dtype=jnp.int32)
    back = pencil >= pencils // 2
    z_index = pencil * z_local + jnp.where(back, (z_local - place_in) % z_local, place_in)
    z_re, z_im = mode_factor(
        signed_modes(z_index, z_len), diffusivity[2], velocity[2], long_len, mid_len
    )
    z_factor = jnp.stack([z_re, z_im]) * (1.0 / math.sqrt(long_len * mid_len * z_len))

    mid = mid_table(mid_len, block_len)
    first, second = long_tables(long_len, block_len)
    tables = [z_table(chunk, CHUNKS, grid_count, pencils, z_len) for chunk in range(CHUNKS)]
    tables = jnp.stack([v.reshape(grid_count, -1, v.shape[1]) for v in tables])
    units = transform_z(samples, levels, coefficients, failed, tables)
    units = [list(units[chunk * grid_count : (chunk + 1) * grid_count]) for chunk in range(CHUNKS)]

    units[0][4], x_factor, y_factor, z_factor = lax.optimization_barrier(
        (units[0][4], x_factor, y_factor, z_factor)
    )
    early, sums = [], []
    for chunk in range(CHUNKS):
        early.append(send_early(units[chunk], early[-1] if early else None))
    for chunk in range(CHUNKS):
        got = early[chunk]
        third = after(units[chunk][4:6], got[3:] if chunk else [])
        sums.append(relay([third[0], got[2], got[0], got[1]], third))
    cores = [send(units[chunk][7], CORES) for chunk in range(CHUNKS)]
    jumps = [send_jump(sums[0], None)]
    enters = [send_enter(units[0], early[-1][:2])]
    arrived = []
    rows = None
    for chunk in range(CHUNKS):
        got = early[chunk]
        sources = [units[chunk][6], cores[chunk]] + enters[chunk] + jumps[chunk] + got[3:5] + got[0:2]
        last = chunk == CHUNKS - 1
        if not last:
            sources = after(sources, sums[chunk + 1])
            jumps.append(send_jump(sums[chunk + 1], jumps[chunk]))
        else:
            sources = after(sources, [rows])
        along_mid = transform_mid(sources, mid, chunk == 0, last, CHUNKS, pencils, slots)
        factor = z_factor[:, chunk * slots : (chunk + 1) * slots]
        if not last:
            enters.append(send_enter(units[chunk + 1], enters[chunk]))
            factor = hold(factor, [cores[chunk + 1]])
            along_mid = along_mid.reshape(along_mid.shape[:4] + (local_long, mid_len))
            lines = [lax.all_to_all(along_mid, "pencil", split_axis=0, concat_axis=0, tiled=True)]
        else:
            along_mid = [v.reshape(v.shape[:3] + (local_long, mid_len)) for v in along_mid]
            lines = exchange(along_mid, "pencil")
        rows = transform_long(
            lines,
            owner_map,
            factor,
            x_factor,
            y_factor,
            first,
            second,
            row_count,
            block_len // 2,
        )
        rows = rows.reshape((grid_count, -1) + rows.shape[1:])
        sent = after([rows], jumps[-1] + enters[-1])[0]
        arrived.append(lax.all_to_all(sent, "grid", split_axis=0, concat_axis=0, tiled=True))
    return lay_rows(arrived, z_local)


def solution(mesh):
    placed = (P("grid", "pencil", None, None), P("grid", None), P("grid"), P("grid"), P(), P(), P())
    devices = mesh.shape["grid"] * mesh.shape["pencil"]

    def run(field, *rest):
        few = mesh.shape["grid"] == 8 and mesh.shape["pencil"] == 4 and field.shape[3] % (devices * CHUNKS) == 0
        return jax.shard_map(
            body if few else wide_body,
            mesh=mesh,
            in_specs=placed,
            out_specs=P("grid", None, "pencil", None),
            check_vma=False,
        )(field, *rest)

    return run
```

```python
import functools
import itertools
import math

import jax
import jax.numpy as jnp
import numpy as np
from jax import lax
from jax.experimental import pallas as pl
from jax.experimental.pallas import tpu as pltpu
from jax.sharding import PartitionSpec as P

CHUNKS = 2
MID_COST = 40
HOLD_COST = 100_000_000_000
ROWS_PER_STEP = 3
VMEM_LIMIT = 56 * 1024 * 1024


def signed_modes(positions, length):
    return jnp.where(positions < length // 2, positions, positions - length).astype(jnp.float32)


def dft_tables(length):
    positions = jnp.arange(length, dtype=jnp.int32)
    product = positions[:, None] * positions[None, :] % length
    angles = product.astype(jnp.float32) * (2.0 * math.pi / length)
    return jnp.stack([jnp.cos(angles), -jnp.sin(angles)]).astype(jnp.bfloat16)


def complex_table(length):
    tables = dft_tables(length)
    return jnp.stack([jnp.stack([tables[0], -tables[1]]), jnp.stack([tables[1], tables[0]])])


def apply_factor(
    spectrum,
    z_modes,
    long_modes,
    mid_modes,
    swapped,
    velocity,
    diffusivity,
    long_len,
    mid_len,
    z_len,
):
    nu_long = jnp.where(swapped, diffusivity[1], diffusivity[0])
    nu_mid = jnp.where(swapped, diffusivity[0], diffusivity[1])
    speed_long = jnp.where(swapped, velocity[1], velocity[0])
    speed_mid = jnp.where(swapped, velocity[0], velocity[1])
    z_grid = z_modes[:, None, None]
    long_grid = long_modes[None, :, None]
    mid_grid = mid_modes[None, None, :]
    exponent = (
        diffusivity[2] * z_grid * z_grid
        + nu_long * long_grid * long_grid
        + nu_mid * mid_grid * mid_grid
    ) * (-4.0 / (long_len * long_len))
    phases = (velocity[2] * z_grid + speed_long * long_grid + speed_mid * mid_grid) * (
        -2.0 * math.pi / mid_len
    )
    magnitude = jnp.exp(exponent) * (1.0 / math.sqrt(long_len * mid_len * z_len))
    factor_re = magnitude * jnp.cos(phases)
    factor_im = magnitude * jnp.sin(phases)
    real_part = spectrum[0] * factor_re - spectrum[1] * factor_im
    imag_part = spectrum[0] * factor_im + spectrum[1] * factor_re
    return jnp.stack([real_part, imag_part])


def block_rows(swapped, owner_map, per_long, per_mid):
    along_long = jnp.arange(per_long, dtype=jnp.int32)[:, None] * jnp.ones((1, per_mid), jnp.int32)
    mid_raw = jnp.arange(per_mid, dtype=jnp.int32)
    mid_global = jnp.where(mid_raw < per_mid // 2, mid_raw, mid_raw + per_long - per_mid)
    along_mid = jnp.ones((per_long, 1), jnp.int32) * mid_global[None, :]
    block_x = jnp.where(swapped, along_mid, along_long)
    block_y = jnp.where(swapped, along_long, along_mid)
    return owner_map[(block_x * per_long + block_y).reshape(-1)]


def turn_inner(grouped):
    return grouped.transpose(0, 1, 2, 3, 5, 4)


def keep_inner(grouped):
    return grouped


def wide_body(field, levels, coefficients, failed, owner_map, velocity, diffusivity):
    samples = field[0]
    local_long, mid_len, z_len = samples.shape
    pencils = lax.axis_size("pencil")
    grid_count = lax.axis_size("grid")
    long_len = local_long * pencils
    z_local = z_len // pencils
    block_len = mid_len // 4
    per_long = long_len // block_len
    per_mid = mid_len // block_len
    swapped = levels[0, 0] < levels[0, 1]
    along_z = jnp.einsum(
        "abc,pck->pabk", samples, dft_tables(z_len), preferred_element_type=jnp.float32
    ).astype(jnp.bfloat16)
    along_mid = jnp.einsum(
        "qabc,pqbd->padc", along_z, complex_table(mid_len), preferred_element_type=jnp.float32
    ).astype(jnp.bfloat16)
    table_long = complex_table(long_len)
    spectrum = jnp.einsum(
        "qabc,pqae->pceb",
        lax.all_to_all(along_mid, "pencil", split_axis=3, concat_axis=1, tiled=True),
        table_long,
        preferred_element_type=jnp.float32,
    )
    z_start = lax.axis_index("pencil") * z_local
    z_modes = signed_modes(z_start + jnp.arange(z_local, dtype=jnp.int32), z_len)
    long_modes = signed_modes(jnp.arange(long_len, dtype=jnp.int32), long_len)
    mid_modes = signed_modes(jnp.arange(mid_len, dtype=jnp.int32), mid_len)
    shifted = apply_factor(
        spectrum,
        z_modes,
        long_modes,
        mid_modes,
        swapped,
        velocity,
        diffusivity,
        long_len,
        mid_len,
        z_len,
    )
    grouped = shifted.reshape(2, z_local, per_long, block_len, per_mid, block_len).transpose(
        2, 4, 0, 1, 3, 5
    )
    turned = lax.cond(swapped, turn_inner, keep_inner, grouped)
    held_count = per_long * per_mid
    blocks = turned.reshape(held_count, 2, z_local, block_len * block_len)
    row_ids = block_rows(swapped, owner_map, per_long, per_mid)
    weight = (coefficients[0] * (1 - failed[0])).astype(jnp.float32)
    weighted = blocks * weight
    slot_count = (2 * held_count - per_mid * per_mid) // grid_count
    capacity = held_count // grid_count
    owners = row_ids // slot_count
    slot_ids = row_ids % slot_count
    positions_all = jnp.arange(held_count, dtype=jnp.int32)
    earlier = (owners[:, None] == owners[None, :]) & (
        positions_all[None, :] < positions_all[:, None]
    )
    rank_in = jnp.sum(earlier.astype(jnp.int32), axis=1)
    target = owners * capacity + rank_in
    outgoing = (
        jnp.zeros_like(weighted)
        .at[target]
        .set(weighted)
        .reshape(grid_count, capacity, 2, z_local, block_len * block_len)
    )
    labels = (
        jnp.zeros((held_count,), jnp.float32)
        .at[target]
        .set(slot_ids.astype(jnp.float32))
        .reshape(grid_count, capacity)
    )
    incoming, got_labels = (
        lax.all_to_all(outgoing, "grid", split_axis=0, concat_axis=0, tiled=True),
        lax.all_to_all(labels, "grid", split_axis=0, concat_axis=0, tiled=True),
    )
    selector = (
        got_labels.reshape(1, -1)
        == jnp.arange(slot_count, dtype=jnp.int32).astype(jnp.float32)[:, None]
    ).astype(jnp.float32)
    combined = jnp.dot(
        selector, incoming.reshape(grid_count * capacity, -1), precision=lax.Precision.HIGHEST
    ).reshape(slot_count, 2, z_local, block_len * block_len)
    return combined


def host_tables(length):
    positions = np.arange(length)
    angles = (positions[:, None] * positions[None, :] % length) * (2.0 * math.pi / length)
    return np.cos(angles), -np.sin(angles)


def z_table(chunk, chunks, grid_count, pencils, z_len):
    groups = pencils // 2
    per_device = z_len // (grid_count * pencils)
    slots = per_device // chunks
    cos, sin = host_tables(z_len)
    table = np.zeros((grid_count, 2, chunks, groups, slots, chunks, z_len))
    for device in range(grid_count):
        for group in range(groups):
            for slot in range(slots):
                index = chunk * slots + slot
                mode = group * (z_len // pencils) + device * per_device + index
                parts = [cos[:, mode], sin[:, mode]]
                if mode == 0:
                    parts[1] = cos[:, z_len // 2]
                for half in range(chunks):
                    table[device, 0, half, group, slot, half] = parts[0]
                    table[device, 1, half, group, slot, half] = parts[1]
    return jnp.asarray(table.reshape(-1, chunks * z_len), jnp.bfloat16)


def mid_table(mid_len, block_len):
    cos, sin = host_tables(mid_len)
    order = np.arange(mid_len).reshape(mid_len // block_len, block_len // 2, 2).transpose(2, 0, 1).reshape(-1)
    plain = np.concatenate([cos, sin], axis=1)
    turned = np.concatenate([cos[:, order], sin[:, order]], axis=1)
    return jnp.asarray(np.stack([plain, turned]), jnp.bfloat16)


def long_tables(long_len, block_len):
    tables = host_tables(long_len)
    order = np.arange(long_len).reshape(long_len // block_len, block_len // 2, 2).transpose(2, 0, 1).reshape(-1)
    first = np.concatenate([table[order] for table in tables], axis=0)
    second = np.concatenate(tables, axis=1)
    return jnp.asarray(first, jnp.bfloat16), jnp.asarray(second, jnp.bfloat16)


def z_kernel(levels_ref, coefficient_ref, failed_ref, table_ref, field_ref, *out_refs):
    halves, rows, mid_len, z_len = field_ref.shape
    tiles, _, columns, lanes = out_refs[0].shape
    last = pl.num_programs(0) - 1
    me = lax.axis_index("grid")
    chip, core = me // 2, me % 2
    odd = chip % 2
    units = []
    for aim in (3 - 3 * odd, 1 + odd, (chip + 2) % 4, chip):
        units += [2 * aim + core, 2 * aim + 1 - core]

    @pl.when(pl.program_id(0) < last)
    def _():
        lines = [field_ref[half].reshape(rows * mid_len, z_len) for half in range(halves)]
        joined = jnp.concatenate(lines, axis=1)
        table = [table_ref[chunk, unit] for chunk in range(halves) for unit in units]
        found = lax.dot_general(
            jnp.concatenate(table, axis=0), joined, (((1,), (1,)), ((), ())), preferred_element_type=jnp.float32
        ).astype(jnp.bfloat16)
        for unit, out_ref in enumerate(out_refs):
            for tile in range(tiles):
                for row in range(rows):
                    left = row * mid_len + tile * lanes
                    out_ref[tile, row] = found[unit * columns : (unit + 1) * columns, left : left + lanes]

    @pl.when(pl.program_id(0) == last)
    def _():
        weight = (coefficient_ref[0] * (1 - failed_ref[0])).astype(jnp.float32)
        swapped = levels_ref[0, 0] < levels_ref[0, 1]
        for tile in range(tiles):
            value = jnp.where(swapped == (tile == 1), weight, 0.0)
            value = jnp.full((columns, lanes), value, jnp.float32).astype(jnp.bfloat16)
            for out_ref in out_refs:
                out_ref[tile, 0] = value


def transform_z(samples, levels, coefficients, failed, table):
    local_long, mid_len, z_len = samples.shape
    chunks, units, columns, _ = table.shape
    rows = 32
    lines = local_long // chunks
    steps = lines // rows
    tiles = 2
    lanes = mid_len // tiles
    units *= chunks
    split = samples.reshape(chunks, lines, mid_len, z_len)
    return pl.pallas_call(
        z_kernel,
        grid=(steps + 1,),
        in_specs=[
            pl.BlockSpec(memory_space=pltpu.SMEM),
            pl.BlockSpec(memory_space=pltpu.SMEM),
            pl.BlockSpec(memory_space=pltpu.SMEM),
            pl.BlockSpec(table.shape, lambda i: (0, 0, 0, 0)),
            pl.BlockSpec((chunks, rows, mid_len, z_len), lambda i: (0, jnp.minimum(i, steps - 1), 0, 0)),
        ],
        out_specs=[pl.BlockSpec((tiles, rows, columns, lanes), lambda i: (0, i, 0, 0))] * units,
        out_shape=[jax.ShapeDtypeStruct((tiles, lines + 1, columns, lanes), jnp.bfloat16)] * units,
        compiler_params=pltpu.CompilerParams(vmem_limit_bytes=VMEM_LIMIT),
        cost_estimate=pl.CostEstimate(
            flops=2 * units * columns * samples.size, bytes_accessed=4 * samples.size, transcendentals=0
        ),
        name="transform_z",
    )(levels, coefficients, failed, table, split)


def is_outer():
    me = lax.axis_index("grid")
    return (me < 2) | (me >= 6)


def unit_specs(shape, rows):
    tiles, lines, columns, lanes = shape
    return [
        pl.BlockSpec((tiles, rows, columns, lanes), lambda i: (0, i, 0, 0)),
        pl.BlockSpec((tiles, 1, columns, lanes), lambda i: (0, lines - 1, 0, 0)),
    ]


def weighted_sum(sources, weights, kind):
    total = None
    for source, weight in zip(sources, weights):
        term = source * weight[kind]
        total = term if total is None else total + term
    return total


def relay_kernel(*refs):
    out_refs = refs[-2:]
    passing = [refs[-4], refs[-3]]
    sources, weights = refs[:-4:2], refs[1:-4:2]
    rows = out_refs[0].shape[1]
    last = pl.num_programs(0) - 1
    outer = is_outer()

    @pl.when(outer)
    def _():
        for out_ref, source in zip(out_refs, passing):
            out_ref[...] = source[...]

    @pl.when(jnp.logical_not(outer))
    def _():
        values = [source[...].astype(jnp.float32) for source in sources]
        scales = [weight[...].astype(jnp.float32) for weight in weights]
        for kind, out_ref in enumerate(out_refs):
            out_ref[...] = weighted_sum(values, scales, kind).astype(jnp.bfloat16)

    @pl.when(jnp.logical_not(outer) & (pl.program_id(0) == last))
    def _():
        for kind, out_ref in enumerate(out_refs):
            for tile in range(out_ref.shape[0]):
                out_ref[tile, rows - 1] = jnp.full(out_ref.shape[2:], float(tile == kind), jnp.bfloat16)


def relay(sources, passing):
    shape = sources[0].shape
    rows = 13 if shape[1] % 13 == 0 else 1
    specs = unit_specs(shape, rows)
    return pl.pallas_call(
        relay_kernel,
        grid=(shape[1] // rows,),
        in_specs=specs * len(sources) + specs[:1] * 2,
        out_specs=specs[:1] * 2,
        out_shape=[jax.ShapeDtypeStruct(shape, jnp.bfloat16)] * 2,
        compiler_params=pltpu.CompilerParams(vmem_limit_bytes=VMEM_LIMIT),
        cost_estimate=pl.CostEstimate(
            flops=0, bytes_accessed=2 * (len(sources) + 4) * math.prod(shape), transcendentals=0
        ),
        name="relay",
    )(*[ref for source in sources for ref in (source, source)], *passing)


def turning(outer, inner):
    rows = np.arange(outer * inner)
    return jnp.asarray(rows[:, None] % outer * inner + rows[:, None] // outer == rows[None, :], jnp.bfloat16)


def mid_kernel(first_chunk, apart, turn_ref, table_ref, *refs):
    out_refs = []
    if apart:
        refs, out_refs = refs[: -apart - 1] + refs[-1:], refs[-apart - 1 : -1]
    refs, out_ref = refs[:-1], refs[-1]
    tiles, rows, columns, lanes = refs[0].shape
    mid_len = tiles * lanes
    half = columns // 2
    pencils, classes, slots, _, halves = out_ref.shape[:5]
    groups = pencils // 2
    lead = lax.axis_index("grid") == 0
    outer = is_outer()
    sources = [ref[...] for ref in refs[0::2]]
    weights = [ref[...] for ref in refs[1::2]]
    for kept in (sources, weights):
        for spare in (-1, -2):
            kept[spare - 2] = jnp.where(outer, kept[spare], kept[spare - 2])
        del kept[-2:]
    sources = [source.astype(jnp.float32) for source in sources]
    weights = [weight.astype(jnp.float32) for weight in weights]
    for kind in range(classes):
        total = weighted_sum(sources, weights, kind).astype(jnp.bfloat16)
        lines = jnp.concatenate([total[tile].reshape(rows * columns, lanes) for tile in range(tiles)], axis=1)
        lines = jnp.dot(turn_ref[...], lines, preferred_element_type=jnp.float32).astype(jnp.bfloat16)
        product = jnp.dot(lines, table_ref[kind], preferred_element_type=jnp.float32)
        product = product.reshape(columns, rows, 2 * mid_len)
        re_cos, re_sin = product[:half, :, :mid_len], product[:half, :, mid_len:]
        im_cos, im_sin = product[half:, :, :mid_len], product[half:, :, mid_len:]
        for part in range(2):
            alone, other = (re_cos, im_cos) if part == 0 else (re_sin, im_sin)
            up = re_cos - im_sin if part == 0 else re_sin + im_cos
            down = re_cos + im_sin if part == 0 else re_sin - im_cos
            for piece in range(halves):
                for group in range(groups):
                    for slot in range(slots):
                        at = (piece * groups + group) * slots + slot
                        value, mirrored = up[at], down[at]
                        if first_chunk and slot == 0:
                            follower = (piece * groups + (group + 1) % groups) * slots
                            if group == 0:
                                value = jnp.where(lead, alone[at], value)
                            turn = down[follower] if group + 1 < groups else other[follower]
                            mirrored = jnp.where(lead, turn, mirrored)
                        out_ref[group, kind, slot, part, piece] = value.astype(jnp.bfloat16)
                        out_ref[pencils - 1 - group, kind, slot, part, piece] = mirrored.astype(jnp.bfloat16)
    for step, apart_ref in enumerate(out_refs):
        apart_ref[...] = out_ref[lax.axis_index("pencil") ^ step]


def transform_mid(sources, table, first_chunk, apart, chunks, pencils, slots):
    tiles, lines, columns, lanes = sources[0].shape
    lines -= 1
    classes, mid_len, _ = table.shape
    rows = 32
    shape = (pencils, classes, slots, 2, chunks, lines, mid_len)
    block = shape[:5] + (rows, mid_len)
    if apart:
        layout = dict(
            out_specs=[pl.BlockSpec(block[1:], lambda i: (0, 0, 0, 0, i, 0))] * pencils,
            out_shape=[jax.ShapeDtypeStruct(shape[1:], jnp.bfloat16)] * pencils,
            scratch_shapes=[pltpu.VMEM(block, jnp.bfloat16)],
        )
    else:
        layout = dict(
            out_specs=pl.BlockSpec(block, lambda i: (0, 0, 0, 0, 0, i, 0)),
            out_shape=jax.ShapeDtypeStruct(shape, jnp.bfloat16),
        )
    size = sources[0].size
    return pl.pallas_call(
        functools.partial(mid_kernel, first_chunk, pencils if apart else 0),
        grid=(lines // rows,),
        in_specs=[
            pl.BlockSpec((rows * columns, rows * columns), lambda i: (0, 0)),
            pl.BlockSpec(table.shape, lambda i: (0, 0, 0)),
        ]
        + unit_specs(sources[0].shape, rows) * len(sources),
        compiler_params=pltpu.CompilerParams(vmem_limit_bytes=VMEM_LIMIT),
        cost_estimate=pl.CostEstimate(
            flops=MID_COST * 8 * size * mid_len,
            bytes_accessed=2 * len(sources) * size + 2 * math.prod(shape),
            transcendentals=0,
        ),
        name="transform_mid",
        **layout,
    )(turning(rows, columns), table, *[ref for source in sources for ref in (source, source)])


def long_kernel(rows_ref, z_ref, x_ref, y_ref, first_ref, second_ref, *refs):
    if len(refs) == 2:
        source_ref, out_ref = refs
    else:
        sources, out_ref, source_ref = refs[:-2], refs[-2], refs[-1]
        for step, source in enumerate(sources):
            source_ref[lax.axis_index("pencil") ^ step] = source[...]
    pencils, classes, _, _, local_long, mid_len = source_ref.shape
    long_len = pencils * local_long
    pairs = out_ref.shape[3]
    per_long = long_len // (2 * pairs)
    per_mid = mid_len // (2 * pairs)
    edge = per_mid // 2
    slot = pl.program_id(0)
    lines = [
        jnp.concatenate(
            [source_ref[:, kind, 0, part].reshape(long_len, mid_len) for part in range(2)], axis=1
        )
        for kind in range(classes)
    ]
    first = jnp.dot(first_ref[...], lines[0], preferred_element_type=jnp.float32)
    second = lax.dot_general(
        lines[1], second_ref[...], (((0,), (0,)), ((), ())), preferred_element_type=jnp.float32
    )
    z_re, z_im = z_ref[0, slot], z_ref[1, slot]
    low = lax.broadcasted_iota(jnp.int32, (pairs, 4 * pairs), 1) < 2 * pairs
    span = 4 * pairs
    for across in range(per_long):
        held = across < edge or across >= per_long - edge
        narrow = across if across < edge else across - (per_long - per_mid)
        columns = []
        for parity in range(2):
            x_re, x_im = (x_ref[part, parity, across * pairs : (across + 1) * pairs] for part in range(2))
            column = (x_re * z_re - x_im * z_im, x_re * z_im + x_im * z_re)
            columns.append([jnp.broadcast_to(value, (pairs, span)) for value in column])
        for couple in range(per_long // 2):
            near = couple < edge // 2 or couple >= (per_long - edge) // 2
            thin = couple if couple < edge // 2 else couple - (per_long - per_mid) // 2
            if not held and not near:
                continue
            y_re, y_im = (y_ref[part : part + 1, couple * span : (couple + 1) * span] for part in range(2))
            tiles = []
            for parity in range(2):
                parts = [None, None]
                if near:
                    top = (parity * per_long + across) * pairs

                    def taken(table, part):
                        left = part * mid_len + thin * span
                        return first[table * long_len + top : table * long_len + top + pairs, left : left + span]

                    parts = [taken(0, 0) - taken(1, 1), taken(1, 0) + taken(0, 1)]
                if held:
                    top = (parity * per_mid + narrow) * pairs

                    def turned(table, part):
                        left = table * long_len + couple * span
                        return second[part * mid_len + top : part * mid_len + top + pairs, left : left + span]

                    terms = [turned(0, 0) - turned(1, 1), turned(1, 0) + turned(0, 1)]
                    parts = [a + b for a, b in zip(parts, terms)] if near else terms
                x_re, x_im = columns[parity]
                factor_re = x_re * y_re - x_im * y_im
                factor_im = x_re * y_im + x_im * y_re
                tiles.append(
                    [
                        parts[0] * factor_re - parts[1] * factor_im,
                        parts[0] * factor_im + parts[1] * factor_re,
                    ]
                )
            for part in range(2):
                even, odd = tiles[0][part], tiles[1][part]
                block = across * per_long + 2 * couple
                left = jnp.where(low, even, pltpu.roll(odd, 2 * pairs, 1))
                right = jnp.where(low, pltpu.roll(even, 2 * pairs, 1), odd)
                out_ref[rows_ref[block], 0, part] = left.astype(jnp.bfloat16)
                out_ref[rows_ref[block + 1], 0, part] = right.astype(jnp.bfloat16)


def transform_long(sources, row_ids, z_factor, x_factor, y_factor, first, second, row_count, pairs):
    if len(sources) == 1:
        pencils, classes, slots, _, local_long, mid_len = sources[0].shape
    else:
        pencils = len(sources)
        classes, slots, _, local_long, mid_len = sources[0].shape
    block = (pencils, classes, 1, 2, local_long, mid_len)
    if len(sources) == 1:
        specs = [pl.BlockSpec(block, lambda i: (0, 0, i, 0, 0, 0))]
        scratch = []
    else:
        specs = [pl.BlockSpec(block[1:], lambda i: (0, i, 0, 0, 0))] * pencils
        scratch = [pltpu.VMEM(block, jnp.bfloat16)]
    depth = 2 * pencils * local_long
    shape = (row_count, slots, 2, pairs, 4 * pairs)
    return pl.pallas_call(
        long_kernel,
        grid=(slots,),
        in_specs=[
            pl.BlockSpec(memory_space=pltpu.SMEM),
            pl.BlockSpec(memory_space=pltpu.SMEM),
            pl.BlockSpec(x_factor.shape, lambda i: (0, 0, 0, 0)),
            pl.BlockSpec(y_factor.shape, lambda i: (0, 0)),
            pl.BlockSpec(first.shape, lambda i: (0, 0)),
            pl.BlockSpec(second.shape, lambda i: (0, 0)),
        ]
        + specs,
        scratch_shapes=scratch,
        out_specs=pl.BlockSpec((row_count, 1, 2, pairs, 4 * pairs), lambda i: (0, i, 0, 0, 0)),
        out_shape=jax.ShapeDtypeStruct(shape, jnp.bfloat16),
        compiler_params=pltpu.CompilerParams(vmem_limit_bytes=VMEM_LIMIT),
        cost_estimate=pl.CostEstimate(
            flops=2 * classes * slots * depth * depth * mid_len,
            bytes_accessed=4 * slots * math.prod(block) + 2 * math.prod(shape) + 4 * depth * depth,
            transcendentals=0,
        ),
        name="transform_long",
    )(row_ids, z_factor, x_factor, y_factor, first, second, *sources)


def rows_kernel(turn_ref, *refs):
    sources, out_ref = refs[:-1], refs[-1]
    back = lax.axis_index("pencil") >= 2
    _, _, slots, parts, pairs, span = sources[0].shape
    z_local = out_ref.shape[2]

    def write(order):
        for row, top in itertools.product(range(out_ref.shape[0]), range(0, z_local, 8)):
            sides = []
            for part in range(parts):
                taken = []
                for z in range(top, top + 8):
                    device, place = divmod(order(z), len(sources) * slots)
                    chunk, slot = divmod(place, slots)
                    taken.append(sources[chunk][device, row, slot, part])
                sides.append(jnp.concatenate(taken, axis=0))
            turned = jnp.dot(
                turn_ref[...], jnp.concatenate(sides, axis=1), preferred_element_type=jnp.float32
            )
            for part in range(parts):
                for pair in range(pairs):
                    out_ref[row, part, top : top + 8, pair * span : (pair + 1) * span] = turned[
                        pair * 8 : (pair + 1) * 8, part * span : (part + 1) * span
                    ]

    @pl.when(jnp.logical_not(back))
    def _():
        write(lambda z: z)

    @pl.when(back)
    def _():
        write(lambda z: (z_local - z) % z_local)


def lay_rows(sources, z_local):
    grid_count, rows, slots, parts, pairs, span = sources[0].shape
    return pl.pallas_call(
        rows_kernel,
        grid=(rows // ROWS_PER_STEP,),
        in_specs=[pl.BlockSpec((8 * pairs, 8 * pairs), lambda i: (0, 0))]
        + [pl.BlockSpec((grid_count, ROWS_PER_STEP, slots, parts, pairs, span), lambda i: (0, i, 0, 0, 0, 0))]
        * len(sources),
        out_specs=pl.BlockSpec((ROWS_PER_STEP, parts, z_local, pairs * span), lambda i: (i, 0, 0, 0)),
        out_shape=jax.ShapeDtypeStruct((rows, parts, z_local, pairs * span), jnp.float32),
        compiler_params=pltpu.CompilerParams(vmem_limit_bytes=VMEM_LIMIT),
        cost_estimate=pl.CostEstimate(
            flops=0, bytes_accessed=6 * len(sources) * sources[0].size, transcendentals=0
        ),
        name="lay_rows",
    )(turning(8, pairs), *sources)


PAIR_SAME = [(d, d ^ 2) for d in range(8)]
PAIR_CROSS = [(d, d ^ 3) for d in range(8)]
INNER_SAME = [(2, 4), (4, 2), (3, 5), (5, 3)]
INNER_CROSS = [(2, 5), (5, 2), (3, 4), (4, 3)]
INNER_CORES = [(d, d ^ 1) for d in range(2, 6)]
CORES = [(d, d ^ 1) for d in range(8)]
ENTER_SAME = [(0, 2), (1, 3), (6, 4), (7, 5)]
ENTER_CROSS = [(0, 3), (1, 2), (6, 5), (7, 4)]
JUMP_SAME = [(d, d ^ 4) for d in range(8)]
JUMP_MIXED = [(0, 5), (1, 4), (6, 3), (7, 2), (2, 6), (3, 7), (4, 0), (5, 1)]


def after(values, earlier):
    return lax.optimization_barrier((list(values), list(earlier)))[0]


def send(value, pairs):
    return lax.ppermute(value, "grid", pairs)


def hold_kernel(value_ref, *refs):
    out_ref = refs[-1]
    for row in range(value_ref.shape[0]):
        for column in range(value_ref.shape[1]):
            out_ref[row, column] = value_ref[row, column]


def hold(value, earlier):
    return pl.pallas_call(
        hold_kernel,
        in_specs=[pl.BlockSpec(memory_space=pltpu.SMEM)]
        + [pl.BlockSpec(memory_space=pl.ANY)] * len(earlier),
        out_specs=pl.BlockSpec(memory_space=pltpu.SMEM),
        out_shape=jax.ShapeDtypeStruct(value.shape, value.dtype),
        cost_estimate=pl.CostEstimate(flops=HOLD_COST, bytes_accessed=0, transcendentals=0),
        name="hold",
    )(value, *earlier)


def exchange(parts, axis):
    count = len(parts)
    got = {0: parts[0]}
    for step in reversed(range(1, count)):
        got[step] = lax.ppermute(parts[step], axis, [(d, d ^ step) for d in range(count)])
    return [got[step] for step in range(count)]


def tied(values, twins):
    return [after([value], [twin])[0] for value, twin in zip(values, twins)]


def send_early(units, twins):
    values = [units[0], units[1], units[5], units[2], units[3]]
    plans = (PAIR_SAME, PAIR_CROSS, INNER_CORES, INNER_SAME, INNER_CROSS)
    if twins:
        values = tied(values, twins)
    return [send(value, pairs) for value, pairs in zip(values, plans)]


def send_jump(sums, twins):
    if twins:
        sums = tied(sums, twins)
    return [send(value, pairs) for value, pairs in zip(sums, (JUMP_SAME, JUMP_MIXED))]


def send_enter(units, twins):
    return [send(value, pairs) for value, pairs in zip(tied(units[2:4], twins), (ENTER_SAME, ENTER_CROSS))]


def mode_factor(modes, diffusion, speed, long_len, mid_len):
    magnitude = jnp.exp(diffusion * modes * modes * (-4.0 / (long_len * long_len)))
    phase = speed * modes * (-2.0 * math.pi / mid_len)
    return magnitude * jnp.cos(phase), magnitude * jnp.sin(phase)


def body(field, levels, coefficients, failed, owner_map, velocity, diffusivity):
    samples = field[0]
    local_long, mid_len, z_len = samples.shape
    pencils = lax.axis_size("pencil")
    grid_count = lax.axis_size("grid")
    long_len = local_long * pencils
    z_local = z_len // pencils
    block_len = mid_len // 4
    per_long = long_len // block_len
    per_mid = mid_len // block_len
    row_count = 2 * per_long * per_mid - per_mid * per_mid
    per_device = z_len // (grid_count * pencils)
    slots = per_device // CHUNKS
    me = lax.axis_index("grid")
    pencil = lax.axis_index("pencil")

    positions = jnp.arange(long_len, dtype=jnp.int32)
    modes = signed_modes(positions, long_len)
    x_re, x_im = mode_factor(modes, diffusivity[0], velocity[0], long_len, mid_len)
    y_re, y_im = mode_factor(modes, diffusivity[1], velocity[1], long_len, mid_len)
    x_factor = jnp.stack([x_re, x_im]).reshape(2, long_len // 2, 2).transpose(0, 2, 1)[..., None]
    y_factor = jnp.stack([y_re, y_im])
    place_in = me * per_device + jnp.arange(per_device, dtype=jnp.int32)
    back = pencil >= pencils // 2
    z_index = pencil * z_local + jnp.where(back, (z_local - place_in) % z_local, place_in)
    z_re, z_im = mode_factor(
        signed_modes(z_index, z_len), diffusivity[2], velocity[2], long_len, mid_len
    )
    z_factor = jnp.stack([z_re, z_im]) * (1.0 / math.sqrt(long_len * mid_len * z_len))

    mid = mid_table(mid_len, block_len)
    first, second = long_tables(long_len, block_len)
    tables = [z_table(chunk, CHUNKS, grid_count, pencils, z_len) for chunk in range(CHUNKS)]
    tables = jnp.stack([v.reshape(grid_count, -1, v.shape[1]) for v in tables])
    units = transform_z(samples, levels, coefficients, failed, tables)
    units = [list(units[chunk * grid_count : (chunk + 1) * grid_count]) for chunk in range(CHUNKS)]

    units[0][4], x_factor, y_factor, z_factor = lax.optimization_barrier(
        (units[0][4], x_factor, y_factor, z_factor)
    )
    early, sums = [], []
    for chunk in range(CHUNKS):
        early.append(send_early(units[chunk], early[-1] if early else None))
    for chunk in range(CHUNKS):
        got = early[chunk]
        third = after(units[chunk][4:6], got[3:] if chunk else [])
        sums.append(relay([third[0], got[2], got[0], got[1]], third))
    cores = [send(units[chunk][7], CORES) for chunk in range(CHUNKS)]
    jumps = [send_jump(sums[0], None)]
    enters = [send_enter(units[0], early[-1][:2])]
    arrived = []
    rows = None
    for chunk in range(CHUNKS):
        got = early[chunk]
        sources = [units[chunk][6], cores[chunk]] + enters[chunk] + jumps[chunk] + got[3:5] + got[0:2]
        last = chunk == CHUNKS - 1
        if not last:
            sources = after(sources, sums[chunk + 1])
            jumps.append(send_jump(sums[chunk + 1], jumps[chunk]))
        else:
            sources = after(sources, [rows])
        along_mid = transform_mid(sources, mid, chunk == 0, last, CHUNKS, pencils, slots)
        factor = z_factor[:, chunk * slots : (chunk + 1) * slots]
        if not last:
            enters.append(send_enter(units[chunk + 1], enters[chunk]))
            factor = hold(factor, [cores[chunk + 1]])
            along_mid = along_mid.reshape(along_mid.shape[:4] + (local_long, mid_len))
            lines = [lax.all_to_all(along_mid, "pencil", split_axis=0, concat_axis=0, tiled=True)]
        else:
            along_mid = [v.reshape(v.shape[:3] + (local_long, mid_len)) for v in along_mid]
            lines = exchange(along_mid, "pencil")
        rows = transform_long(
            lines,
            owner_map,
            factor,
            x_factor,
            y_factor,
            first,
            second,
            row_count,
            block_len // 2,
        )
        rows = rows.reshape((grid_count, -1) + rows.shape[1:])
        sent = rows
        arrived.append(lax.all_to_all(sent, "grid", split_axis=0, concat_axis=0, tiled=True))
    return lay_rows(arrived, z_local)


def solution(mesh):
    placed = (P("grid", "pencil", None, None), P("grid", None), P("grid"), P("grid"), P(), P(), P())
    devices = mesh.shape["grid"] * mesh.shape["pencil"]

    def run(field, *rest):
        few = mesh.shape["grid"] == 8 and mesh.shape["pencil"] == 4 and field.shape[3] % (devices * CHUNKS) == 0
        return jax.shard_map(
            body if few else wide_body,
            mesh=mesh,
            in_specs=placed,
            out_specs=P("grid", None, "pencil", None),
            check_vma=False,
        )(field, *rest)

    return run
```

```python
import functools
import itertools
import math

import jax
import jax.numpy as jnp
import numpy as np
from jax import lax
from jax.experimental import pallas as pl
from jax.experimental.pallas import tpu as pltpu
from jax.sharding import PartitionSpec as P

CHUNKS = 2
MID_COST = 40
HOLD_COST = 1000_000_000_000
ROWS_PER_STEP = 3
VMEM_LIMIT = 56 * 1024 * 1024


def signed_modes(positions, length):
    return jnp.where(positions < length // 2, positions, positions - length).astype(jnp.float32)


def dft_tables(length):
    positions = jnp.arange(length, dtype=jnp.int32)
    product = positions[:, None] * positions[None, :] % length
    angles = product.astype(jnp.float32) * (2.0 * math.pi / length)
    return jnp.stack([jnp.cos(angles), -jnp.sin(angles)]).astype(jnp.bfloat16)


def complex_table(length):
    tables = dft_tables(length)
    return jnp.stack([jnp.stack([tables[0], -tables[1]]), jnp.stack([tables[1], tables[0]])])


def apply_factor(
    spectrum,
    z_modes,
    long_modes,
    mid_modes,
    swapped,
    velocity,
    diffusivity,
    long_len,
    mid_len,
    z_len,
):
    nu_long = jnp.where(swapped, diffusivity[1], diffusivity[0])
    nu_mid = jnp.where(swapped, diffusivity[0], diffusivity[1])
    speed_long = jnp.where(swapped, velocity[1], velocity[0])
    speed_mid = jnp.where(swapped, velocity[0], velocity[1])
    z_grid = z_modes[:, None, None]
    long_grid = long_modes[None, :, None]
    mid_grid = mid_modes[None, None, :]
    exponent = (
        diffusivity[2] * z_grid * z_grid
        + nu_long * long_grid * long_grid
        + nu_mid * mid_grid * mid_grid
    ) * (-4.0 / (long_len * long_len))
    phases = (velocity[2] * z_grid + speed_long * long_grid + speed_mid * mid_grid) * (
        -2.0 * math.pi / mid_len
    )
    magnitude = jnp.exp(exponent) * (1.0 / math.sqrt(long_len * mid_len * z_len))
    factor_re = magnitude * jnp.cos(phases)
    factor_im = magnitude * jnp.sin(phases)
    real_part = spectrum[0] * factor_re - spectrum[1] * factor_im
    imag_part = spectrum[0] * factor_im + spectrum[1] * factor_re
    return jnp.stack([real_part, imag_part])


def block_rows(swapped, owner_map, per_long, per_mid):
    along_long = jnp.arange(per_long, dtype=jnp.int32)[:, None] * jnp.ones((1, per_mid), jnp.int32)
    mid_raw = jnp.arange(per_mid, dtype=jnp.int32)
    mid_global = jnp.where(mid_raw < per_mid // 2, mid_raw, mid_raw + per_long - per_mid)
    along_mid = jnp.ones((per_long, 1), jnp.int32) * mid_global[None, :]
    block_x = jnp.where(swapped, along_mid, along_long)
    block_y = jnp.where(swapped, along_long, along_mid)
    return owner_map[(block_x * per_long + block_y).reshape(-1)]


def turn_inner(grouped):
    return grouped.transpose(0, 1, 2, 3, 5, 4)


def keep_inner(grouped):
    return grouped


def wide_body(field, levels, coefficients, failed, owner_map, velocity, diffusivity):
    samples = field[0]
    local_long, mid_len, z_len = samples.shape
    pencils = lax.axis_size("pencil")
    grid_count = lax.axis_size("grid")
    long_len = local_long * pencils
    z_local = z_len // pencils
    block_len = mid_len // 4
    per_long = long_len // block_len
    per_mid = mid_len // block_len
    swapped = levels[0, 0] < levels[0, 1]
    along_z = jnp.einsum(
        "abc,pck->pabk", samples, dft_tables(z_len), preferred_element_type=jnp.float32
    ).astype(jnp.bfloat16)
    along_mid = jnp.einsum(
        "qabc,pqbd->padc", along_z, complex_table(mid_len), preferred_element_type=jnp.float32
    ).astype(jnp.bfloat16)
    table_long = complex_table(long_len)
    spectrum = jnp.einsum(
        "qabc,pqae->pceb",
        lax.all_to_all(along_mid, "pencil", split_axis=3, concat_axis=1, tiled=True),
        table_long,
        preferred_element_type=jnp.float32,
    )
    z_start = lax.axis_index("pencil") * z_local
    z_modes = signed_modes(z_start + jnp.arange(z_local, dtype=jnp.int32), z_len)
    long_modes = signed_modes(jnp.arange(long_len, dtype=jnp.int32), long_len)
    mid_modes = signed_modes(jnp.arange(mid_len, dtype=jnp.int32), mid_len)
    shifted = apply_factor(
        spectrum,
        z_modes,
        long_modes,
        mid_modes,
        swapped,
        velocity,
        diffusivity,
        long_len,
        mid_len,
        z_len,
    )
    grouped = shifted.reshape(2, z_local, per_long, block_len, per_mid, block_len).transpose(
        2, 4, 0, 1, 3, 5
    )
    turned = lax.cond(swapped, turn_inner, keep_inner, grouped)
    held_count = per_long * per_mid
    blocks = turned.reshape(held_count, 2, z_local, block_len * block_len)
    row_ids = block_rows(swapped, owner_map, per_long, per_mid)
    weight = (coefficients[0] * (1 - failed[0])).astype(jnp.float32)
    weighted = blocks * weight
    slot_count = (2 * held_count - per_mid * per_mid) // grid_count
    capacity = held_count // grid_count
    owners = row_ids // slot_count
    slot_ids = row_ids % slot_count
    positions_all = jnp.arange(held_count, dtype=jnp.int32)
    earlier = (owners[:, None] == owners[None, :]) & (
        positions_all[None, :] < positions_all[:, None]
    )
    rank_in = jnp.sum(earlier.astype(jnp.int32), axis=1)
    target = owners * capacity + rank_in
    outgoing = (
        jnp.zeros_like(weighted)
        .at[target]
        .set(weighted)
        .reshape(grid_count, capacity, 2, z_local, block_len * block_len)
    )
    labels = (
        jnp.zeros((held_count,), jnp.float32)
        .at[target]
        .set(slot_ids.astype(jnp.float32))
        .reshape(grid_count, capacity)
    )
    incoming, got_labels = (
        lax.all_to_all(outgoing, "grid", split_axis=0, concat_axis=0, tiled=True),
        lax.all_to_all(labels, "grid", split_axis=0, concat_axis=0, tiled=True),
    )
    selector = (
        got_labels.reshape(1, -1)
        == jnp.arange(slot_count, dtype=jnp.int32).astype(jnp.float32)[:, None]
    ).astype(jnp.float32)
    combined = jnp.dot(
        selector, incoming.reshape(grid_count * capacity, -1), precision=lax.Precision.HIGHEST
    ).reshape(slot_count, 2, z_local, block_len * block_len)
    return combined


def host_tables(length):
    positions = np.arange(length)
    angles = (positions[:, None] * positions[None, :] % length) * (2.0 * math.pi / length)
    return np.cos(angles), -np.sin(angles)


def z_table(chunk, chunks, grid_count, pencils, z_len):
    groups = pencils // 2
    per_device = z_len // (grid_count * pencils)
    slots = per_device // chunks
    cos, sin = host_tables(z_len)
    table = np.zeros((grid_count, 2, chunks, groups, slots, chunks, z_len))
    for device in range(grid_count):
        for group in range(groups):
            for slot in range(slots):
                index = chunk * slots + slot
                mode = group * (z_len // pencils) + device * per_device + index
                parts = [cos[:, mode], sin[:, mode]]
                if mode == 0:
                    parts[1] = cos[:, z_len // 2]
                for half in range(chunks):
                    table[device, 0, half, group, slot, half] = parts[0]
                    table[device, 1, half, group, slot, half] = parts[1]
    return jnp.asarray(table.reshape(-1, chunks * z_len), jnp.bfloat16)


def mid_table(mid_len, block_len):
    cos, sin = host_tables(mid_len)
    order = np.arange(mid_len).reshape(mid_len // block_len, block_len // 2, 2).transpose(2, 0, 1).reshape(-1)
    plain = np.concatenate([cos, sin], axis=1)
    turned = np.concatenate([cos[:, order], sin[:, order]], axis=1)
    return jnp.asarray(np.stack([plain, turned]), jnp.bfloat16)


def long_tables(long_len, block_len):
    tables = host_tables(long_len)
    order = np.arange(long_len).reshape(long_len // block_len, block_len // 2, 2).transpose(2, 0, 1).reshape(-1)
    first = np.concatenate([table[order] for table in tables], axis=0)
    second = np.concatenate(tables, axis=1)
    return jnp.asarray(first, jnp.bfloat16), jnp.asarray(second, jnp.bfloat16)


def z_kernel(levels_ref, coefficient_ref, failed_ref, table_ref, field_ref, *out_refs):
    halves, rows, mid_len, z_len = field_ref.shape
    tiles, _, columns, lanes = out_refs[0].shape
    last = pl.num_programs(0) - 1
    me = lax.axis_index("grid")
    chip, core = me // 2, me % 2
    odd = chip % 2
    units = []
    for aim in (3 - 3 * odd, 1 + odd, (chip + 2) % 4, chip):
        units += [2 * aim + core, 2 * aim + 1 - core]

    @pl.when(pl.program_id(0) < last)
    def _():
        lines = [field_ref[half].reshape(rows * mid_len, z_len) for half in range(halves)]
        joined = jnp.concatenate(lines, axis=1)
        table = [table_ref[chunk, unit] for chunk in range(halves) for unit in units]
        found = lax.dot_general(
            jnp.concatenate(table, axis=0), joined, (((1,), (1,)), ((), ())), preferred_element_type=jnp.float32
        ).astype(jnp.bfloat16)
        for unit, out_ref in enumerate(out_refs):
            for tile in range(tiles):
                for row in range(rows):
                    left = row * mid_len + tile * lanes
                    out_ref[tile, row] = found[unit * columns : (unit + 1) * columns, left : left + lanes]

    @pl.when(pl.program_id(0) == last)
    def _():
        weight = (coefficient_ref[0] * (1 - failed_ref[0])).astype(jnp.float32)
        swapped = levels_ref[0, 0] < levels_ref[0, 1]
        for tile in range(tiles):
            value = jnp.where(swapped == (tile == 1), weight, 0.0)
            value = jnp.full((columns, lanes), value, jnp.float32).astype(jnp.bfloat16)
            for out_ref in out_refs:
                out_ref[tile, 0] = value


def transform_z(samples, levels, coefficients, failed, table):
    local_long, mid_len, z_len = samples.shape
    chunks, units, columns, _ = table.shape
    rows = 32
    lines = local_long // chunks
    steps = lines // rows
    tiles = 2
    lanes = mid_len // tiles
    units *= chunks
    split = samples.reshape(chunks, lines, mid_len, z_len)
    return pl.pallas_call(
        z_kernel,
        grid=(steps + 1,),
        in_specs=[
            pl.BlockSpec(memory_space=pltpu.SMEM),
            pl.BlockSpec(memory_space=pltpu.SMEM),
            pl.BlockSpec(memory_space=pltpu.SMEM),
            pl.BlockSpec(table.shape, lambda i: (0, 0, 0, 0)),
            pl.BlockSpec((chunks, rows, mid_len, z_len), lambda i: (0, jnp.minimum(i, steps - 1), 0, 0)),
        ],
        out_specs=[pl.BlockSpec((tiles, rows, columns, lanes), lambda i: (0, i, 0, 0))] * units,
        out_shape=[jax.ShapeDtypeStruct((tiles, lines + 1, columns, lanes), jnp.bfloat16)] * units,
        compiler_params=pltpu.CompilerParams(vmem_limit_bytes=VMEM_LIMIT),
        cost_estimate=pl.CostEstimate(
            flops=2 * units * columns * samples.size, bytes_accessed=4 * samples.size, transcendentals=0
        ),
        name="transform_z",
    )(levels, coefficients, failed, table, split)


def is_outer():
    me = lax.axis_index("grid")
    return (me < 2) | (me >= 6)


def unit_specs(shape, rows):
    tiles, lines, columns, lanes = shape
    return [
        pl.BlockSpec((tiles, rows, columns, lanes), lambda i: (0, i, 0, 0)),
        pl.BlockSpec((tiles, 1, columns, lanes), lambda i: (0, lines - 1, 0, 0)),
    ]


def weighted_sum(sources, weights, kind):
    total = None
    for source, weight in zip(sources, weights):
        term = source * weight[kind]
        total = term if total is None else total + term
    return total


def relay_kernel(*refs):
    out_refs = refs[-2:]
    passing = [refs[-4], refs[-3]]
    sources, weights = refs[:-4:2], refs[1:-4:2]
    rows = out_refs[0].shape[1]
    last = pl.num_programs(0) - 1
    outer = is_outer()

    @pl.when(outer)
    def _():
        for out_ref, source in zip(out_refs, passing):
            out_ref[...] = source[...]

    @pl.when(jnp.logical_not(outer))
    def _():
        values = [source[...].astype(jnp.float32) for source in sources]
        scales = [weight[...].astype(jnp.float32) for weight in weights]
        for kind, out_ref in enumerate(out_refs):
            out_ref[...] = weighted_sum(values, scales, kind).astype(jnp.bfloat16)

    @pl.when(jnp.logical_not(outer) & (pl.program_id(0) == last))
    def _():
        for kind, out_ref in enumerate(out_refs):
            for tile in range(out_ref.shape[0]):
                out_ref[tile, rows - 1] = jnp.full(out_ref.shape[2:], float(tile == kind), jnp.bfloat16)


def relay(sources, passing):
    shape = sources[0].shape
    rows = 13 if shape[1] % 13 == 0 else 1
    specs = unit_specs(shape, rows)
    return pl.pallas_call(
        relay_kernel,
        grid=(shape[1] // rows,),
        in_specs=specs * len(sources) + specs[:1] * 2,
        out_specs=specs[:1] * 2,
        out_shape=[jax.ShapeDtypeStruct(shape, jnp.bfloat16)] * 2,
        compiler_params=pltpu.CompilerParams(vmem_limit_bytes=VMEM_LIMIT),
        cost_estimate=pl.CostEstimate(
            flops=0, bytes_accessed=2 * (len(sources) + 4) * math.prod(shape), transcendentals=0
        ),
        name="relay",
    )(*[ref for source in sources for ref in (source, source)], *passing)


def turning(outer, inner):
    rows = np.arange(outer * inner)
    return jnp.asarray(rows[:, None] % outer * inner + rows[:, None] // outer == rows[None, :], jnp.bfloat16)


def mid_kernel(first_chunk, apart, turn_ref, table_ref, *refs):
    out_refs = []
    if apart:
        refs, out_refs = refs[: -apart - 1] + refs[-1:], refs[-apart - 1 : -1]
    refs, out_ref = refs[:-1], refs[-1]
    tiles, rows, columns, lanes = refs[0].shape
    mid_len = tiles * lanes
    half = columns // 2
    pencils, classes, slots, _, halves = out_ref.shape[:5]
    groups = pencils // 2
    lead = lax.axis_index("grid") == 0
    outer = is_outer()
    sources = [ref[...] for ref in refs[0::2]]
    weights = [ref[...] for ref in refs[1::2]]
    for kept in (sources, weights):
        for spare in (-1, -2):
            kept[spare - 2] = jnp.where(outer, kept[spare], kept[spare - 2])
        del kept[-2:]
    sources = [source.astype(jnp.float32) for source in sources]
    weights = [weight.astype(jnp.float32) for weight in weights]
    for kind in range(classes):
        total = weighted_sum(sources, weights, kind).astype(jnp.bfloat16)
        lines = jnp.concatenate([total[tile].reshape(rows * columns, lanes) for tile in range(tiles)], axis=1)
        lines = jnp.dot(turn_ref[...], lines, preferred_element_type=jnp.float32).astype(jnp.bfloat16)
        product = jnp.dot(lines, table_ref[kind], preferred_element_type=jnp.float32)
        product = product.reshape(columns, rows, 2 * mid_len)
        re_cos, re_sin = product[:half, :, :mid_len], product[:half, :, mid_len:]
        im_cos, im_sin = product[half:, :, :mid_len], product[half:, :, mid_len:]
        for part in range(2):
            alone, other = (re_cos, im_cos) if part == 0 else (re_sin, im_sin)
            up = re_cos - im_sin if part == 0 else re_sin + im_cos
            down = re_cos + im_sin if part == 0 else re_sin - im_cos
            for piece in range(halves):
                for group in range(groups):
                    for slot in range(slots):
                        at = (piece * groups + group) * slots + slot
                        value, mirrored = up[at], down[at]
                        if first_chunk and slot == 0:
                            follower = (piece * groups + (group + 1) % groups) * slots
                            if group == 0:
                                value = jnp.where(lead, alone[at], value)
                            turn = down[follower] if group + 1 < groups else other[follower]
                            mirrored = jnp.where(lead, turn, mirrored)
                        out_ref[group, kind, slot, part, piece] = value.astype(jnp.bfloat16)
                        out_ref[pencils - 1 - group, kind, slot, part, piece] = mirrored.astype(jnp.bfloat16)
    for step, apart_ref in enumerate(out_refs):
        apart_ref[...] = out_ref[lax.axis_index("pencil") ^ step]


def transform_mid(sources, table, first_chunk, apart, chunks, pencils, slots):
    tiles, lines, columns, lanes = sources[0].shape
    lines -= 1
    classes, mid_len, _ = table.shape
    rows = 32
    shape = (pencils, classes, slots, 2, chunks, lines, mid_len)
    block = shape[:5] + (rows, mid_len)
    if apart:
        layout = dict(
            out_specs=[pl.BlockSpec(block[1:], lambda i: (0, 0, 0, 0, i, 0))] * pencils,
            out_shape=[jax.ShapeDtypeStruct(shape[1:], jnp.bfloat16)] * pencils,
            scratch_shapes=[pltpu.VMEM(block, jnp.bfloat16)],
        )
    else:
        layout = dict(
            out_specs=pl.BlockSpec(block, lambda i: (0, 0, 0, 0, 0, i, 0)),
            out_shape=jax.ShapeDtypeStruct(shape, jnp.bfloat16),
        )
    size = sources[0].size
    return pl.pallas_call(
        functools.partial(mid_kernel, first_chunk, pencils if apart else 0),
        grid=(lines // rows,),
        in_specs=[
            pl.BlockSpec((rows * columns, rows * columns), lambda i: (0, 0)),
            pl.BlockSpec(table.shape, lambda i: (0, 0, 0)),
        ]
        + unit_specs(sources[0].shape, rows) * len(sources),
        compiler_params=pltpu.CompilerParams(vmem_limit_bytes=VMEM_LIMIT),
        cost_estimate=pl.CostEstimate(
            flops=MID_COST * 8 * size * mid_len,
            bytes_accessed=2 * len(sources) * size + 2 * math.prod(shape),
            transcendentals=0,
        ),
        name="transform_mid",
        **layout,
    )(turning(rows, columns), table, *[ref for source in sources for ref in (source, source)])


def long_kernel(rows_ref, z_ref, x_ref, y_ref, first_ref, second_ref, *refs):
    if len(refs) == 2:
        source_ref, out_ref = refs
    else:
        sources, out_ref, source_ref = refs[:-2], refs[-2], refs[-1]
        for step, source in enumerate(sources):
            source_ref[lax.axis_index("pencil") ^ step] = source[...]
    pencils, classes, _, _, local_long, mid_len = source_ref.shape
    long_len = pencils * local_long
    pairs = out_ref.shape[3]
    per_long = long_len // (2 * pairs)
    per_mid = mid_len // (2 * pairs)
    edge = per_mid // 2
    slot = pl.program_id(0)
    lines = [
        jnp.concatenate(
            [source_ref[:, kind, 0, part].reshape(long_len, mid_len) for part in range(2)], axis=1
        )
        for kind in range(classes)
    ]
    first = jnp.dot(first_ref[...], lines[0], preferred_element_type=jnp.float32)
    second = lax.dot_general(
        lines[1], second_ref[...], (((0,), (0,)), ((), ())), preferred_element_type=jnp.float32
    )
    z_re, z_im = z_ref[0, slot], z_ref[1, slot]
    low = lax.broadcasted_iota(jnp.int32, (pairs, 4 * pairs), 1) < 2 * pairs
    span = 4 * pairs
    for across in range(per_long):
        held = across < edge or across >= per_long - edge
        narrow = across if across < edge else across - (per_long - per_mid)
        columns = []
        for parity in range(2):
            x_re, x_im = (x_ref[part, parity, across * pairs : (across + 1) * pairs] for part in range(2))
            column = (x_re * z_re - x_im * z_im, x_re * z_im + x_im * z_re)
            columns.append([jnp.broadcast_to(value, (pairs, span)) for value in column])
        for couple in range(per_long // 2):
            near = couple < edge // 2 or couple >= (per_long - edge) // 2
            thin = couple if couple < edge // 2 else couple - (per_long - per_mid) // 2
            if not held and not near:
                continue
            y_re, y_im = (y_ref[part : part + 1, couple * span : (couple + 1) * span] for part in range(2))
            tiles = []
            for parity in range(2):
                parts = [None, None]
                if near:
                    top = (parity * per_long + across) * pairs

                    def taken(table, part):
                        left = part * mid_len + thin * span
                        return first[table * long_len + top : table * long_len + top + pairs, left : left + span]

                    parts = [taken(0, 0) - taken(1, 1), taken(1, 0) + taken(0, 1)]
                if held:
                    top = (parity * per_mid + narrow) * pairs

                    def turned(table, part):
                        left = table * long_len + couple * span
                        return second[part * mid_len + top : part * mid_len + top + pairs, left : left + span]

                    terms = [turned(0, 0) - turned(1, 1), turned(1, 0) + turned(0, 1)]
                    parts = [a + b for a, b in zip(parts, terms)] if near else terms
                x_re, x_im = columns[parity]
                factor_re = x_re * y_re - x_im * y_im
                factor_im = x_re * y_im + x_im * y_re
                tiles.append(
                    [
                        parts[0] * factor_re - parts[1] * factor_im,
                        parts[0] * factor_im + parts[1] * factor_re,
                    ]
                )
            for part in range(2):
                even, odd = tiles[0][part], tiles[1][part]
                block = across * per_long + 2 * couple
                left = jnp.where(low, even, pltpu.roll(odd, 2 * pairs, 1))
                right = jnp.where(low, pltpu.roll(even, 2 * pairs, 1), odd)
                out_ref[rows_ref[block], 0, part] = left.astype(jnp.bfloat16)
                out_ref[rows_ref[block + 1], 0, part] = right.astype(jnp.bfloat16)


def transform_long(sources, row_ids, z_factor, x_factor, y_factor, first, second, row_count, pairs):
    if len(sources) == 1:
        pencils, classes, slots, _, local_long, mid_len = sources[0].shape
    else:
        pencils = len(sources)
        classes, slots, _, local_long, mid_len = sources[0].shape
    block = (pencils, classes, 1, 2, local_long, mid_len)
    if len(sources) == 1:
        specs = [pl.BlockSpec(block, lambda i: (0, 0, i, 0, 0, 0))]
        scratch = []
    else:
        specs = [pl.BlockSpec(block[1:], lambda i: (0, i, 0, 0, 0))] * pencils
        scratch = [pltpu.VMEM(block, jnp.bfloat16)]
    depth = 2 * pencils * local_long
    shape = (row_count, slots, 2, pairs, 4 * pairs)
    return pl.pallas_call(
        long_kernel,
        grid=(slots,),
        in_specs=[
            pl.BlockSpec(memory_space=pltpu.SMEM),
            pl.BlockSpec(memory_space=pltpu.SMEM),
            pl.BlockSpec(x_factor.shape, lambda i: (0, 0, 0, 0)),
            pl.BlockSpec(y_factor.shape, lambda i: (0, 0)),
            pl.BlockSpec(first.shape, lambda i: (0, 0)),
            pl.BlockSpec(second.shape, lambda i: (0, 0)),
        ]
        + specs,
        scratch_shapes=scratch,
        out_specs=pl.BlockSpec((row_count, 1, 2, pairs, 4 * pairs), lambda i: (0, i, 0, 0, 0)),
        out_shape=jax.ShapeDtypeStruct(shape, jnp.bfloat16),
        compiler_params=pltpu.CompilerParams(vmem_limit_bytes=20 * 1024 * 1024),
        cost_estimate=pl.CostEstimate(
            flops=2 * classes * slots * depth * depth * mid_len,
            bytes_accessed=4 * slots * math.prod(block) + 2 * math.prod(shape) + 4 * depth * depth,
            transcendentals=0,
        ),
        name="transform_long",
    )(row_ids, z_factor, x_factor, y_factor, first, second, *sources)


def rows_kernel(turn_ref, *refs):
    sources, out_ref = refs[:-1], refs[-1]
    back = lax.axis_index("pencil") >= 2
    _, _, slots, parts, pairs, span = sources[0].shape
    z_local = out_ref.shape[2]

    def write(order):
        for row, top in itertools.product(range(out_ref.shape[0]), range(0, z_local, 8)):
            sides = []
            for part in range(parts):
                taken = []
                for z in range(top, top + 8):
                    device, place = divmod(order(z), len(sources) * slots)
                    chunk, slot = divmod(place, slots)
                    taken.append(sources[chunk][device, row, slot, part])
                sides.append(jnp.concatenate(taken, axis=0))
            turned = jnp.dot(
                turn_ref[...], jnp.concatenate(sides, axis=1), preferred_element_type=jnp.float32
            )
            for part in range(parts):
                for pair in range(pairs):
                    out_ref[row, part, top : top + 8, pair * span : (pair + 1) * span] = turned[
                        pair * 8 : (pair + 1) * 8, part * span : (part + 1) * span
                    ]

    @pl.when(jnp.logical_not(back))
    def _():
        write(lambda z: z)

    @pl.when(back)
    def _():
        write(lambda z: (z_local - z) % z_local)


def lay_rows(sources, z_local):
    grid_count, rows, slots, parts, pairs, span = sources[0].shape
    return pl.pallas_call(
        rows_kernel,
        grid=(rows // ROWS_PER_STEP,),
        in_specs=[pl.BlockSpec((8 * pairs, 8 * pairs), lambda i: (0, 0))]
        + [pl.BlockSpec((grid_count, ROWS_PER_STEP, slots, parts, pairs, span), lambda i: (0, i, 0, 0, 0, 0))]
        * len(sources),
        out_specs=pl.BlockSpec((ROWS_PER_STEP, parts, z_local, pairs * span), lambda i: (i, 0, 0, 0)),
        out_shape=jax.ShapeDtypeStruct((rows, parts, z_local, pairs * span), jnp.float32),
        compiler_params=pltpu.CompilerParams(vmem_limit_bytes=20 * 1024 * 1024),
        cost_estimate=pl.CostEstimate(
            flops=0, bytes_accessed=6 * len(sources) * sources[0].size, transcendentals=0
        ),
        name="lay_rows",
    )(turning(8, pairs), *sources)


PAIR_SAME = [(d, d ^ 2) for d in range(8)]
PAIR_CROSS = [(d, d ^ 3) for d in range(8)]
INNER_SAME = [(2, 4), (4, 2), (3, 5), (5, 3)]
INNER_CROSS = [(2, 5), (5, 2), (3, 4), (4, 3)]
INNER_CORES = [(d, d ^ 1) for d in range(2, 6)]
CORES = [(d, d ^ 1) for d in range(8)]
ENTER_SAME = [(0, 2), (1, 3), (6, 4), (7, 5)]
ENTER_CROSS = [(0, 3), (1, 2), (6, 5), (7, 4)]
JUMP_SAME = [(d, d ^ 4) for d in range(8)]
JUMP_MIXED = [(0, 5), (1, 4), (6, 3), (7, 2), (2, 6), (3, 7), (4, 0), (5, 1)]


def after(values, earlier):
    return lax.optimization_barrier((list(values), list(earlier)))[0]


def send(value, pairs):
    return lax.ppermute(value, "grid", pairs)


def hold_kernel(value_ref, *refs):
    out_ref = refs[-1]
    for row in range(value_ref.shape[0]):
        for column in range(value_ref.shape[1]):
            out_ref[row, column] = value_ref[row, column]


def hold(value, earlier):
    return pl.pallas_call(
        hold_kernel,
        in_specs=[pl.BlockSpec(memory_space=pltpu.SMEM)]
        + [pl.BlockSpec(memory_space=pl.ANY)] * len(earlier),
        out_specs=pl.BlockSpec(memory_space=pltpu.SMEM),
        out_shape=jax.ShapeDtypeStruct(value.shape, value.dtype),
        cost_estimate=pl.CostEstimate(flops=HOLD_COST, bytes_accessed=0, transcendentals=0),
        name="hold",
    )(value, *earlier)


def exchange(parts, axis):
    count = len(parts)
    got = {0: parts[0]}
    for step in reversed(range(1, count)):
        got[step] = lax.ppermute(parts[step], axis, [(d, d ^ step) for d in range(count)])
    return [got[step] for step in range(count)]


def tied(values, twins):
    return [after([value], [twin])[0] for value, twin in zip(values, twins)]


def send_early(units, twins):
    values = [units[0], units[1], units[5], units[2], units[3]]
    plans = (PAIR_SAME, PAIR_CROSS, INNER_CORES, INNER_SAME, INNER_CROSS)
    if twins:
        values = tied(values, twins)
    return [send(value, pairs) for value, pairs in zip(values, plans)]


def send_jump(sums, twins):
    if twins:
        sums = tied(sums, twins)
    return [send(value, pairs) for value, pairs in zip(sums, (JUMP_SAME, JUMP_MIXED))]


def send_enter(units, twins):
    return [send(value, pairs) for value, pairs in zip(tied(units[2:4], twins), (ENTER_SAME, ENTER_CROSS))]


def mode_factor(modes, diffusion, speed, long_len, mid_len):
    magnitude = jnp.exp(diffusion * modes * modes * (-4.0 / (long_len * long_len)))
    phase = speed * modes * (-2.0 * math.pi / mid_len)
    return magnitude * jnp.cos(phase), magnitude * jnp.sin(phase)


def body(field, levels, coefficients, failed, owner_map, velocity, diffusivity):
    samples = field[0]
    local_long, mid_len, z_len = samples.shape
    pencils = lax.axis_size("pencil")
    grid_count = lax.axis_size("grid")
    long_len = local_long * pencils
    z_local = z_len // pencils
    block_len = mid_len // 4
    per_long = long_len // block_len
    per_mid = mid_len // block_len
    row_count = 2 * per_long * per_mid - per_mid * per_mid
    per_device = z_len // (grid_count * pencils)
    slots = per_device // CHUNKS
    me = lax.axis_index("grid")
    pencil = lax.axis_index("pencil")

    positions = jnp.arange(long_len, dtype=jnp.int32)
    modes = signed_modes(positions, long_len)
    x_re, x_im = mode_factor(modes, diffusivity[0], velocity[0], long_len, mid_len)
    y_re, y_im = mode_factor(modes, diffusivity[1], velocity[1], long_len, mid_len)
    x_factor = jnp.stack([x_re, x_im]).reshape(2, long_len // 2, 2).transpose(0, 2, 1)[..., None]
    y_factor = jnp.stack([y_re, y_im])
    place_in = me * per_device + jnp.arange(per_device, dtype=jnp.int32)
    back = pencil >= pencils // 2
    z_index = pencil * z_local + jnp.where(back, (z_local - place_in) % z_local, place_in)
    z_re, z_im = mode_factor(
        signed_modes(z_index, z_len), diffusivity[2], velocity[2], long_len, mid_len
    )
    z_factor = jnp.stack([z_re, z_im]) * (1.0 / math.sqrt(long_len * mid_len * z_len))

    mid = mid_table(mid_len, block_len)
    first, second = long_tables(long_len, block_len)
    tables = [z_table(chunk, CHUNKS, grid_count, pencils, z_len) for chunk in range(CHUNKS)]
    tables = jnp.stack([v.reshape(grid_count, -1, v.shape[1]) for v in tables])
    units = transform_z(samples, levels, coefficients, failed, tables)
    units = [list(units[chunk * grid_count : (chunk + 1) * grid_count]) for chunk in range(CHUNKS)]

    units[0][4], x_factor, y_factor, z_factor = lax.optimization_barrier(
        (units[0][4], x_factor, y_factor, z_factor)
    )
    early, sums = [], []
    for chunk in range(CHUNKS):
        early.append(send_early(units[chunk], early[-1] if early else None))
    for chunk in range(CHUNKS):
        got = early[chunk]
        third = after(units[chunk][4:6], got[3:] if chunk else [])
        sums.append(relay([third[0], got[2], got[0], got[1]], third))
    cores = [send(units[chunk][7], CORES) for chunk in range(CHUNKS)]
    jumps = [send_jump(sums[0], None)]
    enters = [send_enter(units[0], early[0][3:])]
    arrived = []
    rows = None
    for chunk in range(CHUNKS):
        got = early[chunk]
        sources = [units[chunk][6], cores[chunk]] + enters[chunk] + jumps[chunk] + got[3:5] + got[0:2]
        last = chunk == CHUNKS - 1
        if not last:
            sources = after(sources, sums[chunk + 1])
            jumps.append(send_jump(sums[chunk + 1], jumps[chunk]))
        else:
            sources = after(sources, [rows])
        along_mid = transform_mid(sources, mid, chunk == 0, last, CHUNKS, pencils, slots)
        factor = z_factor[:, chunk * slots : (chunk + 1) * slots]
        if not last:
            enters.append(send_enter(units[chunk + 1], enters[chunk]))
            factor = hold(factor, [cores[chunk + 1]])
            along_mid = along_mid.reshape(along_mid.shape[:4] + (local_long, mid_len))
            lines = [lax.all_to_all(along_mid, "pencil", split_axis=0, concat_axis=0, tiled=True)]
        else:
            along_mid = [v.reshape(v.shape[:3] + (local_long, mid_len)) for v in along_mid]
            lines = exchange(along_mid, "pencil")
        rows = transform_long(
            lines,
            owner_map,
            factor,
            x_factor,
            y_factor,
            first,
            second,
            row_count,
            block_len // 2,
        )
        rows = rows.reshape((grid_count, -1) + rows.shape[1:])
        sent = rows
        arrived.append(lax.all_to_all(sent, "grid", split_axis=0, concat_axis=0, tiled=True))
    return lay_rows(arrived, z_local)


def solution(mesh):
    placed = (P("grid", "pencil", None, None), P("grid", None), P("grid"), P("grid"), P(), P(), P())
    devices = mesh.shape["grid"] * mesh.shape["pencil"]

    def run(field, *rest):
        few = mesh.shape["grid"] == 8 and mesh.shape["pencil"] == 4 and field.shape[3] % (devices * CHUNKS) == 0
        return jax.shard_map(
            body if few else wide_body,
            mesh=mesh,
            in_specs=placed,
            out_specs=P("grid", None, "pencil", None),
            check_vma=False,
        )(field, *rest)

    return run
```

```python
import functools
import itertools
import math

import jax
import jax.numpy as jnp
import numpy as np
from jax import lax
from jax.experimental import pallas as pl
from jax.experimental.pallas import tpu as pltpu
from jax.sharding import PartitionSpec as P

CHUNKS = 2
MID_COST = 40
HOLD_COST = 1000_000_000_000
ROWS_PER_STEP = 2
VMEM_LIMIT = 56 * 1024 * 1024


def signed_modes(positions, length):
    return jnp.where(positions < length // 2, positions, positions - length).astype(jnp.float32)


def dft_tables(length):
    positions = jnp.arange(length, dtype=jnp.int32)
    product = positions[:, None] * positions[None, :] % length
    angles = product.astype(jnp.float32) * (2.0 * math.pi / length)
    return jnp.stack([jnp.cos(angles), -jnp.sin(angles)]).astype(jnp.bfloat16)


def complex_table(length):
    tables = dft_tables(length)
    return jnp.stack([jnp.stack([tables[0], -tables[1]]), jnp.stack([tables[1], tables[0]])])


def apply_factor(
    spectrum,
    z_modes,
    long_modes,
    mid_modes,
    swapped,
    velocity,
    diffusivity,
    long_len,
    mid_len,
    z_len,
):
    nu_long = jnp.where(swapped, diffusivity[1], diffusivity[0])
    nu_mid = jnp.where(swapped, diffusivity[0], diffusivity[1])
    speed_long = jnp.where(swapped, velocity[1], velocity[0])
    speed_mid = jnp.where(swapped, velocity[0], velocity[1])
    z_grid = z_modes[:, None, None]
    long_grid = long_modes[None, :, None]
    mid_grid = mid_modes[None, None, :]
    exponent = (
        diffusivity[2] * z_grid * z_grid
        + nu_long * long_grid * long_grid
        + nu_mid * mid_grid * mid_grid
    ) * (-4.0 / (long_len * long_len))
    phases = (velocity[2] * z_grid + speed_long * long_grid + speed_mid * mid_grid) * (
        -2.0 * math.pi / mid_len
    )
    magnitude = jnp.exp(exponent) * (1.0 / math.sqrt(long_len * mid_len * z_len))
    factor_re = magnitude * jnp.cos(phases)
    factor_im = magnitude * jnp.sin(phases)
    real_part = spectrum[0] * factor_re - spectrum[1] * factor_im
    imag_part = spectrum[0] * factor_im + spectrum[1] * factor_re
    return jnp.stack([real_part, imag_part])


def block_rows(swapped, owner_map, per_long, per_mid):
    along_long = jnp.arange(per_long, dtype=jnp.int32)[:, None] * jnp.ones((1, per_mid), jnp.int32)
    mid_raw = jnp.arange(per_mid, dtype=jnp.int32)
    mid_global = jnp.where(mid_raw < per_mid // 2, mid_raw, mid_raw + per_long - per_mid)
    along_mid = jnp.ones((per_long, 1), jnp.int32) * mid_global[None, :]
    block_x = jnp.where(swapped, along_mid, along_long)
    block_y = jnp.where(swapped, along_long, along_mid)
    return owner_map[(block_x * per_long + block_y).reshape(-1)]


def turn_inner(grouped):
    return grouped.transpose(0, 1, 2, 3, 5, 4)


def keep_inner(grouped):
    return grouped


def wide_body(field, levels, coefficients, failed, owner_map, velocity, diffusivity):
    samples = field[0]
    local_long, mid_len, z_len = samples.shape
    pencils = lax.axis_size("pencil")
    grid_count = lax.axis_size("grid")
    long_len = local_long * pencils
    z_local = z_len // pencils
    block_len = mid_len // 4
    per_long = long_len // block_len
    per_mid = mid_len // block_len
    swapped = levels[0, 0] < levels[0, 1]
    along_z = jnp.einsum(
        "abc,pck->pabk", samples, dft_tables(z_len), preferred_element_type=jnp.float32
    ).astype(jnp.bfloat16)
    along_mid = jnp.einsum(
        "qabc,pqbd->padc", along_z, complex_table(mid_len), preferred_element_type=jnp.float32
    ).astype(jnp.bfloat16)
    table_long = complex_table(long_len)
    spectrum = jnp.einsum(
        "qabc,pqae->pceb",
        lax.all_to_all(along_mid, "pencil", split_axis=3, concat_axis=1, tiled=True),
        table_long,
        preferred_element_type=jnp.float32,
    )
    z_start = lax.axis_index("pencil") * z_local
    z_modes = signed_modes(z_start + jnp.arange(z_local, dtype=jnp.int32), z_len)
    long_modes = signed_modes(jnp.arange(long_len, dtype=jnp.int32), long_len)
    mid_modes = signed_modes(jnp.arange(mid_len, dtype=jnp.int32), mid_len)
    shifted = apply_factor(
        spectrum,
        z_modes,
        long_modes,
        mid_modes,
        swapped,
        velocity,
        diffusivity,
        long_len,
        mid_len,
        z_len,
    )
    grouped = shifted.reshape(2, z_local, per_long, block_len, per_mid, block_len).transpose(
        2, 4, 0, 1, 3, 5
    )
    turned = lax.cond(swapped, turn_inner, keep_inner, grouped)
    held_count = per_long * per_mid
    blocks = turned.reshape(held_count, 2, z_local, block_len * block_len)
    row_ids = block_rows(swapped, owner_map, per_long, per_mid)
    weight = (coefficients[0] * (1 - failed[0])).astype(jnp.float32)
    weighted = blocks * weight
    slot_count = (2 * held_count - per_mid * per_mid) // grid_count
    capacity = held_count // grid_count
    owners = row_ids // slot_count
    slot_ids = row_ids % slot_count
    positions_all = jnp.arange(held_count, dtype=jnp.int32)
    earlier = (owners[:, None] == owners[None, :]) & (
        positions_all[None, :] < positions_all[:, None]
    )
    rank_in = jnp.sum(earlier.astype(jnp.int32), axis=1)
    target = owners * capacity + rank_in
    outgoing = (
        jnp.zeros_like(weighted)
        .at[target]
        .set(weighted)
        .reshape(grid_count, capacity, 2, z_local, block_len * block_len)
    )
    labels = (
        jnp.zeros((held_count,), jnp.float32)
        .at[target]
        .set(slot_ids.astype(jnp.float32))
        .reshape(grid_count, capacity)
    )
    incoming, got_labels = (
        lax.all_to_all(outgoing, "grid", split_axis=0, concat_axis=0, tiled=True),
        lax.all_to_all(labels, "grid", split_axis=0, concat_axis=0, tiled=True),
    )
    selector = (
        got_labels.reshape(1, -1)
        == jnp.arange(slot_count, dtype=jnp.int32).astype(jnp.float32)[:, None]
    ).astype(jnp.float32)
    combined = jnp.dot(
        selector, incoming.reshape(grid_count * capacity, -1), precision=lax.Precision.HIGHEST
    ).reshape(slot_count, 2, z_local, block_len * block_len)
    return combined


def host_tables(length):
    positions = np.arange(length)
    angles = (positions[:, None] * positions[None, :] % length) * (2.0 * math.pi / length)
    return np.cos(angles), -np.sin(angles)


def z_table(chunk, chunks, grid_count, pencils, z_len):
    groups = pencils // 2
    per_device = z_len // (grid_count * pencils)
    slots = per_device // chunks
    cos, sin = host_tables(z_len)
    table = np.zeros((grid_count, 2, chunks, groups, slots, chunks, z_len))
    for device in range(grid_count):
        for group in range(groups):
            for slot in range(slots):
                index = chunk * slots + slot
                mode = group * (z_len // pencils) + device * per_device + index
                parts = [cos[:, mode], sin[:, mode]]
                if mode == 0:
                    parts[1] = cos[:, z_len // 2]
                for half in range(chunks):
                    table[device, 0, half, group, slot, half] = parts[0]
                    table[device, 1, half, group, slot, half] = parts[1]
    return jnp.asarray(table.reshape(-1, chunks * z_len), jnp.bfloat16)


def mid_table(mid_len, block_len):
    cos, sin = host_tables(mid_len)
    order = np.arange(mid_len).reshape(mid_len // block_len, block_len // 2, 2).transpose(2, 0, 1).reshape(-1)
    plain = np.concatenate([cos, sin], axis=1)
    turned = np.concatenate([cos[:, order], sin[:, order]], axis=1)
    return jnp.asarray(np.stack([plain, turned]), jnp.bfloat16)


def long_tables(long_len, block_len):
    tables = host_tables(long_len)
    order = np.arange(long_len).reshape(long_len // block_len, block_len // 2, 2).transpose(2, 0, 1).reshape(-1)
    first = np.concatenate([table[order] for table in tables], axis=0)
    second = np.concatenate(tables, axis=1)
    return jnp.asarray(first, jnp.bfloat16), jnp.asarray(second, jnp.bfloat16)


def z_kernel(levels_ref, coefficient_ref, failed_ref, table_ref, field_ref, *out_refs):
    halves, rows, mid_len, z_len = field_ref.shape
    tiles, _, columns, lanes = out_refs[0].shape
    last = pl.num_programs(0) - 1
    me = lax.axis_index("grid")
    chip, core = me // 2, me % 2
    odd = chip % 2
    units = []
    for aim in (3 - 3 * odd, 1 + odd, (chip + 2) % 4, chip):
        units += [2 * aim + core, 2 * aim + 1 - core]

    @pl.when(pl.program_id(0) < last)
    def _():
        lines = [field_ref[half].reshape(rows * mid_len, z_len) for half in range(halves)]
        joined = jnp.concatenate(lines, axis=1)
        table = [table_ref[chunk, unit] for chunk in range(halves) for unit in units]
        found = lax.dot_general(
            jnp.concatenate(table, axis=0), joined, (((1,), (1,)), ((), ())), preferred_element_type=jnp.float32
        ).astype(jnp.bfloat16)
        for unit, out_ref in enumerate(out_refs):
            for tile in range(tiles):
                for row in range(rows):
                    left = row * mid_len + tile * lanes
                    out_ref[tile, row] = found[unit * columns : (unit + 1) * columns, left : left + lanes]

    @pl.when(pl.program_id(0) == last)
    def _():
        weight = (coefficient_ref[0] * (1 - failed_ref[0])).astype(jnp.float32)
        swapped = levels_ref[0, 0] < levels_ref[0, 1]
        for tile in range(tiles):
            value = jnp.where(swapped == (tile == 1), weight, 0.0)
            value = jnp.full((columns, lanes), value, jnp.float32).astype(jnp.bfloat16)
            for out_ref in out_refs:
                out_ref[tile, 0] = value


def transform_z(samples, levels, coefficients, failed, table):
    local_long, mid_len, z_len = samples.shape
    chunks, units, columns, _ = table.shape
    rows = 32
    lines = local_long // chunks
    steps = lines // rows
    tiles = 2
    lanes = mid_len // tiles
    units *= chunks
    split = samples.reshape(chunks, lines, mid_len, z_len)
    return pl.pallas_call(
        z_kernel,
        grid=(steps + 1,),
        in_specs=[
            pl.BlockSpec(memory_space=pltpu.SMEM),
            pl.BlockSpec(memory_space=pltpu.SMEM),
            pl.BlockSpec(memory_space=pltpu.SMEM),
            pl.BlockSpec(table.shape, lambda i: (0, 0, 0, 0)),
            pl.BlockSpec((chunks, rows, mid_len, z_len), lambda i: (0, jnp.minimum(i, steps - 1), 0, 0)),
        ],
        out_specs=[pl.BlockSpec((tiles, rows, columns, lanes), lambda i: (0, i, 0, 0))] * units,
        out_shape=[jax.ShapeDtypeStruct((tiles, lines + 1, columns, lanes), jnp.bfloat16)] * units,
        compiler_params=pltpu.CompilerParams(vmem_limit_bytes=VMEM_LIMIT),
        cost_estimate=pl.CostEstimate(
            flops=2 * units * columns * samples.size, bytes_accessed=4 * samples.size, transcendentals=0
        ),
        name="transform_z",
    )(levels, coefficients, failed, table, split)


def is_outer():
    me = lax.axis_index("grid")
    return (me < 2) | (me >= 6)


def unit_specs(shape, rows):
    tiles, lines, columns, lanes = shape
    return [
        pl.BlockSpec((tiles, rows, columns, lanes), lambda i: (0, i, 0, 0)),
        pl.BlockSpec((tiles, 1, columns, lanes), lambda i: (0, lines - 1, 0, 0)),
    ]


def weighted_sum(sources, weights, kind):
    total = None
    for source, weight in zip(sources, weights):
        term = source * weight[kind]
        total = term if total is None else total + term
    return total


def relay_kernel(*refs):
    out_refs = refs[-2:]
    passing = [refs[-4], refs[-3]]
    sources, weights = refs[:-4:2], refs[1:-4:2]
    rows = out_refs[0].shape[1]
    last = pl.num_programs(0) - 1
    outer = is_outer()

    @pl.when(outer)
    def _():
        for out_ref, source in zip(out_refs, passing):
            out_ref[...] = source[...]

    @pl.when(jnp.logical_not(outer))
    def _():
        values = [source[...].astype(jnp.float32) for source in sources]
        scales = [weight[...].astype(jnp.float32) for weight in weights]
        for kind, out_ref in enumerate(out_refs):
            out_ref[...] = weighted_sum(values, scales, kind).astype(jnp.bfloat16)

    @pl.when(jnp.logical_not(outer) & (pl.program_id(0) == last))
    def _():
        for kind, out_ref in enumerate(out_refs):
            for tile in range(out_ref.shape[0]):
                out_ref[tile, rows - 1] = jnp.full(out_ref.shape[2:], float(tile == kind), jnp.bfloat16)


def relay(sources, passing):
    shape = sources[0].shape
    rows = shape[1]
    specs = unit_specs(shape, rows)
    return pl.pallas_call(
        relay_kernel,
        grid=(shape[1] // rows,),
        in_specs=specs * len(sources) + specs[:1] * 2,
        out_specs=specs[:1] * 2,
        out_shape=[jax.ShapeDtypeStruct(shape, jnp.bfloat16)] * 2,
        compiler_params=pltpu.CompilerParams(vmem_limit_bytes=VMEM_LIMIT),
        cost_estimate=pl.CostEstimate(
            flops=0, bytes_accessed=2 * (len(sources) + 4) * math.prod(shape), transcendentals=0
        ),
        name="relay",
    )(*[ref for source in sources for ref in (source, source)], *passing)


def turning(outer, inner):
    rows = np.arange(outer * inner)
    return jnp.asarray(rows[:, None] % outer * inner + rows[:, None] // outer == rows[None, :], jnp.bfloat16)


def mid_kernel(first_chunk, apart, turn_ref, table_ref, *refs):
    out_refs = []
    if apart:
        refs, out_refs = refs[: -apart - 1] + refs[-1:], refs[-apart - 1 : -1]
    refs, out_ref = refs[:-1], refs[-1]
    tiles, rows, columns, lanes = refs[0].shape
    mid_len = tiles * lanes
    half = columns // 2
    pencils, classes, slots, _, halves = out_ref.shape[:5]
    groups = pencils // 2
    lead = lax.axis_index("grid") == 0
    outer = is_outer()
    sources = [ref[...] for ref in refs[0::2]]
    weights = [ref[...] for ref in refs[1::2]]
    for kept in (sources, weights):
        for spare in (-1, -2):
            kept[spare - 2] = jnp.where(outer, kept[spare], kept[spare - 2])
        del kept[-2:]
    sources = [source.astype(jnp.float32) for source in sources]
    weights = [weight.astype(jnp.float32) for weight in weights]
    for kind in range(classes):
        total = weighted_sum(sources, weights, kind).astype(jnp.bfloat16)
        lines = jnp.concatenate([total[tile].reshape(rows * columns, lanes) for tile in range(tiles)], axis=1)
        lines = jnp.dot(turn_ref[...], lines, preferred_element_type=jnp.float32).astype(jnp.bfloat16)
        product = jnp.dot(lines, table_ref[kind], preferred_element_type=jnp.float32)
        product = product.reshape(columns, rows, 2 * mid_len)
        re_cos, re_sin = product[:half, :, :mid_len], product[:half, :, mid_len:]
        im_cos, im_sin = product[half:, :, :mid_len], product[half:, :, mid_len:]
        for part in range(2):
            alone, other = (re_cos, im_cos) if part == 0 else (re_sin, im_sin)
            up = re_cos - im_sin if part == 0 else re_sin + im_cos
            down = re_cos + im_sin if part == 0 else re_sin - im_cos
            for piece in range(halves):
                for group in range(groups):
                    for slot in range(slots):
                        at = (piece * groups + group) * slots + slot
                        value, mirrored = up[at], down[at]
                        if first_chunk and slot == 0:
                            follower = (piece * groups + (group + 1) % groups) * slots
                            if group == 0:
                                value = jnp.where(lead, alone[at], value)
                            turn = down[follower] if group + 1 < groups else other[follower]
                            mirrored = jnp.where(lead, turn, mirrored)
                        out_ref[group, kind, slot, part, piece] = value.astype(jnp.bfloat16)
                        out_ref[pencils - 1 - group, kind, slot, part, piece] = mirrored.astype(jnp.bfloat16)
    for step, apart_ref in enumerate(out_refs):
        apart_ref[...] = out_ref[lax.axis_index("pencil") ^ step]


def transform_mid(sources, table, first_chunk, apart, chunks, pencils, slots):
    tiles, lines, columns, lanes = sources[0].shape
    lines -= 1
    classes, mid_len, _ = table.shape
    rows = 32
    shape = (pencils, classes, slots, 2, chunks, lines, mid_len)
    block = shape[:5] + (rows, mid_len)
    if apart:
        layout = dict(
            out_specs=[pl.BlockSpec(block[1:], lambda i: (0, 0, 0, 0, i, 0))] * pencils,
            out_shape=[jax.ShapeDtypeStruct(shape[1:], jnp.bfloat16)] * pencils,
            scratch_shapes=[pltpu.VMEM(block, jnp.bfloat16)],
        )
    else:
        layout = dict(
            out_specs=pl.BlockSpec(block, lambda i: (0, 0, 0, 0, 0, i, 0)),
            out_shape=jax.ShapeDtypeStruct(shape, jnp.bfloat16),
        )
    size = sources[0].size
    return pl.pallas_call(
        functools.partial(mid_kernel, first_chunk, pencils if apart else 0),
        grid=(lines // rows,),
        in_specs=[
            pl.BlockSpec((rows * columns, rows * columns), lambda i: (0, 0)),
            pl.BlockSpec(table.shape, lambda i: (0, 0, 0)),
        ]
        + unit_specs(sources[0].shape, rows) * len(sources),
        compiler_params=pltpu.CompilerParams(vmem_limit_bytes=VMEM_LIMIT),
        cost_estimate=pl.CostEstimate(
            flops=MID_COST * 8 * size * mid_len,
            bytes_accessed=2 * len(sources) * size + 2 * math.prod(shape),
            transcendentals=0,
        ),
        name="transform_mid",
        **layout,
    )(turning(rows, columns), table, *[ref for source in sources for ref in (source, source)])


def long_kernel(rows_ref, z_ref, x_ref, y_ref, first_ref, second_ref, *refs):
    if len(refs) == 2:
        source_ref, out_ref = refs
    else:
        sources, out_ref, source_ref = refs[:-2], refs[-2], refs[-1]
        for step, source in enumerate(sources):
            source_ref[lax.axis_index("pencil") ^ step] = source[...]
    pencils, classes, _, _, local_long, mid_len = source_ref.shape
    long_len = pencils * local_long
    pairs = out_ref.shape[3]
    per_long = long_len // (2 * pairs)
    per_mid = mid_len // (2 * pairs)
    edge = per_mid // 2
    slot = pl.program_id(0)
    lines = [
        jnp.concatenate(
            [source_ref[:, kind, 0, part].reshape(long_len, mid_len) for part in range(2)], axis=1
        )
        for kind in range(classes)
    ]
    first = jnp.dot(first_ref[...], lines[0], preferred_element_type=jnp.float32)
    second = lax.dot_general(
        lines[1], second_ref[...], (((0,), (0,)), ((), ())), preferred_element_type=jnp.float32
    )
    z_re, z_im = z_ref[0, slot], z_ref[1, slot]
    low = lax.broadcasted_iota(jnp.int32, (pairs, 4 * pairs), 1) < 2 * pairs
    span = 4 * pairs
    for across in range(per_long):
        held = across < edge or across >= per_long - edge
        narrow = across if across < edge else across - (per_long - per_mid)
        columns = []
        for parity in range(2):
            x_re, x_im = (x_ref[part, parity, across * pairs : (across + 1) * pairs] for part in range(2))
            column = (x_re * z_re - x_im * z_im, x_re * z_im + x_im * z_re)
            columns.append([jnp.broadcast_to(value, (pairs, span)) for value in column])
        for couple in range(per_long // 2):
            near = couple < edge // 2 or couple >= (per_long - edge) // 2
            thin = couple if couple < edge // 2 else couple - (per_long - per_mid) // 2
            if not held and not near:
                continue
            y_re, y_im = (y_ref[part : part + 1, couple * span : (couple + 1) * span] for part in range(2))
            tiles = []
            for parity in range(2):
                parts = [None, None]
                if near:
                    top = (parity * per_long + across) * pairs

                    def taken(table, part):
                        left = part * mid_len + thin * span
                        return first[table * long_len + top : table * long_len + top + pairs, left : left + span]

                    parts = [taken(0, 0) - taken(1, 1), taken(1, 0) + taken(0, 1)]
                if held:
                    top = (parity * per_mid + narrow) * pairs

                    def turned(table, part):
                        left = table * long_len + couple * span
                        return second[part * mid_len + top : part * mid_len + top + pairs, left : left + span]

                    terms = [turned(0, 0) - turned(1, 1), turned(1, 0) + turned(0, 1)]
                    parts = [a + b for a, b in zip(parts, terms)] if near else terms
                x_re, x_im = columns[parity]
                factor_re = x_re * y_re - x_im * y_im
                factor_im = x_re * y_im + x_im * y_re
                tiles.append(
                    [
                        parts[0] * factor_re - parts[1] * factor_im,
                        parts[0] * factor_im + parts[1] * factor_re,
                    ]
                )
            for part in range(2):
                even, odd = tiles[0][part], tiles[1][part]
                block = across * per_long + 2 * couple
                left = jnp.where(low, even, pltpu.roll(odd, 2 * pairs, 1))
                right = jnp.where(low, pltpu.roll(even, 2 * pairs, 1), odd)
                out_ref[rows_ref[block], 0, part] = left.astype(jnp.bfloat16)
                out_ref[rows_ref[block + 1], 0, part] = right.astype(jnp.bfloat16)


def transform_long(sources, row_ids, z_factor, x_factor, y_factor, first, second, row_count, pairs):
    if len(sources) == 1:
        pencils, classes, slots, _, local_long, mid_len = sources[0].shape
    else:
        pencils = len(sources)
        classes, slots, _, local_long, mid_len = sources[0].shape
    block = (pencils, classes, 1, 2, local_long, mid_len)
    if len(sources) == 1:
        specs = [pl.BlockSpec(block, lambda i: (0, 0, i, 0, 0, 0))]
        scratch = []
    else:
        specs = [pl.BlockSpec(block[1:], lambda i: (0, i, 0, 0, 0))] * pencils
        scratch = [pltpu.VMEM(block, jnp.bfloat16)]
    depth = 2 * pencils * local_long
    shape = (row_count, slots, 2, pairs, 4 * pairs)
    return pl.pallas_call(
        long_kernel,
        grid=(slots,),
        in_specs=[
            pl.BlockSpec(memory_space=pltpu.SMEM),
            pl.BlockSpec(memory_space=pltpu.SMEM),
            pl.BlockSpec(x_factor.shape, lambda i: (0, 0, 0, 0)),
            pl.BlockSpec(y_factor.shape, lambda i: (0, 0)),
            pl.BlockSpec(first.shape, lambda i: (0, 0)),
            pl.BlockSpec(second.shape, lambda i: (0, 0)),
        ]
        + specs,
        scratch_shapes=scratch,
        out_specs=pl.BlockSpec((row_count, 1, 2, pairs, 4 * pairs), lambda i: (0, i, 0, 0, 0)),
        out_shape=jax.ShapeDtypeStruct(shape, jnp.bfloat16),
        compiler_params=pltpu.CompilerParams(vmem_limit_bytes=20 * 1024 * 1024),
        cost_estimate=pl.CostEstimate(
            flops=2 * classes * slots * depth * depth * mid_len,
            bytes_accessed=4 * slots * math.prod(block) + 2 * math.prod(shape) + 4 * depth * depth,
            transcendentals=0,
        ),
        name="transform_long",
    )(row_ids, z_factor, x_factor, y_factor, first, second, *sources)


def rows_kernel(turn_ref, *refs):
    sources, out_ref = refs[:-1], refs[-1]
    back = lax.axis_index("pencil") >= 2
    _, _, slots, parts, pairs, span = sources[0].shape
    z_local = out_ref.shape[2]

    def write(order):
        for row, top in itertools.product(range(out_ref.shape[0]), range(0, z_local, 8)):
            sides = []
            for part in range(parts):
                taken = []
                for z in range(top, top + 8):
                    device, place = divmod(order(z), len(sources) * slots)
                    chunk, slot = divmod(place, slots)
                    taken.append(sources[chunk][device, row, slot, part])
                sides.append(jnp.concatenate(taken, axis=0))
            turned = jnp.dot(
                turn_ref[...], jnp.concatenate(sides, axis=1), preferred_element_type=jnp.float32
            )
            for part in range(parts):
                for pair in range(pairs):
                    out_ref[row, part, top : top + 8, pair * span : (pair + 1) * span] = turned[
                        pair * 8 : (pair + 1) * 8, part * span : (part + 1) * span
                    ]

    @pl.when(jnp.logical_not(back))
    def _():
        write(lambda z: z)

    @pl.when(back)
    def _():
        write(lambda z: (z_local - z) % z_local)


def lay_rows(sources, z_local):
    grid_count, rows, slots, parts, pairs, span = sources[0].shape
    return pl.pallas_call(
        rows_kernel,
        grid=(rows // ROWS_PER_STEP,),
        in_specs=[pl.BlockSpec((8 * pairs, 8 * pairs), lambda i: (0, 0))]
        + [pl.BlockSpec((grid_count, ROWS_PER_STEP, slots, parts, pairs, span), lambda i: (0, i, 0, 0, 0, 0))]
        * len(sources),
        out_specs=pl.BlockSpec((ROWS_PER_STEP, parts, z_local, pairs * span), lambda i: (i, 0, 0, 0)),
        out_shape=jax.ShapeDtypeStruct((rows, parts, z_local, pairs * span), jnp.float32),
        compiler_params=pltpu.CompilerParams(vmem_limit_bytes=20 * 1024 * 1024),
        cost_estimate=pl.CostEstimate(
            flops=0, bytes_accessed=6 * len(sources) * sources[0].size, transcendentals=0
        ),
        name="lay_rows",
    )(turning(8, pairs), *sources)


PAIR_SAME = [(d, d ^ 2) for d in range(8)]
PAIR_CROSS = [(d, d ^ 3) for d in range(8)]
INNER_SAME = [(2, 4), (4, 2), (3, 5), (5, 3)]
INNER_CROSS = [(2, 5), (5, 2), (3, 4), (4, 3)]
INNER_CORES = [(d, d ^ 1) for d in range(2, 6)]
CORES = [(d, d ^ 1) for d in range(8)]
ENTER_SAME = [(0, 2), (1, 3), (6, 4), (7, 5)]
ENTER_CROSS = [(0, 3), (1, 2), (6, 5), (7, 4)]
JUMP_SAME = [(d, d ^ 4) for d in range(8)]
JUMP_MIXED = [(0, 5), (1, 4), (6, 3), (7, 2), (2, 6), (3, 7), (4, 0), (5, 1)]


def after(values, earlier):
    return lax.optimization_barrier((list(values), list(earlier)))[0]


def send(value, pairs):
    return lax.ppermute(value, "grid", pairs)


def hold_kernel(value_ref, *refs):
    out_ref = refs[-1]
    for row in range(value_ref.shape[0]):
        for column in range(value_ref.shape[1]):
            out_ref[row, column] = value_ref[row, column]


def hold(value, earlier):
    return pl.pallas_call(
        hold_kernel,
        in_specs=[pl.BlockSpec(memory_space=pltpu.SMEM)]
        + [pl.BlockSpec(memory_space=pl.ANY)] * len(earlier),
        out_specs=pl.BlockSpec(memory_space=pltpu.SMEM),
        out_shape=jax.ShapeDtypeStruct(value.shape, value.dtype),
        cost_estimate=pl.CostEstimate(flops=HOLD_COST, bytes_accessed=0, transcendentals=0),
        name="hold",
    )(value, *earlier)


def exchange(parts, axis):
    count = len(parts)
    got = {0: parts[0]}
    for step in reversed(range(1, count)):
        got[step] = lax.ppermute(parts[step], axis, [(d, d ^ step) for d in range(count)])
    return [got[step] for step in range(count)]


def tied(values, twins):
    return [after([value], [twin])[0] for value, twin in zip(values, twins)]


def send_early(units, twins):
    values = [units[0], units[1], units[5], units[2], units[3]]
    plans = (PAIR_SAME, PAIR_CROSS, INNER_CORES, INNER_SAME, INNER_CROSS)
    if twins:
        values = tied(values, twins)
    return [send(value, pairs) for value, pairs in zip(values, plans)]


def send_jump(sums, twins):
    if twins:
        sums = tied(sums, twins)
    return [send(value, pairs) for value, pairs in zip(sums, (JUMP_SAME, JUMP_MIXED))]


def send_enter(units, twins):
    return [send(value, pairs) for value, pairs in zip(tied(units[2:4], twins), (ENTER_SAME, ENTER_CROSS))]


def mode_factor(modes, diffusion, speed, long_len, mid_len):
    magnitude = jnp.exp(diffusion * modes * modes * (-4.0 / (long_len * long_len)))
    phase = speed * modes * (-2.0 * math.pi / mid_len)
    return magnitude * jnp.cos(phase), magnitude * jnp.sin(phase)


def body(field, levels, coefficients, failed, owner_map, velocity, diffusivity):
    samples = field[0]
    local_long, mid_len, z_len = samples.shape
    pencils = lax.axis_size("pencil")
    grid_count = lax.axis_size("grid")
    long_len = local_long * pencils
    z_local = z_len // pencils
    block_len = mid_len // 4
    per_long = long_len // block_len
    per_mid = mid_len // block_len
    row_count = 2 * per_long * per_mid - per_mid * per_mid
    per_device = z_len // (grid_count * pencils)
    slots = per_device // CHUNKS
    me = lax.axis_index("grid")
    pencil = lax.axis_index("pencil")

    positions = jnp.arange(long_len, dtype=jnp.int32)
    modes = signed_modes(positions, long_len)
    x_re, x_im = mode_factor(modes, diffusivity[0], velocity[0], long_len, mid_len)
    y_re, y_im = mode_factor(modes, diffusivity[1], velocity[1], long_len, mid_len)
    x_factor = jnp.stack([x_re, x_im]).reshape(2, long_len // 2, 2).transpose(0, 2, 1)[..., None]
    y_factor = jnp.stack([y_re, y_im])
    place_in = me * per_device + jnp.arange(per_device, dtype=jnp.int32)
    back = pencil >= pencils // 2
    z_index = pencil * z_local + jnp.where(back, (z_local - place_in) % z_local, place_in)
    z_re, z_im = mode_factor(
        signed_modes(z_index, z_len), diffusivity[2], velocity[2], long_len, mid_len
    )
    z_factor = jnp.stack([z_re, z_im]) * (1.0 / math.sqrt(long_len * mid_len * z_len))

    mid = mid_table(mid_len, block_len)
    first, second = long_tables(long_len, block_len)
    tables = [z_table(chunk, CHUNKS, grid_count, pencils, z_len) for chunk in range(CHUNKS)]
    tables = jnp.stack([v.reshape(grid_count, -1, v.shape[1]) for v in tables])
    units = transform_z(samples, levels, coefficients, failed, tables)
    units = [list(units[chunk * grid_count : (chunk + 1) * grid_count]) for chunk in range(CHUNKS)]

    units[0][4], x_factor, y_factor, z_factor = lax.optimization_barrier(
        (units[0][4], x_factor, y_factor, z_factor)
    )
    early, sums = [], []
    for chunk in range(CHUNKS):
        early.append(send_early(units[chunk], early[-1] if early else None))
    for chunk in range(CHUNKS):
        got = early[chunk]
        third = after(units[chunk][4:6], got[3:] if chunk else [])
        sums.append(relay([third[0], got[2], got[0], got[1]], third))
    cores = [send(units[chunk][7], CORES) for chunk in range(CHUNKS)]
    jumps = [send_jump(sums[0], None)]
    enters = [send_enter(units[0], early[0][3:])]
    arrived = []
    rows = None
    for chunk in range(CHUNKS):
        got = early[chunk]
        sources = [units[chunk][6], cores[chunk]] + enters[chunk] + jumps[chunk] + got[3:5] + got[0:2]
        last = chunk == CHUNKS - 1
        if not last:
            sources = after(sources, sums[chunk + 1])
            jumps.append(send_jump(sums[chunk + 1], jumps[chunk]))
        else:
            sources = after(sources, [rows])
        along_mid = transform_mid(sources, mid, chunk == 0, last, CHUNKS, pencils, slots)
        factor = z_factor[:, chunk * slots : (chunk + 1) * slots]
        if not last:
            enters.append(send_enter(units[chunk + 1], jumps[chunk]))
            factor = hold(factor, [cores[chunk + 1]])
            along_mid = along_mid.reshape(along_mid.shape[:4] + (local_long, mid_len))
            lines = [lax.all_to_all(along_mid, "pencil", split_axis=0, concat_axis=0, tiled=True)]
        else:
            along_mid = [v.reshape(v.shape[:3] + (local_long, mid_len)) for v in along_mid]
            lines = exchange(along_mid, "pencil")
        rows = transform_long(
            lines,
            owner_map,
            factor,
            x_factor,
            y_factor,
            first,
            second,
            row_count,
            block_len // 2,
        )
        rows = rows.reshape((grid_count, -1) + rows.shape[1:])
        sent = rows
        arrived.append(lax.all_to_all(sent, "grid", split_axis=0, concat_axis=0, tiled=True))
    return lay_rows(arrived, z_local)


def solution(mesh):
    placed = (P("grid", "pencil", None, None), P("grid", None), P("grid"), P("grid"), P(), P(), P())
    devices = mesh.shape["grid"] * mesh.shape["pencil"]

    def run(field, *rest):
        few = mesh.shape["grid"] == 8 and mesh.shape["pencil"] == 4 and field.shape[3] % (devices * CHUNKS) == 0
        return jax.shard_map(
            body if few else wide_body,
            mesh=mesh,
            in_specs=placed,
            out_specs=P("grid", None, "pencil", None),
            check_vma=False,
        )(field, *rest)

    return run
```
